512 devices in a mesh: dp: 32 (over y, x), seq: 16 (over z, core).
Axes of the slice: x: 4, y: 8, z: 8, core: 2. Of those that a mesh axis runs over, the one named last changes fastest.
Arguments:
- tokens: bfloat16 [32, 2048, 2048], P('dp', 'seq'), may hold values from -24 to 24
- qk_weight: bfloat16 [2048, 256], replicated, may hold values from -0.125 to 0.125
- values: bfloat16 [32, 2048, 1024], P('dp', 'seq'), may hold values from -6 to 6
- cotangent: bfloat16 [32, 2048, 1024], P('dp', 'seq'), may hold values from -6 to 6
- key_span: bfloat16 [32, 16, 8, 273, 128], P('dp', 'seq'), may hold values from -96 to 96
- key_span_norm: float32 [32, 16, 8, 273], P('dp', 'seq'), as said below
- query_span: bfloat16 [32, 16, 8, 273, 128], P('dp', 'seq'), may hold values from -0.4375 to 0.4375
- query_span_norm: float32 [32, 16, 8, 273], P('dp', 'seq'), may hold values from -0.4375 to 0.4375
Outputs:
- token_grad: bfloat16 [32, 2048, 2048], P('dp', 'seq')
- value_grad: bfloat16 [32, 2048, 1024], P('dp', 'seq')
- weight_grad: float32 [2048, 256], P('seq')
The draws below stay inside these ranges and needn't reach their ends.
Inputs may be any that keep to these rules, and one draw needn't show every extreme that they name: Each head's row is a positive combination of phi of head vectors, so phi(u) . key_span_norm is positive for every u.
All inputs are finite; a program needn't handle non-finite values.
Results may differ from the reference program's by a relative error of at most 0.0072.
Values sent between devices are 32-bit elements; how exact they have to be, the bound alone decides.
A program may use at most 128 MiB of HBM per device.

```python
import math
import jax
import jax.numpy as jnp
from jax import lax

D = 2048
H = 8
FD = 16
DV = 128
F = 273
TOK_DEV = 128
LENGTH = 2048
DOCS = 32
N_SEQ = 16


def draw_tokens(key, part):
    key = jax.random.fold_in(key, 11)
    first, second, third = jax.random.split(key, 3)
    shape_all = (DOCS, LENGTH, D)
    base = jnp.clip(jax.random.normal(first, shape_all, jnp.float32), -4.5, 4.5)
    row_scale = jnp.exp(jax.random.uniform(second, (DOCS, LENGTH, 1), jnp.float32, 0.0, math.log(3.0)))
    col_scale = jnp.exp(jax.random.uniform(third, (1, 1, D), jnp.float32, -0.5, 0.5))
    return (base * row_scale * col_scale).astype(jnp.bfloat16)


def draw_key_span_norm(key, part):
    key = jax.random.fold_in(key, 23)
    first, second = jax.random.split(key, 2)
    shape_keys = (DOCS, N_SEQ, H, 8, FD)
    pseudo = jnp.clip(jax.random.normal(first, shape_keys, jnp.float32), -3.0, 3.0)
    outer_prod = (pseudo[..., :, None] * pseudo[..., None, :]).reshape(DOCS, N_SEQ, H, 8, FD * FD)
    ones_col = jnp.ones((DOCS, N_SEQ, H, 8, 1), jnp.float32)
    feats = jnp.concatenate([ones_col, pseudo / FD ** 0.25, outer_prod / math.sqrt(2.0 * FD)], -1)
    mixing = jax.random.uniform(second, (DOCS, N_SEQ, H, 8, 1), jnp.float32, 0.5, 1.5) * (TOK_DEV / 4.0)
    return jnp.sum(feats * mixing, axis=3).astype(jnp.float32)


def steps_of(key, shape, pieces, least, top_value):
    factor_of, own = 1.0, jax.random.fold_in(key, 6)
    for dim, blocks in pieces:
        steps = jnp.exp(jax.random.uniform(jax.random.fold_in(own, dim), (blocks,), jnp.float32, least / len(pieces), top_value / len(pieces)))
        factor_of = factor_of * jnp.repeat(steps, shape[dim] // blocks).reshape([-1 if axis == dim else 1 for axis in range(len(shape))])
    return factor_of


def gaussian(stream_key, dims, scale, most, cuts=(), dtype=jnp.bfloat16):
    result = scale * jax.random.normal(stream_key, dims, jnp.float32)
    if cuts:
        result = result * steps_of(stream_key, dims, cuts, -0.22, 0.18)
    return jnp.clip(result, -most, most).astype(dtype)


def setup_inputs(seed: int = 0) -> dict:
    key_of = jax.random.split(jax.random.key(seed), 9)
    return {
        "tokens": draw_tokens(jax.random.fold_in(key_of[8], 71), 0),
        "qk_weight": gaussian(key_of[1], (D, 2 * H * FD), D ** -0.5, 0.125),
        "values": gaussian(key_of[2], (DOCS, LENGTH, H * DV), 1.0, 6.0, ((0, 32), (1, 16))),
        "cotangent": gaussian(key_of[3], (DOCS, LENGTH, H * DV), 1.0, 6.0, ((0, 32), (1, 16))),
        "key_span": gaussian(key_of[4], (DOCS, N_SEQ, H, F, DV), 16.0, 96.0, ((0, 32), (1, 16))),
        "key_span_norm": draw_key_span_norm(jax.random.fold_in(key_of[8], 71), 0),
        "query_span": gaussian(key_of[6], (DOCS, N_SEQ, H, F, DV), 0.03, 0.4375, ((0, 32), (1, 16))),
        "query_span_norm": gaussian(key_of[7], (DOCS, N_SEQ, H, F), 0.03, 0.4375, ((0, 32), (1, 16)), jnp.float32),
    }


highest = lax.Precision.HIGHEST

def rounded(array_in):
    return lax.optimization_barrier(array_in.astype(jnp.bfloat16)).astype(jnp.float32)

def taylor_features(inputs):
    width = inputs.shape[-1]
    outer_prod = (inputs[..., :, None] * inputs[..., None, :]).reshape(inputs.shape[:-1] + (width * width,))
    ones_col = jnp.ones(inputs.shape[:-1] + (1,), jnp.float32)
    return jnp.concatenate([ones_col, inputs / width ** 0.25, outer_prod / math.sqrt(2.0 * width)], -1)

def feature_grad(inputs, upstream):
    width = inputs.shape[-1]
    linear = upstream[..., 1:1 + width] / width ** 0.25
    outer_prod = upstream[..., 1 + width:].reshape(upstream.shape[:-1] + (width, width))
    left_part = jnp.einsum('...ab,...b->...a', outer_prod, inputs, precision=highest)
    right_part = jnp.einsum('...ab,...a->...b', outer_prod, inputs, precision=highest)
    return linear + (left_part + right_part) / math.sqrt(2.0 * width)

def exclusive_sum(stacked):
    return jnp.concatenate([jnp.zeros_like(stacked[:1]), jnp.cumsum(stacked, axis=0)[:-1]], 0)

def one_document(activations, value_rows, cot_rows, key_span, key_span_norm, query_span, query_span_norm, qk_weight):
    projected = rounded(jnp.dot(activations, qk_weight, preferred_element_type=jnp.float32))
    query_rows = projected[:, :H * FD].reshape(N_SEQ, TOK_DEV, H, FD)
    key_rows = projected[:, H * FD:].reshape(N_SEQ, TOK_DEV, H, FD)
    value_heads = value_rows.astype(jnp.float32).reshape(N_SEQ, TOK_DEV, H, DV)
    cot_heads = cot_rows.astype(jnp.float32).reshape(N_SEQ, TOK_DEV, H, DV)
    span_keys = key_span.astype(jnp.float32)
    span_queries = query_span.astype(jnp.float32)
    phi_query = rounded(taylor_features(query_rows))
    phi_keys = rounded(taylor_features(key_rows))
    scores = jnp.einsum('bthf,bshf->bhts', query_rows, key_rows, precision=highest) / math.sqrt(FD)
    causal = jnp.arange(TOK_DEV)[:, None] >= jnp.arange(TOK_DEV)[None, :]
    weights = jnp.where(causal, 1.0 + scores + 0.5 * scores * scores, 0.0)
    weights_low = rounded(weights)
    local_state = jnp.einsum('bthf,bthd->bhfd', phi_keys, value_heads, precision=highest)
    local_norm = lax.optimization_barrier(jnp.sum(phi_keys, axis=1))
    prefix_state = exclusive_sum(local_state + span_keys) + span_keys
    prefix_norm = exclusive_sum(local_norm + key_span_norm) + key_span_norm
    prefix_low = rounded(prefix_state)
    numer = jnp.einsum('bthf,bhfd->bthd', phi_query, prefix_low, precision=highest)
    numer = numer + jnp.einsum('bhts,bshd->bthd', weights_low, value_heads, precision=highest)
    denom = jnp.einsum('bthf,bhf->bth', phi_query, prefix_norm, precision=highest)
    denom = denom + lax.optimization_barrier(jnp.sum(weights, axis=-1)).transpose(0, 2, 1)
    grad_low = rounded(cot_heads / denom[..., None])
    grad_den = -lax.optimization_barrier(jnp.sum(cot_heads * numer, axis=-1)) / (denom * denom)
    query_state = jnp.einsum('bthf,bthd->bhfd', phi_query, grad_low, precision=highest)
    query_norm = jnp.einsum('bth,bthf->bhf', grad_den, phi_query, precision=highest)
    suffix_state = jnp.flip(exclusive_sum(jnp.flip(query_state + span_queries, 0)), 0)
    suffix_norm = jnp.flip(exclusive_sum(jnp.flip(query_norm + query_span_norm, 0)), 0)
    suffix_low = rounded(suffix_state)
    value_grad = jnp.einsum('bhts,bthd->bshd', weights_low, grad_low, precision=highest)
    value_grad = value_grad + jnp.einsum('bthf,bhfd->bthd', phi_keys, suffix_low, precision=highest)
    grad_weights = jnp.einsum('bthd,bshd->bhts', grad_low, value_heads, precision=highest)
    grad_weights = jnp.where(causal, grad_weights + grad_den.transpose(0, 2, 1)[..., None], 0.0)
    grad_scores = rounded(grad_weights * (1.0 + scores) / math.sqrt(FD))
    query_inner = jnp.einsum('bhts,bshf->bthf', grad_scores, key_rows, precision=highest)
    key_inner = jnp.einsum('bhts,bthf->bshf', grad_scores, query_rows, precision=highest)
    dphi_query = jnp.einsum('bthd,bhfd->bthf', grad_low, prefix_low, precision=highest)
    dphi_query = dphi_query + grad_den[..., None] * prefix_norm[:, None]
    dphi_keys = jnp.einsum('bthd,bhfd->bthf', value_heads, suffix_low, precision=highest)
    dphi_keys = dphi_keys + suffix_norm[:, None]
    dquery = query_inner + feature_grad(query_rows, dphi_query)
    dkey = key_inner + feature_grad(key_rows, dphi_keys)
    dprojected = jnp.concatenate([dquery.reshape(LENGTH, H * FD), dkey.reshape(LENGTH, H * FD)], 1).astype(jnp.bfloat16)
    token_grad = jnp.dot(dprojected, qk_weight.T, preferred_element_type=jnp.float32).astype(jnp.bfloat16)
    grad_term = jnp.dot(activations.T, dprojected, preferred_element_type=jnp.float32)
    return (token_grad, value_grad.reshape(LENGTH, H * DV).astype(jnp.bfloat16), grad_term)

def reference(tokens, qk_weight, values, cotangent, key_span, key_span_norm, query_span, query_span_norm):

    def per_document(doc_items):
        return one_document(doc_items[0], doc_items[1], doc_items[2], doc_items[3], doc_items[4], doc_items[5], doc_items[6], qk_weight)
    token_grad, value_grad, grad_terms = lax.map(per_document, (tokens, values, cotangent, key_span, key_span_norm, query_span, query_span_norm))
    weight_grad = lax.optimization_barrier(jnp.sum(grad_terms, axis=0)) / DOCS
    return (token_grad, value_grad, weight_grad)
```

```python
import functools
import math

import jax
import jax.numpy as jnp
from jax import lax
from jax.experimental import pallas as pl
from jax.experimental.pallas import tpu as pltpu
from jax.sharding import PartitionSpec as P

H = 8
FD = 16
DV = 128
F = 273
T = 128
R = 160
HALF = H // 2
PAIR = 1.0 / math.sqrt(2.0 * FD)
LINEAR = 1.0 / FD**0.25
f32 = jnp.float32
bf16 = jnp.bfloat16
MESH = pl.DeviceIdType.MESH


def dot(left, right, left_dim=1, right_dim=0):
    return lax.dot_general(
        left, right, (((left_dim,), (right_dim,)), ((), ())), preferred_element_type=f32
    )


def split(x, parts):
    out = []
    for _ in range(parts):
        low = x.astype(bf16)
        out.append(low)
        x = x - low.astype(f32)
    return out


def fold_matrix():
    row = lax.broadcasted_iota(jnp.int32, (R, F), 0)
    col = lax.broadcasted_iota(jnp.int32, (R, F), 1)
    pair = col - 17
    a, b = (pair >> 4) & 15, pair & 15
    d = (b - a) & 15
    target = jnp.where(d <= 7, d * 16 + a, (16 - d) * 16 + b)
    target = jnp.where(d == 8, 144 + jnp.minimum(a, b), target)
    target = jnp.where(col <= 16, 127 + col, target)
    target = jnp.where(col == 0, 152, target)
    return jnp.where(row == target, 1.0, 0.0).astype(bf16)


def twice(shape, dim):
    row = lax.broadcasted_iota(jnp.int32, shape, dim)
    doubled = ((row >= 16) & (row < 128)) | ((row >= 144) & (row < 152))
    return jnp.where(doubled, 2.0, 1.0)


def features(u):
    rows = [u * (u if d == 0 else pltpu.roll(u, FD - d, 0)) * PAIR for d in range(8)]
    rows.append(u * LINEAR)
    rows.append(u[:8] * u[8:] * PAIR)
    rows.append(jnp.where(lax.broadcasted_iota(jnp.int32, (8, T), 0) == 0, 1.0, 0.0))
    return jnp.concatenate(rows, 0)


def feature_grad(u, y):
    acc = 2.0 * y[:16] * u
    for d in range(1, 8):
        part = y[16 * d : 16 * d + 16]
        acc = acc + part * pltpu.roll(u, FD - d, 0) + pltpu.roll(part * u, d, 0)
    last = y[144:152]
    acc = acc + jnp.concatenate([last * u[8:], last * u[:8]], 0)
    return y[128:144] * LINEAR + acc * PAIR


def kernel(
    sizes,
    tok_h, w_h, val_h, cot_h, ks_h, kn_h, qs_h, qn_h,
    tg_h, vg_h, wg_h,
    tok, w, val, cot, ks, kn, qs, qn,
    tg, vg, wg,
    qt, kt, phi_q, phi_k, phi_qt, phi_kt, fold,
    score, a_low, value_part, den, g_low, gs, p_low, norm_t,
    span, contrib, other, chain_in, chain_out, pre, pre_out,
    norm_own, norm_in, gden_t, dproj_t,
    term, core_in, z_out, z_in, y_out, y_in, x_in, y_all,
    in_sem, out_sem,
    norm_send, norm_recv, other_send, other_recv, chain_send, chain_recv, pre_send, pre_recv,
    core_send, core_recv, z_send, z_recv, y_send, y_recv, x_send, x_recv, all_send, all_recv,
):
    ns, ny, nx, d_model = sizes
    nz = ns // 2
    rows = d_model // ns
    piece = rows // ny
    dp = lax.axis_index("dp")
    me = lax.axis_index("seq")
    z, c = me // 2, lax.rem(me, 2)
    y, x = dp // nx, lax.rem(dp, nx)
    mate = 2 * z + (1 - c)

    def seq_peer(step):
        return lax.rem(me + step, ns)

    def z_peer(step):
        return lax.rem(z + step, nz)

    def y_peer(step):
        return lax.rem(y + step, ny)

    def x_peer(step):
        return lax.rem(x + step, nx)

    loads = [
        pltpu.make_async_copy(src, dst, in_sem.at[i])
        for i, (src, dst) in enumerate(
            [(tok_h, tok), (w_h, w), (val_h, val), (ks_h, ks), (kn_h, kn), (cot_h, cot), (qs_h, qs), (qn_h, qn)]
        )
    ]
    for load in loads:
        load.start()

    barrier = pltpu.get_barrier_semaphore()
    for step in range(1, ns):
        pl.semaphore_signal(barrier, inc=1, device_id=(dp, seq_peer(step)), device_id_type=MESH)
    for step in range(1, ny):
        pl.semaphore_signal(barrier, inc=1, device_id=(y_peer(step) * nx + x, me), device_id_type=MESH)
    for step in range(1, nx):
        pl.semaphore_signal(barrier, inc=1, device_id=(y * nx + x_peer(step), me), device_id_type=MESH)

    def remote(src, dst, send, recv, device):
        return pltpu.make_async_remote_copy(
            src_ref=src, dst_ref=dst, send_sem=send, recv_sem=recv, device_id=device, device_id_type=MESH
        )

    def norm_copy(which, step):
        return remote(
            norm_own.at[which], norm_in.at[which, step],
            norm_send.at[which, step], norm_recv.at[which, step], (dp, seq_peer(step)),
        )

    def other_copy(which, k):
        return remote(
            contrib.at[which, (1 - c) * HALF + k], other.at[which, k],
            other_send.at[which, k], other_recv.at[which, k], (dp, mate),
        )

    def chain_copy(which, k):
        target = jnp.clip(z + 1 - 2 * which, 0, nz - 1)
        return remote(
            chain_out.at[which, k], chain_in.at[which, k],
            chain_send.at[which, k], chain_recv.at[which, k], (dp, 2 * target + c),
        )

    def pre_copy(which, k):
        return remote(
            pre_out.at[which, k], pre.at[which, c * HALF + k],
            pre_send.at[which, k], pre_recv.at[which, k], (dp, mate),
        )

    def core_copy(k):
        return remote(
            term.at[2 * k + (1 - c)], core_in.at[k], core_send.at[k], core_recv.at[k], (dp, mate)
        )

    def z_copy(step):
        return remote(
            z_out.at[z_peer(step)], z_in.at[step], z_send.at[step], z_recv.at[step],
            (dp, 2 * z_peer(step) + c),
        )

    def y_copy(step):
        return remote(
            y_out.at[y_peer(step)], y_in.at[step], y_send.at[step], y_recv.at[step],
            (y_peer(step) * nx + x, me),
        )

    def x_copy(step):
        return remote(
            x_in.at[x], x_in.at[x], x_send.at[step], x_recv.at[step], (y * nx + x_peer(step), me)
        )

    def all_copy(step):
        return remote(
            y_all.at[y], y_all.at[y], all_send.at[step], all_recv.at[step],
            (y_peer(step) * nx + x, me),
        )

    coef = twice((R, DV), 0)
    coef_row = twice((H, R), 1)
    head_row = lax.broadcasted_iota(jnp.int32, (H, R), 0)
    fold[...] = fold_matrix()

    def lanes(h):
        return slice(h * DV, (h + 1) * DV)

    def feat(h):
        return slice(h * FD, (h + 1) * FD)

    def fold_norm(value):
        return sum(dot(part, fold[...], 1, 1) for part in split(value, 3))

    loads[0].wait()
    loads[1].wait()
    projected = dot(tok[0], w[...]).astype(bf16)
    qt[...] = projected[:, : H * FD].astype(f32).T
    kt[...] = projected[:, H * FD :].astype(f32).T
    total = jnp.zeros((H, R), f32)
    ones = jnp.ones((H, T), bf16)
    for h in range(H):
        phi = features(kt[feat(h), :])
        phi_k[h] = phi.astype(bf16)
        phi_kt[h] = phi.T.astype(bf16)
        total = jnp.where(head_row == h, dot(ones, phi_k[h], 1, 1), total)
    loads[4].wait()
    own_norm = fold_norm(kn[0, 0])
    norm_own[0] = total * coef_row + own_norm
    pl.semaphore_wait(barrier, ns + ny + nx - 3)
    for step in range(1, ns):
        norm_copy(0, step).start()

    loads[2].wait()
    loads[3].wait()
    for h in range(H):
        span[h] = dot(fold[...], ks[0, 0, h])
        contrib[0, h] = dot(phi_k[h], val[0, :, lanes(h)]) * coef + span[h]
    for k in range(HALF):
        other_copy(0, k).start()

    causal = lax.broadcasted_iota(jnp.int32, (T, T), 0) >= lax.broadcasted_iota(jnp.int32, (T, T), 1)
    head_lane = lax.broadcasted_iota(jnp.int32, (T, H * FD), 1) // FD
    query, key = projected[:, : H * FD], projected[:, H * FD :]
    for h in range(H):
        phi = features(qt[feat(h), :])
        phi_q[h] = phi.astype(bf16)
        phi_qt[h] = phi.T.astype(bf16)
        masked = jnp.where(head_lane == h, query, jnp.zeros_like(query))
        s = dot(masked, key, 1, 1) * (1.0 / math.sqrt(FD))
        score[h] = s
        a = jnp.where(causal, 1.0 + s + 0.5 * s * s, 0.0)
        a_low[h] = a.astype(bf16)
        den[h] = jnp.broadcast_to(jnp.sum(a, axis=1, keepdims=True), (T, DV))

    for step in range(1, ns):
        norm_copy(0, step).wait_recv()
    norm = own_norm
    for step in range(1, ns):
        norm = norm + jnp.where(me >= step, norm_in[0, step], 0.0)
    norm_parts = jnp.concatenate(split(norm, 3), 0)
    two_parts = split(norm, 2)
    norm_t[...] = jnp.concatenate(two_parts + two_parts, 0).astype(f32).T.astype(bf16)

    loads[5].wait()
    loads[6].wait()
    part_lane = lax.broadcasted_iota(jnp.int32, (T, 3 * H), 1) & (H - 1)
    for h in range(H):
        inner = dot(phi_qt[h], norm_parts, 1, 1)
        whole = den[h] + jnp.sum(jnp.where(part_lane == h, inner, 0.0), axis=1, keepdims=True)
        den[h] = whole
        g_low[h] = (cot[0, :, lanes(h)].astype(f32) / whole).astype(bf16)
        contrib[1, h] = dot(phi_q[h], g_low[h]) * coef + dot(fold[...], qs[0, 0, h])
    for k in range(HALF):
        other_copy(1, k).start()
    for h in range(H):
        value_part[h] = dot(a_low[h], val[0, :, lanes(h)])

    ahead = jnp.clip(5 * (nz - 1 - 2 * z) // 4, -HALF, HALF)

    def pass_on(which, k):
        mine = c * HALF + k
        first = jnp.where(which == 0, z == 0, z == nz - 1)
        last = jnp.where(which == 0, z == nz - 1, z == 0)
        other_copy(which, k).wait_recv()

        @pl.when(first)
        def _():
            chain_in[which, k] = jnp.zeros((R, DV), f32)

        @pl.when(jnp.logical_not(first))
        def _():
            chain_copy(which, k).wait_recv()

        before = chain_in[which, k]
        here = contrib[which, mine]
        there = other[which, k]

        @pl.when(jnp.logical_not(last))
        def _():
            chain_out[which, k] = before + (here + there)
            chain_copy(which, k).start()

        second = (c ^ which) == 1
        pre[which, mine] = before + jnp.where(second, there, 0.0)
        pre_out[which, k] = before + jnp.where(second, 0.0, here)
        pre_copy(which, k).start()

    def chain_step(i, carry):
        for which, lag in ((0, jnp.maximum(-ahead, 0)), (1, jnp.maximum(ahead, 0))):
            k = i - lag

            @pl.when((k >= 0) & (k < HALF))
            def _():
                pass_on(which, k)

        return carry

    lax.fori_loop(0, 2 * HALF, chain_step, 0)
    for which in range(2):
        for k in range(HALF):
            pre_copy(which, k).wait_recv()

    lane = lax.broadcasted_iota(jnp.int32, (T, DV), 1)
    gden_all = jnp.zeros((T, DV), f32)
    for h in range(H):
        p_low[h] = (pre[0, h] + span[h]).astype(bf16)
        numer = dot(phi_qt[h], p_low[h]) + value_part[h]
        weighted = jnp.sum(cot[0, :, lanes(h)].astype(f32) * numer, axis=1, keepdims=True)
        gden = -weighted / (den[h] * den[h])
        gden_all = jnp.where(lane == h, gden, gden_all)
        ga = jnp.where(causal, dot(g_low[h], val[0, :, lanes(h)], 1, 1) + gden, 0.0)
        gs[h] = (ga * (1.0 + score[h]) * (1.0 / math.sqrt(FD))).astype(bf16)
    gden_t[...] = gden_all.T[:H]
    gden_parts = jnp.concatenate(split(gden_t[...], 3), 0)
    total = jnp.zeros((H, R), f32)
    for h in range(H):
        every = dot(gden_parts, phi_q[h], 1, 1)
        every = every[:H] + every[H : 2 * H] + every[2 * H :]
        total = jnp.where(head_row == h, every, total)
    loads[7].wait()
    norm_own[1] = total * coef_row + fold_norm(qn[0, 0])
    for step in range(1, ns):
        norm_copy(1, step).start()

    high, low = split(gden_t[...], 2)
    gden_rows = jnp.concatenate([high, high, low, low], 0)
    four_row = lax.broadcasted_iota(jnp.int32, (4 * H, T), 0) & (H - 1)
    for h in range(H):
        only = jnp.where(four_row == h, gden_rows, jnp.zeros_like(gden_rows))
        up = dot(p_low[h], g_low[h], 1, 1) + dot(norm_t[...], only)
        u = qt[feat(h), :]
        dproj_t[feat(h), :] = feature_grad(u, up) + dot(kt[feat(h), :].astype(bf16), gs[h], 1, 1)
    for h in range(H):
        p_low[h] = pre[1, h].astype(bf16)
        vg[0, :, lanes(h)] = (dot(a_low[h], g_low[h], 0, 0) + dot(phi_kt[h], p_low[h])).astype(bf16)
    store_vg = pltpu.make_async_copy(vg, vg_h, out_sem.at[0])
    store_vg.start()

    for step in range(1, ns):
        norm_copy(1, step).wait_recv()
    norm = jnp.zeros((H, R), f32)
    for step in range(1, ns):
        norm = norm + jnp.where(me + (ns - step) < ns, norm_in[1, step], 0.0)
    parts = split(norm, 3)
    norm_t[...] = jnp.concatenate(parts + [jnp.zeros_like(parts[0])], 0).astype(f32).T.astype(bf16)
    for h in range(H):
        only = jnp.where(four_row == h, 1.0, 0.0).astype(bf16)
        up = dot(p_low[h], val[0, :, lanes(h)], 1, 1) + dot(norm_t[...], only)
        u = kt[feat(h), :]
        inner = dot(qt[feat(h), :].astype(bf16), gs[h])
        dproj_t[H * FD + h * FD : H * FD + (h + 1) * FD, :] = feature_grad(u, up) + inner
    dproj = dproj_t[...].T.astype(bf16)

    for k in range(nz):
        chunk = pl.ds(pl.multiple_of((2 * k + 1 - c) * rows, rows), rows)
        term[2 * k + 1 - c] = dot(tok[0, :, chunk], dproj, 0, 0)
        core_copy(k).start()
    for k in range(nz):
        chunk = pl.ds(pl.multiple_of((2 * k + c) * rows, rows), rows)
        term[2 * k + c] = dot(tok[0, :, chunk], dproj, 0, 0)
    for k in range(nz):
        core_copy(k).wait_recv()
    for k in range(nz):
        z_out[k] = term[2 * k + c] + core_in[k]
    for step in range(1, nz):
        z_copy(step).start()

    cols = min(512, d_model)
    for j in range(d_model // cols):
        tg[0, :, j * cols : (j + 1) * cols] = dot(dproj, w[j * cols : (j + 1) * cols, :], 1, 1).astype(bf16)
    store_tg = pltpu.make_async_copy(tg, tg_h, out_sem.at[1])
    store_tg.start()

    acc = z_out[z]
    for step in range(1, nz):
        z_copy(step).wait_recv()
        acc = acc + z_in[step]
    y_out[...] = acc.reshape(ny, piece, 2 * H * FD)
    for step in range(1, ny):
        y_copy(step).start()
    acc = y_out[y]
    for step in range(1, ny):
        y_copy(step).wait_recv()
        acc = acc + y_in[step]
    x_in[x] = acc
    for step in range(1, nx):
        x_copy(step).start()
    for step in range(1, nx):
        source = lax.rem(x + nx - step, nx)
        remote(
            x_in.at[source], x_in.at[source], x_send.at[step], x_recv.at[step],
            (y * nx + x_peer(step), me),
        ).wait_recv()
    acc = x_in[0]
    for j in range(1, nx):
        acc = acc + x_in[j]
    y_all[y] = acc * (1.0 / (ny * nx))
    for step in range(1, ny):
        all_copy(step).start()
    for step in range(1, ny):
        source = lax.rem(y + ny - step, ny)
        remote(
            y_all.at[source], y_all.at[source], all_send.at[step], all_recv.at[step],
            (y_peer(step) * nx + x, me),
        ).wait_recv()
    wg[...] = y_all[...].reshape(rows, 2 * H * FD)
    store_wg = pltpu.make_async_copy(wg, wg_h, out_sem.at[2])
    store_wg.start()

    for which in range(2):
        for step in range(1, ns):
            norm_copy(which, step).wait_send()
        last = (z == nz - 1) if which == 0 else (z == 0)
        for k in range(HALF):
            other_copy(which, k).wait_send()
            pre_copy(which, k).wait_send()

            @pl.when(jnp.logical_not(last))
            def _():
                chain_copy(which, k).wait_send()

    for k in range(nz):
        core_copy(k).wait_send()
    for step in range(1, nz):
        z_copy(step).wait_send()
    for step in range(1, ny):
        y_copy(step).wait_send()
        all_copy(step).wait_send()
    for step in range(1, nx):
        x_copy(step).wait_send()
    store_vg.wait()
    store_tg.wait()
    store_wg.wait()


def on_device(sizes, tokens, qk_weight, values, cotangent, key_span, key_norm, query_span, query_norm):
    ns, ny, nx, d_model = sizes
    nz = ns // 2
    rows = d_model // ns
    piece = rows // ny
    width = 2 * H * FD
    args = (tokens, qk_weight, values, cotangent, key_span, key_norm, query_span, query_norm)
    out_shape = (
        jax.ShapeDtypeStruct((1, T, d_model), bf16),
        jax.ShapeDtypeStruct((1, T, H * DV), bf16),
        jax.ShapeDtypeStruct((rows, width), f32),
    )
    vmem, dma = pltpu.VMEM, pltpu.SemaphoreType.DMA
    scratch = [vmem(a.shape, a.dtype) for a in args] + [vmem(o.shape, o.dtype) for o in out_shape]
    scratch += [
        vmem((H * FD, T), f32),
        vmem((H * FD, T), f32),
        vmem((H, R, T), bf16),
        vmem((H, R, T), bf16),
        vmem((H, T, R), bf16),
        vmem((H, T, R), bf16),
        vmem((R, F), bf16),
        vmem((H, T, T), f32),
        vmem((H, T, T), bf16),
        vmem((H, T, DV), f32),
        vmem((H, T, DV), f32),
        vmem((H, T, DV), bf16),
        vmem((H, T, T), bf16),
        vmem((H, R, DV), bf16),
        vmem((R, 4 * H), bf16),
        vmem((H, R, DV), f32),
        vmem((2, H, R, DV), f32),
        vmem((2, HALF, R, DV), f32),
        vmem((2, HALF, R, DV), f32),
        vmem((2, HALF, R, DV), f32),
        vmem((2, H, R, DV), f32),
        vmem((2, HALF, R, DV), f32),
        vmem((2, H, R), f32),
        vmem((2, ns, H, R), f32),
        vmem((H, T), f32),
        vmem((width, T), f32),
        vmem((ns, rows, width), f32),
        vmem((nz, rows, width), f32),
        vmem((nz, rows, width), f32),
        vmem((nz, rows, width), f32),
        vmem((ny, piece, width), f32),
        vmem((ny, piece, width), f32),
        vmem((nx, piece, width), f32),
        vmem((ny, piece, width), f32),
        dma((8,)), dma((3,)),
        dma((2, ns)), dma((2, ns)),
        dma((2, HALF)), dma((2, HALF)),
        dma((2, HALF)), dma((2, HALF)),
        dma((2, HALF)), dma((2, HALF)),
        dma((nz,)), dma((nz,)),
        dma((nz,)), dma((nz,)),
        dma((ny,)), dma((ny,)),
        dma((nx,)), dma((nx,)),
        dma((ny,)), dma((ny,)),
    ]
    return pl.pallas_call(
        functools.partial(kernel, sizes),
        out_shape=out_shape,
        in_specs=[pl.BlockSpec(memory_space=pl.ANY)] * 8,
        out_specs=(pl.BlockSpec(memory_space=pl.ANY),) * 3,
        scratch_shapes=scratch,
        compiler_params=pltpu.CompilerParams(
            collective_id=0, has_side_effects=True, vmem_limit_bytes=48 * 1024 * 1024
        ),
    )(*args)


def solution(mesh):
    ns, docs = mesh.shape["seq"], mesh.shape["dp"]
    nx = 4 if docs >= 16 else 2

    def whole(*args):
        sizes = (ns, docs // nx, nx, args[0].shape[2])
        in_specs = (
            P("dp", "seq", None),
            P(),
            P("dp", "seq", None),
            P("dp", "seq", None),
            P("dp", "seq", None, None, None),
            P("dp", "seq", None, None),
            P("dp", "seq", None, None, None),
            P("dp", "seq", None, None),
        )
        out_specs = (P("dp", "seq", None), P("dp", "seq", None), P("seq", None))
        return jax.shard_map(
            functools.partial(on_device, sizes),
            mesh=mesh,
            in_specs=in_specs,
            out_specs=out_specs,
            check_vma=False,
        )(*args)

    return whole
```

```python
import functools
import math

import jax
import jax.numpy as jnp
from jax import lax
from jax.experimental import pallas as pl
from jax.experimental.pallas import tpu as pltpu
from jax.sharding import PartitionSpec as P

H = 8
FD = 16
DV = 128
F = 273
T = 128
R = 160
HALF = H // 2
PAIR = 1.0 / math.sqrt(2.0 * FD)
LINEAR = 1.0 / FD**0.25
f32 = jnp.float32
bf16 = jnp.bfloat16
MESH = pl.DeviceIdType.MESH


def dot(left, right, left_dim=1, right_dim=0):
    return lax.dot_general(
        left, right, (((left_dim,), (right_dim,)), ((), ())), preferred_element_type=f32
    )


def split(x, parts):
    out = []
    for _ in range(parts):
        low = x.astype(bf16)
        out.append(low)
        x = x - low.astype(f32)
    return out


def fold_matrix():
    row = lax.broadcasted_iota(jnp.int32, (R, F), 0)
    col = lax.broadcasted_iota(jnp.int32, (R, F), 1)
    pair = col - 17
    a, b = (pair >> 4) & 15, pair & 15
    d = (b - a) & 15
    target = jnp.where(d <= 7, d * 16 + a, (16 - d) * 16 + b)
    target = jnp.where(d == 8, 144 + jnp.minimum(a, b), target)
    target = jnp.where(col <= 16, 127 + col, target)
    target = jnp.where(col == 0, 152, target)
    return jnp.where(row == target, 1.0, 0.0).astype(bf16)


def twice(shape, dim):
    row = lax.broadcasted_iota(jnp.int32, shape, dim)
    doubled = ((row >= 16) & (row < 128)) | ((row >= 144) & (row < 152))
    return jnp.where(doubled, 2.0, 1.0)


def features(u):
    rows = [u * (u if d == 0 else pltpu.roll(u, FD - d, 0)) * PAIR for d in range(8)]
    rows.append(u * LINEAR)
    rows.append(u[:8] * u[8:] * PAIR)
    rows.append(jnp.where(lax.broadcasted_iota(jnp.int32, (8, T), 0) == 0, 1.0, 0.0))
    return jnp.concatenate(rows, 0)


def feature_grad(u, y):
    acc = 2.0 * y[:16] * u
    for d in range(1, 8):
        part = y[16 * d : 16 * d + 16]
        acc = acc + part * pltpu.roll(u, FD - d, 0) + pltpu.roll(part * u, d, 0)
    last = y[144:152]
    acc = acc + jnp.concatenate([last * u[8:], last * u[:8]], 0)
    return y[128:144] * LINEAR + acc * PAIR


def kernel(
    sizes,
    tok_h, w_h, val_h, cot_h, ks_h, kn_h, qs_h, qn_h,
    tg_h, vg_h, wg_h,
    tok, w, val, cot, ks, kn, qs, qn,
    tg, vg, wg,
    qt, kt, phi_q, phi_k, phi_qt, phi_kt, fold,
    score, a_low, value_part, den, g_low, gs, p_low, norm_t,
    span, contrib, other, pair_out, pair_in, chain_in, chain_out, back_out, back_in, pre, pre_out,
    row_sum, norm_own, norm_mate, norm_chip, norm_in, gden_t, dproj_t,
    term, core_in, z_out, z_in, zx_out, zx_in, xs_out, xs_in, xz_out, xz_in, y_part, x_part,
    in_sem, out_sem,
    mate_send, mate_recv, norm_send, norm_recv, other_send, other_recv, pair_send, pair_recv,
    chain_send, chain_recv, back_send, back_recv, pre_send, pre_recv,
    core_send, core_recv, z_send, z_recv, zx_send, zx_recv, xs_send, xs_recv, xz_send, xz_recv,
    y_send, y_recv, x_send, x_recv,
):
    ns, ny, nx, d_model = sizes
    nz = ns // 2
    rows = d_model // ns
    pairs = nz // 2
    half = rows // 2
    piece = half // nx
    dp = lax.axis_index("dp")
    me = lax.axis_index("seq")
    z, c = me // 2, lax.rem(me, 2)
    y, x = dp // nx, lax.rem(dp, nx)
    p, e = z // 2, lax.rem(z, 2)
    mate = 2 * z + (1 - c)
    partner = 4 * p + 2 * (1 - e) + c

    def z_peer(step):
        return lax.rem(z + step, nz)

    def y_peer(step):
        return lax.rem(y + step, ny)

    def x_peer(step):
        return lax.rem(x + step, nx)

    loads = [
        pltpu.make_async_copy(src, dst, in_sem.at[i])
        for i, (src, dst) in enumerate(
            [(tok_h, tok), (w_h, w), (val_h, val), (ks_h, ks), (kn_h, kn), (cot_h, cot), (qs_h, qs), (qn_h, qn)]
        )
    ]
    for load in loads:
        load.start()

    def across_z(step):
        return (dp, 2 * z_peer(step) + c)

    def across_y(step):
        return (y_peer(step) * nx + x, me)

    def across_x(step):
        return (y * nx + x_peer(step), me)

    barrier = pltpu.get_barrier_semaphore()
    pl.semaphore_signal(barrier, inc=1, device_id=(dp, mate), device_id_type=MESH)
    for step in range(1, nz):
        pl.semaphore_signal(barrier, inc=1, device_id=across_z(step), device_id_type=MESH)
    for step in range(1, ny):
        pl.semaphore_signal(barrier, inc=1, device_id=across_y(step), device_id_type=MESH)
    for step in range(1, nx):
        pl.semaphore_signal(barrier, inc=1, device_id=across_x(step), device_id_type=MESH)

    def remote(src, dst, send, recv, device):
        return pltpu.make_async_remote_copy(
            src_ref=src, dst_ref=dst, send_sem=send, recv_sem=recv, device_id=device, device_id_type=MESH
        )

    def mate_copy(which):
        return remote(
            norm_own.at[which], norm_mate.at[which], mate_send.at[which], mate_recv.at[which], (dp, mate)
        )

    def norm_copy(which, step):
        return remote(
            norm_chip.at[which], norm_in.at[which, step],
            norm_send.at[which, step], norm_recv.at[which, step], across_z(step),
        )

    def other_copy(which, k):
        return remote(
            contrib.at[which, (1 - c) * HALF + k], other.at[which, k],
            other_send.at[which, k], other_recv.at[which, k], (dp, mate),
        )

    def pair_copy(which, j):
        return remote(
            pair_out.at[which, j], pair_in.at[which, j],
            pair_send.at[which, j], pair_recv.at[which, j], (dp, partner),
        )

    def chain_copy(which, j):
        target = jnp.clip(p + 1 - 2 * which, 0, pairs - 1)
        return remote(
            chain_out.at[which, j], chain_in.at[which, j],
            chain_send.at[which, j], chain_recv.at[which, j], (dp, 4 * target + 2 * e + c),
        )

    def back_copy(which, j):
        return remote(
            back_out.at[which, j], back_in.at[which, j],
            back_send.at[which, j], back_recv.at[which, j], (dp, partner),
        )

    def pre_copy(which, k):
        return remote(
            pre_out.at[which, k], pre.at[which, c * HALF + k],
            pre_send.at[which, k], pre_recv.at[which, k], (dp, mate),
        )

    def core_copy(k):
        return remote(
            term.at[2 * k + (1 - c)], core_in.at[k], core_send.at[k], core_recv.at[k], (dp, mate)
        )

    def z_copy(step):
        return remote(
            z_out.at[z_peer(step)], z_in.at[step], z_send.at[step], z_recv.at[step], across_z(step)
        )

    def zx_copy(step):
        return remote(
            zx_out.at[x_peer(step)], zx_in.at[step], zx_send.at[step], zx_recv.at[step], across_x(step)
        )

    def xs_copy(step):
        return remote(
            xs_out.at[x_peer(step)], xs_in.at[step], xs_send.at[step], xs_recv.at[step], across_x(step)
        )

    def xz_copy(step):
        return remote(
            xz_out.at[z_peer(step)], xz_in.at[step], xz_send.at[step], xz_recv.at[step], across_z(step)
        )

    def y_copy(part, step, source):
        return remote(
            y_part.at[part, source], y_part.at[part, source],
            y_send.at[part, step], y_recv.at[part, step], across_y(step),
        )

    def x_copy(part, step, source):
        return remote(
            x_part.at[part, source], x_part.at[part, source],
            x_send.at[part, step], x_recv.at[part, step], across_x(step),
        )

    coef = twice((R, DV), 0)
    coef_row = twice((H, R), 1)
    head_row = lax.broadcasted_iota(jnp.int32, (H, R), 0)
    fold[...] = fold_matrix()

    def lanes(h):
        return slice(h * DV, (h + 1) * DV)

    def feat(h):
        return slice(h * FD, (h + 1) * FD)

    def fold_rows(source):
        def lap(a, carry):
            for d in range(8):
                b = (a + d) & 15
                row = source[0, 0, 17 + 16 * a + b].astype(f32)
                if d:
                    row = row + source[0, 0, 17 + 16 * b + a].astype(f32)
                row_sum[pl.ds(pl.multiple_of((16 * d + a) * H, H), H), :] = row
            row_sum[pl.ds(pl.multiple_of((128 + a) * H, H), H), :] = source[0, 0, 1 + a].astype(f32)
            return carry

        def last_lap(a, carry):
            row = source[0, 0, 25 + 17 * a].astype(f32) + source[0, 0, 17 + 16 * (a + 8) + a].astype(f32)
            row_sum[pl.ds(pl.multiple_of((144 + a) * H, H), H), :] = row
            return carry

        lax.fori_loop(0, 16, lap, 0)
        lax.fori_loop(0, 8, last_lap, 0)
        row_sum[152 * H : 153 * H, :] = source[0, 0, 0].astype(f32)

    row_sum[153 * H :, :] = jnp.zeros(((R - 153) * H, DV), f32)

    def fold_norm(value):
        return sum(dot(part, fold[...], 1, 1) for part in split(value, 3))

    loads[0].wait()
    loads[1].wait()
    projected = dot(tok[0], w[...]).astype(bf16)
    qt[...] = projected[:, : H * FD].astype(f32).T
    kt[...] = projected[:, H * FD :].astype(f32).T
    total = jnp.zeros((H, R), f32)
    ones = jnp.ones((H, T), bf16)
    for h in range(H):
        phi = features(kt[feat(h), :])
        phi_k[h] = phi.astype(bf16)
        phi_kt[h] = phi.T.astype(bf16)
        total = jnp.where(head_row == h, dot(ones, phi_k[h], 1, 1), total)
    loads[4].wait()
    own_norm = fold_norm(kn[0, 0])
    norm_own[0] = total * coef_row + own_norm
    pl.semaphore_wait(barrier, nz + ny + nx - 2)
    mate_copy(0).start()

    loads[2].wait()
    loads[3].wait()
    fold_rows(ks)
    for h in range(H):
        span[h] = row_sum[pl.ds(h, R, stride=H), :]
        contrib[0, h] = dot(phi_k[h], val[0, :, lanes(h)]) * coef + span[h]
    for k in range(HALF):
        other_copy(0, k).start()
    mate_copy(0).wait_recv()
    norm_chip[0] = norm_own[0] + norm_mate[0]
    for step in range(1, nz):
        norm_copy(0, step).start()

    causal = lax.broadcasted_iota(jnp.int32, (T, T), 0) >= lax.broadcasted_iota(jnp.int32, (T, T), 1)
    head_lane = lax.broadcasted_iota(jnp.int32, (T, H * FD), 1) // FD
    query, key = projected[:, : H * FD], projected[:, H * FD :]
    for h in range(H):
        phi = features(qt[feat(h), :])
        phi_q[h] = phi.astype(bf16)
        phi_qt[h] = phi.T.astype(bf16)
        masked = jnp.where(head_lane == h, query, jnp.zeros_like(query))
        s = dot(masked, key, 1, 1) * (1.0 / math.sqrt(FD))
        score[h] = s
        a = jnp.where(causal, 1.0 + s + 0.5 * s * s, 0.0)
        a_low[h] = a.astype(bf16)
        den[h] = jnp.broadcast_to(jnp.sum(a, axis=1, keepdims=True), (T, DV))

    def step_one(which):
        for j in range(2):
            k = 2 * (1 - e) + j
            other_copy(which, k).wait_recv()
            pair_out[which, j] = contrib[which, c * HALF + k] + other[which, k]
            pair_copy(which, j).start()

    def finish(which, k, before):
        second = (c ^ which) == 1
        mine = c * HALF + k
        pre[which, mine] = before + jnp.where(second, other[which, k], 0.0)
        pre_out[which, k] = before + jnp.where(second, 0.0, contrib[which, mine])
        pre_copy(which, k).start()

    def step_two(which):
        first = jnp.where(which == 0, p == 0, p == pairs - 1)
        last = jnp.where(which == 0, p == pairs - 1, p == 0)
        for j in range(2):
            k = 2 * e + j
            other_copy(which, k).wait_recv()
            pair_copy(which, j).wait_recv()

            @pl.when(first)
            def _():
                chain_in[which, j] = jnp.zeros((R, DV), f32)

            @pl.when(jnp.logical_not(first))
            def _():
                chain_copy(which, j).wait_recv()

            before = chain_in[which, j]
            here = contrib[which, c * HALF + k] + other[which, k]
            there = pair_in[which, j]

            @pl.when(jnp.logical_not(last))
            def _():
                chain_out[which, j] = before + (here + there)
                chain_copy(which, j).start()

            second = (e ^ which) == 1
            back_out[which, j] = before + jnp.where(second, 0.0, here)
            back_copy(which, j).start()
            finish(which, k, before + jnp.where(second, there, 0.0))

    def step_three(which):
        for j in range(2):
            back_copy(which, j).wait_recv()
            finish(which, 2 * (1 - e) + j, back_in[which, j])

    def step_four(which):
        for k in range(HALF):
            pre_copy(which, k).wait_recv()

    early = 2 * p < pairs
    late = jnp.logical_not(early)
    step_one(0)

    @pl.when(early)
    def _():
        step_two(0)

    for step in range(1, nz):
        norm_copy(0, step).wait_recv()
    norm = own_norm + jnp.where(c == 1, norm_mate[0], 0.0)
    for step in range(1, nz):
        norm = norm + jnp.where(z >= step, norm_in[0, step], 0.0)
    norm_parts = jnp.concatenate(split(norm, 3), 0)
    two_parts = split(norm, 2)
    norm_t[...] = jnp.concatenate(two_parts + two_parts, 0).astype(f32).T.astype(bf16)

    loads[5].wait()
    loads[6].wait()
    fold_rows(qs)
    part_lane = lax.broadcasted_iota(jnp.int32, (T, 3 * H), 1) & (H - 1)
    for h in range(H):
        inner = dot(phi_qt[h], norm_parts, 1, 1)
        whole = den[h] + jnp.sum(jnp.where(part_lane == h, inner, 0.0), axis=1, keepdims=True)
        den[h] = whole
        g_low[h] = (cot[0, :, lanes(h)].astype(f32) / whole).astype(bf16)
        contrib[1, h] = dot(phi_q[h], g_low[h]) * coef + row_sum[pl.ds(h, R, stride=H), :]
    for k in range(HALF):
        other_copy(1, k).start()
    step_one(1)
    for h in range(H):
        value_part[h] = dot(a_low[h], val[0, :, lanes(h)])

    @pl.when(late)
    def _():
        def either(i, carry):
            step_two(i ^ (p == pairs - 1).astype(jnp.int32))
            return carry

        lax.fori_loop(0, 2, either, 0)
        step_three(1)

    step_three(0)
    step_four(0)

    lane = lax.broadcasted_iota(jnp.int32, (T, DV), 1)
    gden_all = jnp.zeros((T, DV), f32)
    for h in range(H):
        p_low[h] = (pre[0, h] + span[h]).astype(bf16)
        numer = dot(phi_qt[h], p_low[h]) + value_part[h]
        weighted = jnp.sum(cot[0, :, lanes(h)].astype(f32) * numer, axis=1, keepdims=True)
        gden = -weighted / (den[h] * den[h])
        gden_all = jnp.where(lane == h, gden, gden_all)
        ga = jnp.where(causal, dot(g_low[h], val[0, :, lanes(h)], 1, 1) + gden, 0.0)
        gs[h] = (ga * (1.0 + score[h]) * (1.0 / math.sqrt(FD))).astype(bf16)
    gden_t[...] = gden_all.T[:H]
    gden_parts = jnp.concatenate(split(gden_t[...], 3), 0)
    total = jnp.zeros((H, R), f32)
    for h in range(H):
        every = dot(gden_parts, phi_q[h], 1, 1)
        every = every[:H] + every[H : 2 * H] + every[2 * H :]
        total = jnp.where(head_row == h, every, total)
    loads[7].wait()
    norm_own[1] = total * coef_row + fold_norm(qn[0, 0])
    mate_copy(1).start()
    mate_copy(1).wait_recv()
    norm_chip[1] = norm_own[1] + norm_mate[1]
    for step in range(1, nz):
        norm_copy(1, step).start()

    high, low = split(gden_t[...], 2)
    gden_rows = jnp.concatenate([high, high, low, low], 0)
    four_row = lax.broadcasted_iota(jnp.int32, (4 * H, T), 0) & (H - 1)
    for h in range(H):
        only = jnp.where(four_row == h, gden_rows, jnp.zeros_like(gden_rows))
        up = dot(p_low[h], g_low[h], 1, 1) + dot(norm_t[...], only)
        u = qt[feat(h), :]
        dproj_t[feat(h), :] = feature_grad(u, up) + dot(kt[feat(h), :].astype(bf16), gs[h], 1, 1)

    @pl.when(early)
    def _():
        step_two(1)
        step_three(1)

    step_four(1)
    for h in range(H):
        p_low[h] = pre[1, h].astype(bf16)
        vg[0, :, lanes(h)] = (dot(a_low[h], g_low[h], 0, 0) + dot(phi_kt[h], p_low[h])).astype(bf16)
    store_vg = pltpu.make_async_copy(vg, vg_h, out_sem.at[0])
    store_vg.start()

    for step in range(1, nz):
        norm_copy(1, step).wait_recv()
    norm = jnp.where(c == 0, norm_mate[1], 0.0)
    for step in range(1, nz):
        norm = norm + jnp.where(z < step, norm_in[1, step], 0.0)
    parts = split(norm, 3)
    norm_t[...] = jnp.concatenate(parts + [jnp.zeros_like(parts[0])], 0).astype(f32).T.astype(bf16)
    for h in range(H):
        only = jnp.where(four_row == h, 1.0, 0.0).astype(bf16)
        up = dot(p_low[h], val[0, :, lanes(h)], 1, 1) + dot(norm_t[...], only)
        u = kt[feat(h), :]
        inner = dot(qt[feat(h), :].astype(bf16), gs[h])
        dproj_t[H * FD + h * FD : H * FD + (h + 1) * FD, :] = feature_grad(u, up) + inner
    dproj = dproj_t[...].T.astype(bf16)

    for k in range(nz):
        chunk = pl.ds(pl.multiple_of((2 * k + 1 - c) * rows, rows), rows)
        term[2 * k + 1 - c] = dot(tok[0, :, chunk], dproj, 0, 0)
        core_copy(k).start()
    for k in range(nz):
        chunk = pl.ds(pl.multiple_of((2 * k + c) * rows, rows), rows)
        term[2 * k + c] = dot(tok[0, :, chunk], dproj, 0, 0)
    for k in range(nz):
        core_copy(k).wait_recv()
        both = term[2 * k + c] + core_in[k]
        z_out[k] = both[:half]
        for j in range(nx):
            xs_out[j, k] = both[half + j * piece : half + (j + 1) * piece]
    for step in range(1, nx):
        xs_copy(step).start()
    for step in range(1, nz):
        z_copy(step).start()

    cols = min(512, d_model)
    for j in range(d_model // cols):
        tg[0, :, j * cols : (j + 1) * cols] = dot(dproj, w[j * cols : (j + 1) * cols, :], 1, 1).astype(bf16)
    store_tg = pltpu.make_async_copy(tg, tg_h, out_sem.at[1])
    store_tg.start()

    for step in range(1, nx):
        xs_copy(step).wait_recv()
    for k in range(nz):
        acc = xs_out[x, k]
        for step in range(1, nx):
            acc = acc + xs_in[step, k]
        xz_out[k] = acc
    for step in range(1, nz):
        xz_copy(step).start()
    acc = z_out[z]
    for step in range(1, nz):
        z_copy(step).wait_recv()
        acc = acc + z_in[step]
    for j in range(nx):
        zx_out[j] = acc[j * piece : (j + 1) * piece]
    for step in range(1, nx):
        zx_copy(step).start()
    acc = xz_out[z]
    for step in range(1, nz):
        xz_copy(step).wait_recv()
        acc = acc + xz_in[step]
    y_part[1, y] = acc
    for step in range(1, ny):
        y_copy(1, step, y).start()
    acc = zx_out[x]
    for step in range(1, nx):
        zx_copy(step).wait_recv()
        acc = acc + zx_in[step]
    y_part[0, y] = acc
    for step in range(1, ny):
        y_copy(0, step, y).start()
    for part in (1, 0):
        for step in range(1, ny):
            y_copy(part, step, lax.rem(y + ny - step, ny)).wait_recv()
        acc = y_part[part, 0]
        for j in range(1, ny):
            acc = acc + y_part[part, j]
        x_part[part, x] = acc * (1.0 / (ny * nx))
        for step in range(1, nx):
            x_copy(part, step, x).start()
    for part in (1, 0):
        for step in range(1, nx):
            x_copy(part, step, lax.rem(x + nx - step, nx)).wait_recv()
    wg[...] = x_part[...].reshape(rows, 2 * H * FD)
    store_wg = pltpu.make_async_copy(wg, wg_h, out_sem.at[2])
    store_wg.start()

    for which in range(2):
        mate_copy(which).wait_send()
        for step in range(1, nz):
            norm_copy(which, step).wait_send()
        last = (p == pairs - 1) if which == 0 else (p == 0)
        for k in range(HALF):
            other_copy(which, k).wait_send()
            pre_copy(which, k).wait_send()
        for j in range(2):
            pair_copy(which, j).wait_send()
            back_copy(which, j).wait_send()

            @pl.when(jnp.logical_not(last))
            def _():
                chain_copy(which, j).wait_send()

    for k in range(nz):
        core_copy(k).wait_send()
    for step in range(1, nz):
        z_copy(step).wait_send()
        xz_copy(step).wait_send()
    for step in range(1, nx):
        xs_copy(step).wait_send()
        zx_copy(step).wait_send()
    for part in range(2):
        for step in range(1, ny):
            y_copy(part, step, y).wait_send()
        for step in range(1, nx):
            x_copy(part, step, x).wait_send()
    store_vg.wait()
    store_tg.wait()
    store_wg.wait()


def on_device(sizes, tokens, qk_weight, values, cotangent, key_span, key_norm, query_span, query_norm):
    ns, ny, nx, d_model = sizes
    nz = ns // 2
    rows = d_model // ns
    half = rows // 2
    piece = half // nx
    width = 2 * H * FD
    key_span, query_span = (jnp.swapaxes(a, 2, 3) for a in (key_span, query_span))
    args = (tokens, qk_weight, values, cotangent, key_span, key_norm, query_span, query_norm)
    out_shape = (
        jax.ShapeDtypeStruct((1, T, d_model), bf16),
        jax.ShapeDtypeStruct((1, T, H * DV), bf16),
        jax.ShapeDtypeStruct((rows, width), f32),
    )
    vmem, dma = pltpu.VMEM, pltpu.SemaphoreType.DMA
    scratch = [vmem(a.shape, a.dtype) for a in args] + [vmem(o.shape, o.dtype) for o in out_shape]
    scratch += [
        vmem((H * FD, T), f32),
        vmem((H * FD, T), f32),
        vmem((H, R, T), bf16),
        vmem((H, R, T), bf16),
        vmem((H, T, R), bf16),
        vmem((H, T, R), bf16),
        vmem((R, F), bf16),
        vmem((H, T, T), f32),
        vmem((H, T, T), bf16),
        vmem((H, T, DV), f32),
        vmem((H, T, DV), f32),
        vmem((H, T, DV), bf16),
        vmem((H, T, T), bf16),
        vmem((H, R, DV), bf16),
        vmem((R, 4 * H), bf16),
        vmem((H, R, DV), f32),
        vmem((2, H, R, DV), f32),
        vmem((2, HALF, R, DV), f32),
        vmem((2, 2, R, DV), f32),
        vmem((2, 2, R, DV), f32),
        vmem((2, 2, R, DV), f32),
        vmem((2, 2, R, DV), f32),
        vmem((2, 2, R, DV), f32),
        vmem((2, 2, R, DV), f32),
        vmem((2, H, R, DV), f32),
        vmem((2, HALF, R, DV), f32),
        vmem((R * H, DV), f32),
        vmem((2, H, R), f32),
        vmem((2, H, R), f32),
        vmem((2, H, R), f32),
        vmem((2, nz, H, R), f32),
        vmem((H, T), f32),
        vmem((width, T), f32),
        vmem((ns, rows, width), f32),
        vmem((nz, rows, width), f32),
        vmem((nz, half, width), f32),
        vmem((nz, half, width), f32),
        vmem((nx, piece, width), f32),
        vmem((nx, piece, width), f32),
        vmem((nx, nz, piece, width), f32),
        vmem((nx, nz, piece, width), f32),
        vmem((nz, piece, width), f32),
        vmem((nz, piece, width), f32),
        vmem((2, ny, piece, width), f32),
        vmem((2, nx, piece, width), f32),
        dma((8,)), dma((3,)),
        dma((2,)), dma((2,)),
        dma((2, nz)), dma((2, nz)),
        dma((2, HALF)), dma((2, HALF)),
        dma((2, 2)), dma((2, 2)),
        dma((2, 2)), dma((2, 2)),
        dma((2, 2)), dma((2, 2)),
        dma((2, HALF)), dma((2, HALF)),
        dma((nz,)), dma((nz,)),
        dma((nz,)), dma((nz,)),
        dma((nx,)), dma((nx,)),
        dma((nx,)), dma((nx,)),
        dma((nz,)), dma((nz,)),
        dma((2, ny)), dma((2, ny)),
        dma((2, nx)), dma((2, nx)),
    ]
    return pl.pallas_call(
        functools.partial(kernel, sizes),
        out_shape=out_shape,
        in_specs=[pl.BlockSpec(memory_space=pl.ANY)] * 8,
        out_specs=(pl.BlockSpec(memory_space=pl.ANY),) * 3,
        scratch_shapes=scratch,
        compiler_params=pltpu.CompilerParams(
            collective_id=0, has_side_effects=True, vmem_limit_bytes=48 * 1024 * 1024
        ),
    )(*args)


def solution(mesh):
    ns, docs = mesh.shape["seq"], mesh.shape["dp"]
    nx = 4 if docs >= 16 else 2

    def whole(*args):
        sizes = (ns, docs // nx, nx, args[0].shape[2])
        in_specs = (
            P("dp", "seq", None),
            P(),
            P("dp", "seq", None),
            P("dp", "seq", None),
            P("dp", "seq", None, None, None),
            P("dp", "seq", None, None),
            P("dp", "seq", None, None, None),
            P("dp", "seq", None, None),
        )
        out_specs = (P("dp", "seq", None), P("dp", "seq", None), P("seq", None))
        return jax.shard_map(
            functools.partial(on_device, sizes),
            mesh=mesh,
            in_specs=in_specs,
            out_specs=out_specs,
            check_vma=False,
        )(*args)

    return whole
```

```python
import functools
import math

import jax
import jax.numpy as jnp
from jax import lax
from jax.experimental import pallas as pl
from jax.experimental.pallas import tpu as pltpu
from jax.sharding import PartitionSpec as P

H = 8
FD = 16
DV = 128
F = 273
T = 128
R = 160
HALF = H // 2
PAIR = 1.0 / math.sqrt(2.0 * FD)
LINEAR = 1.0 / FD**0.25
f32 = jnp.float32
bf16 = jnp.bfloat16
MESH = pl.DeviceIdType.MESH


def dot(left, right, left_dim=1, right_dim=0):
    return lax.dot_general(
        left, right, (((left_dim,), (right_dim,)), ((), ())), preferred_element_type=f32
    )


def split(x, parts):
    out = []
    for _ in range(parts):
        low = x.astype(bf16)
        out.append(low)
        x = x - low.astype(f32)
    return out


def fold_matrix():
    row = lax.broadcasted_iota(jnp.int32, (R, F), 0)
    col = lax.broadcasted_iota(jnp.int32, (R, F), 1)
    pair = col - 17
    a, b = (pair >> 4) & 15, pair & 15
    d = (b - a) & 15
    target = jnp.where(d <= 7, d * 16 + a, (16 - d) * 16 + b)
    target = jnp.where(d == 8, 144 + jnp.minimum(a, b), target)
    target = jnp.where(col <= 16, 127 + col, target)
    target = jnp.where(col == 0, 152, target)
    return jnp.where(row == target, 1.0, 0.0).astype(bf16)


def twice(shape, dim):
    row = lax.broadcasted_iota(jnp.int32, shape, dim)
    doubled = ((row >= 16) & (row < 128)) | ((row >= 144) & (row < 152))
    return jnp.where(doubled, 2.0, 1.0)


def features(u):
    rows = [u * (u if d == 0 else pltpu.roll(u, FD - d, 0)) * PAIR for d in range(8)]
    rows.append(u * LINEAR)
    rows.append(u[:8] * u[8:] * PAIR)
    rows.append(jnp.where(lax.broadcasted_iota(jnp.int32, (8, T), 0) == 0, 1.0, 0.0))
    return jnp.concatenate(rows, 0)


def feature_grad(u, y):
    acc = 2.0 * y[:16] * u
    for d in range(1, 8):
        part = y[16 * d : 16 * d + 16]
        acc = acc + part * pltpu.roll(u, FD - d, 0) + pltpu.roll(part * u, d, 0)
    last = y[144:152]
    acc = acc + jnp.concatenate([last * u[8:], last * u[:8]], 0)
    return y[128:144] * LINEAR + acc * PAIR


def kernel(
    sizes,
    tok_h, w_h, val_h, cot_h, ks_h, kn_h, qs_h, qn_h,
    tg_h, vg_h, wg_h,
    tok, w, val, cot, ks, kn, qs, qn,
    tg, vg, wg,
    qt, kt, phi_q, phi_k, phi_qt, phi_kt, fold,
    score, a_low, value_part, den, g_low, gs, p_low, norm_t,
    span, contrib, other, pair_out, pair_in, chain_in, chain_out, back_out, back_in, pre, pre_out,
    row_sum, query_sum, norm_own, norm_mate, norm_chip, norm_in, gden_t, dproj_t,
    term, core_in, xs_out, xs_in, xz_out, xz_in, y_part, x_part,
    in_sem, out_sem,
    mate_send, mate_recv, norm_send, norm_recv, other_send, other_recv, pair_send, pair_recv,
    chain_send, chain_recv, back_send, back_recv, pre_send, pre_recv,
    core_send, core_recv, xs_send, xs_recv, xz_send, xz_recv,
    y_send, y_recv, x_send, x_recv,
):
    ns, ny, nx, d_model = sizes
    nz = ns // 2
    rows = d_model // ns
    pairs = nz // 2
    half = H * FD
    piece = half // nx
    dp = lax.axis_index("dp")
    me = lax.axis_index("seq")
    z, c = me // 2, lax.rem(me, 2)
    y, x = dp // nx, lax.rem(dp, nx)
    p, e = z // 2, lax.rem(z, 2)
    mate = 2 * z + (1 - c)
    partner = 4 * p + 2 * (1 - e) + c

    def z_peer(step):
        return lax.rem(z + step, nz)

    def y_peer(step):
        return lax.rem(y + step, ny)

    def x_peer(step):
        return lax.rem(x + step, nx)

    loads = [
        pltpu.make_async_copy(src, dst, in_sem.at[i])
        for i, (src, dst) in enumerate(
            [(tok_h, tok), (w_h, w), (val_h, val), (ks_h, ks), (kn_h, kn), (cot_h, cot), (qs_h, qs), (qn_h, qn)]
        )
    ]
    for load in loads:
        load.start()

    def across_z(step):
        return (dp, 2 * z_peer(step) + c)

    def across_y(step):
        return (y_peer(step) * nx + x, me)

    def across_x(step):
        return (y * nx + x_peer(step), me)

    barrier = pltpu.get_barrier_semaphore()
    pl.semaphore_signal(barrier, inc=1, device_id=(dp, mate), device_id_type=MESH)
    for step in range(1, nz):
        pl.semaphore_signal(barrier, inc=1, device_id=across_z(step), device_id_type=MESH)
    for step in range(1, ny):
        pl.semaphore_signal(barrier, inc=1, device_id=across_y(step), device_id_type=MESH)
    for step in range(1, nx):
        pl.semaphore_signal(barrier, inc=1, device_id=across_x(step), device_id_type=MESH)

    def remote(src, dst, send, recv, device):
        return pltpu.make_async_remote_copy(
            src_ref=src, dst_ref=dst, send_sem=send, recv_sem=recv, device_id=device, device_id_type=MESH
        )

    def mate_copy(which):
        return remote(
            norm_own.at[which], norm_mate.at[which], mate_send.at[which], mate_recv.at[which], (dp, mate)
        )

    def norm_copy(which, step):
        return remote(
            norm_chip.at[which], norm_in.at[which, step],
            norm_send.at[which, step], norm_recv.at[which, step], across_z(step),
        )

    def other_copy(which, k):
        return remote(
            contrib.at[which, (1 - c) * HALF + k], other.at[which, k],
            other_send.at[which, k], other_recv.at[which, k], (dp, mate),
        )

    def pair_copy(which, j):
        return remote(
            pair_out.at[which, j], pair_in.at[which, j],
            pair_send.at[which, j], pair_recv.at[which, j], (dp, partner),
        )

    def chain_copy(which, j):
        target = jnp.clip(p + 1 - 2 * which, 0, pairs - 1)
        return remote(
            chain_out.at[which, j], chain_in.at[which, j],
            chain_send.at[which, j], chain_recv.at[which, j], (dp, 4 * target + 2 * e + c),
        )

    def back_copy(which, j):
        return remote(
            back_out.at[which, j], back_in.at[which, j],
            back_send.at[which, j], back_recv.at[which, j], (dp, partner),
        )

    def pre_copy(which, k):
        return remote(
            pre_out.at[which, k], pre.at[which, c * HALF + k],
            pre_send.at[which, k], pre_recv.at[which, k], (dp, mate),
        )

    def core_copy(part, k):
        return remote(
            term.at[part, 2 * k + (1 - c)], core_in.at[part, k],
            core_send.at[part, k], core_recv.at[part, k], (dp, mate),
        )

    def xs_copy(part, step):
        return remote(
            xs_out.at[part, x_peer(step)], xs_in.at[part, step],
            xs_send.at[part, step], xs_recv.at[part, step], across_x(step),
        )

    def xz_copy(part, step):
        return remote(
            xz_out.at[part, z_peer(step)], xz_in.at[part, step],
            xz_send.at[part, step], xz_recv.at[part, step], across_z(step),
        )

    def y_copy(part, step, source):
        return remote(
            y_part.at[part, source], y_part.at[part, source],
            y_send.at[part, step], y_recv.at[part, step], across_y(step),
        )

    def x_copy(part, step, source):
        return remote(
            x_part.at[part, source], x_part.at[part, source],
            x_send.at[part, step], x_recv.at[part, step], across_x(step),
        )

    coef = twice((R, DV), 0)
    coef_row = twice((H, R), 1)
    head_row = lax.broadcasted_iota(jnp.int32, (H, R), 0)
    fold[...] = fold_matrix()

    def lanes(h):
        return slice(h * DV, (h + 1) * DV)

    def feat(h):
        return slice(h * FD, (h + 1) * FD)

    def fold_rows(source, row_sum):
        def lap(a, carry):
            for d in range(8):
                b = (a + d) & 15
                row = source[0, 0, 17 + 16 * a + b].astype(f32)
                if d:
                    row = row + source[0, 0, 17 + 16 * b + a].astype(f32)
                row_sum[pl.ds(pl.multiple_of((16 * d + a) * H, H), H), :] = row
            row_sum[pl.ds(pl.multiple_of((128 + a) * H, H), H), :] = source[0, 0, 1 + a].astype(f32)
            return carry

        def last_lap(a, carry):
            row = source[0, 0, 25 + 17 * a].astype(f32) + source[0, 0, 17 + 16 * (a + 8) + a].astype(f32)
            row_sum[pl.ds(pl.multiple_of((144 + a) * H, H), H), :] = row
            return carry

        lax.fori_loop(0, 16, lap, 0)
        lax.fori_loop(0, 8, last_lap, 0)
        row_sum[152 * H : 153 * H, :] = source[0, 0, 0].astype(f32)
        row_sum[153 * H :, :] = jnp.zeros(((R - 153) * H, DV), f32)

    def fold_norm(value):
        return sum(dot(part, fold[...], 1, 1) for part in split(value, 3))

    loads[0].wait()
    loads[1].wait()
    projected = dot(tok[0], w[...]).astype(bf16)
    qt[...] = projected[:, : H * FD].astype(f32).T
    kt[...] = projected[:, H * FD :].astype(f32).T
    total = jnp.zeros((H, R), f32)
    ones = jnp.ones((H, T), bf16)
    for h in range(H):
        phi = features(kt[feat(h), :])
        phi_k[h] = phi.astype(bf16)
        total = jnp.where(head_row == h, dot(ones, phi_k[h], 1, 1), total)
    loads[4].wait()
    own_norm = fold_norm(kn[0, 0])
    norm_own[0] = total * coef_row + own_norm
    pl.semaphore_wait(barrier, nz + ny + nx - 2)
    mate_copy(0).start()

    loads[2].wait()
    loads[3].wait()
    fold_rows(ks, row_sum)
    for h in range(H):
        span[h] = row_sum[pl.ds(h, R, stride=H), :]
        contrib[0, h] = dot(phi_k[h], val[0, :, lanes(h)]) * coef + span[h]
    for k in range(HALF):
        other_copy(0, k).start()
    mate_copy(0).wait_recv()
    norm_chip[0] = norm_own[0] + norm_mate[0]
    for step in range(1, nz):
        norm_copy(0, step).start()

    causal = lax.broadcasted_iota(jnp.int32, (T, T), 0) >= lax.broadcasted_iota(jnp.int32, (T, T), 1)
    head_lane = lax.broadcasted_iota(jnp.int32, (T, H * FD), 1) // FD
    query, key = projected[:, : H * FD], projected[:, H * FD :]
    for h in range(H):
        phi = features(qt[feat(h), :])
        phi_q[h] = phi.astype(bf16)
        phi_qt[h] = phi.T.astype(bf16)
        masked = jnp.where(head_lane == h, query, jnp.zeros_like(query))
        s = dot(masked, key, 1, 1) * (1.0 / math.sqrt(FD))
        score[h] = s
        a = jnp.where(causal, 1.0 + s + 0.5 * s * s, 0.0)
        a_low[h] = a.astype(bf16)
        den[h] = jnp.broadcast_to(jnp.sum(a, axis=1, keepdims=True), (T, DV))

    def step_one(which):
        for j in range(2):
            k = 2 * (1 - e) + j
            other_copy(which, k).wait_recv()
            pair_out[which, j] = contrib[which, c * HALF + k] + other[which, k]
            pair_copy(which, j).start()

    def finish(which, k, before):
        second = (c ^ which) == 1
        mine = c * HALF + k
        pre[which, mine] = before + jnp.where(second, other[which, k], 0.0)
        pre_out[which, k] = before + jnp.where(second, 0.0, contrib[which, mine])
        pre_copy(which, k).start()

    def step_two(which):
        first = jnp.where(which == 0, p == 0, p == pairs - 1)
        last = jnp.where(which == 0, p == pairs - 1, p == 0)
        for j in range(2):
            k = 2 * e + j
            other_copy(which, k).wait_recv()
            pair_copy(which, j).wait_recv()

            @pl.when(first)
            def _():
                chain_in[which, j] = jnp.zeros((R, DV), f32)

            @pl.when(jnp.logical_not(first))
            def _():
                chain_copy(which, j).wait_recv()

            before = chain_in[which, j]
            here = contrib[which, c * HALF + k] + other[which, k]
            there = pair_in[which, j]

            @pl.when(jnp.logical_not(last))
            def _():
                chain_out[which, j] = before + (here + there)
                chain_copy(which, j).start()

            second = (e ^ which) == 1
            back_out[which, j] = before + jnp.where(second, 0.0, here)
            back_copy(which, j).start()
            finish(which, k, before + jnp.where(second, there, 0.0))

    def step_three(which):
        for j in range(2):
            back_copy(which, j).wait_recv()
            finish(which, 2 * (1 - e) + j, back_in[which, j])

    def step_four(which):
        for k in range(HALF):
            pre_copy(which, k).wait_recv()

    early = 2 * p < pairs
    late = jnp.logical_not(early)
    step_one(0)
    loads[6].wait()
    fold_rows(qs, query_sum)

    @pl.when(early)
    def _():
        step_two(0)

    for step in range(1, nz):
        norm_copy(0, step).wait_recv()
    norm = own_norm + jnp.where(c == 1, norm_mate[0], 0.0)
    for step in range(1, nz):
        norm = norm + jnp.where(z >= step, norm_in[0, step], 0.0)
    norm_parts = jnp.concatenate(split(norm, 3), 0)
    two_parts = split(norm, 2)
    norm_t[...] = jnp.concatenate(two_parts + two_parts, 0).astype(f32).T.astype(bf16)

    loads[5].wait()
    part_lane = lax.broadcasted_iota(jnp.int32, (T, 3 * H), 1) & (H - 1)
    for h in range(H):
        inner = dot(phi_qt[h], norm_parts, 1, 1)
        whole = den[h] + jnp.sum(jnp.where(part_lane == h, inner, 0.0), axis=1, keepdims=True)
        den[h] = whole
        g_low[h] = (cot[0, :, lanes(h)].astype(f32) / whole).astype(bf16)
        contrib[1, h] = dot(phi_q[h], g_low[h]) * coef + query_sum[pl.ds(h, R, stride=H), :]
    for k in range(HALF):
        other_copy(1, k).start()
    step_one(1)
    for h in range(H):
        value_part[h] = dot(a_low[h], val[0, :, lanes(h)])
        phi_kt[h] = phi_k[h].astype(f32).T.astype(bf16)

    @pl.when(late)
    def _():
        def either(i, carry):
            step_two(i ^ (p == pairs - 1).astype(jnp.int32))
            return carry

        lax.fori_loop(0, 2, either, 0)
        step_three(1)

    step_three(0)
    step_four(0)

    def send_terms(part):
        left = dproj_t[part * half : (part + 1) * half, :].astype(bf16)
        for k in range(nz):
            chunk = pl.ds(pl.multiple_of((2 * k + 1 - c) * rows, rows), rows)
            term[part, 2 * k + 1 - c] = dot(left, tok[0, :, chunk])
            core_copy(part, k).start()
        for k in range(nz):
            chunk = pl.ds(pl.multiple_of((2 * k + c) * rows, rows), rows)
            term[part, 2 * k + c] = dot(left, tok[0, :, chunk])

    def send_x(part):
        for k in range(nz):
            core_copy(part, k).wait_recv()
            both = term[part, 2 * k + c] + core_in[part, k]
            for j in range(nx):
                xs_out[part, j, k] = both[j * piece : (j + 1) * piece]
        for step in range(1, nx):
            xs_copy(part, step).start()

    def send_z(part):
        for step in range(1, nx):
            xs_copy(part, step).wait_recv()
        for k in range(nz):
            acc = xs_out[part, x, k]
            for step in range(1, nx):
                acc = acc + xs_in[part, step, k]
            xz_out[part, k] = acc
        for step in range(1, nz):
            xz_copy(part, step).start()

    def send_y(part):
        acc = xz_out[part, z]
        for step in range(1, nz):
            xz_copy(part, step).wait_recv()
            acc = acc + xz_in[part, step]
        y_part[part, y] = acc
        for step in range(1, ny):
            y_copy(part, step, y).start()

    def send_all(part):
        for step in range(1, ny):
            y_copy(part, step, lax.rem(y + ny - step, ny)).wait_recv()
        acc = y_part[part, 0]
        for j in range(1, ny):
            acc = acc + y_part[part, j]
        x_part[part, x] = acc * (1.0 / (ny * nx))
        for step in range(1, nx):
            x_copy(part, step, x).start()

    def collect(part):
        for step in range(1, nx):
            x_copy(part, step, lax.rem(x + nx - step, nx)).wait_recv()
        wg[:, part * half : (part + 1) * half] = x_part[part].reshape(half, rows).T

    lane = lax.broadcasted_iota(jnp.int32, (T, DV), 1)
    gden_all = jnp.zeros((T, DV), f32)
    for h in range(H):
        p_low[h] = (pre[0, h] + span[h]).astype(bf16)
        numer = dot(phi_qt[h], p_low[h]) + value_part[h]
        weighted = jnp.sum(cot[0, :, lanes(h)].astype(f32) * numer, axis=1, keepdims=True)
        gden = -weighted / (den[h] * den[h])
        gden_all = jnp.where(lane == h, gden, gden_all)
        den[h] = jnp.broadcast_to(gden, (T, DV))
    gden_t[...] = gden_all.T[:H]
    gden_parts = jnp.concatenate(split(gden_t[...], 3), 0)
    total = jnp.zeros((H, R), f32)
    for h in range(H):
        every = dot(gden_parts, phi_q[h], 1, 1)
        every = every[:H] + every[H : 2 * H] + every[2 * H :]
        total = jnp.where(head_row == h, every, total)
    loads[7].wait()
    norm_own[1] = total * coef_row + fold_norm(qn[0, 0])
    mate_copy(1).start()
    mate_copy(1).wait_recv()
    norm_chip[1] = norm_own[1] + norm_mate[1]
    for step in range(1, nz):
        norm_copy(1, step).start()

    high, low = split(gden_t[...], 2)
    gden_rows = jnp.concatenate([high, high, low, low], 0)
    four_row = lax.broadcasted_iota(jnp.int32, (4 * H, T), 0) & (H - 1)
    for h in range(H):
        ga = jnp.where(causal, dot(g_low[h], val[0, :, lanes(h)], 1, 1) + den[h], 0.0)
        gs[h] = (ga * (1.0 + score[h]) * (1.0 / math.sqrt(FD))).astype(bf16)
        only = jnp.where(four_row == h, gden_rows, jnp.zeros_like(gden_rows))
        up = dot(p_low[h], g_low[h], 1, 1) + dot(norm_t[...], only)
        u = qt[feat(h), :]
        dproj_t[feat(h), :] = feature_grad(u, up) + dot(kt[feat(h), :].astype(bf16), gs[h], 1, 1)
    send_terms(0)
    send_x(0)

    @pl.when(early)
    def _():
        step_two(1)
        step_three(1)

    step_four(1)
    for step in range(1, nz):
        norm_copy(1, step).wait_recv()
    norm = jnp.where(c == 0, norm_mate[1], 0.0)
    for step in range(1, nz):
        norm = norm + jnp.where(z < step, norm_in[1, step], 0.0)
    parts = split(norm, 3)
    norm_t[...] = jnp.concatenate(parts + [jnp.zeros_like(parts[0])], 0).astype(f32).T.astype(bf16)
    for h in range(H):
        only = jnp.where(four_row == h, 1.0, 0.0).astype(bf16)
        p_low[h] = pre[1, h].astype(bf16)
        up = dot(p_low[h], val[0, :, lanes(h)], 1, 1) + dot(norm_t[...], only)
        u = kt[feat(h), :]
        inner = dot(qt[feat(h), :].astype(bf16), gs[h])
        dproj_t[H * FD + h * FD : H * FD + (h + 1) * FD, :] = feature_grad(u, up) + inner
    send_terms(1)
    send_z(0)
    send_x(1)

    for h in range(H):
        vg[0, :, lanes(h)] = (dot(a_low[h], g_low[h], 0, 0) + dot(phi_kt[h], p_low[h])).astype(bf16)
    store_vg = pltpu.make_async_copy(vg, vg_h, out_sem.at[0])
    store_vg.start()
    dproj = dproj_t[...].T.astype(bf16)
    cols = min(512, d_model)
    for j in range(d_model // cols):
        tg[0, :, j * cols : (j + 1) * cols] = dot(dproj, w[j * cols : (j + 1) * cols, :], 1, 1).astype(bf16)
    store_tg = pltpu.make_async_copy(tg, tg_h, out_sem.at[1])
    store_tg.start()

    send_y(0)
    send_z(1)
    send_all(0)
    send_y(1)
    collect(0)
    send_all(1)
    collect(1)
    store_wg = pltpu.make_async_copy(wg, wg_h, out_sem.at[2])
    store_wg.start()

    for which in range(2):
        mate_copy(which).wait_send()
        for step in range(1, nz):
            norm_copy(which, step).wait_send()
        last = (p == pairs - 1) if which == 0 else (p == 0)
        for k in range(HALF):
            other_copy(which, k).wait_send()
            pre_copy(which, k).wait_send()
        for j in range(2):
            pair_copy(which, j).wait_send()
            back_copy(which, j).wait_send()

            @pl.when(jnp.logical_not(last))
            def _():
                chain_copy(which, j).wait_send()

    for part in range(2):
        for k in range(nz):
            core_copy(part, k).wait_send()
        for step in range(1, nz):
            xz_copy(part, step).wait_send()
        for step in range(1, ny):
            y_copy(part, step, y).wait_send()
        for step in range(1, nx):
            xs_copy(part, step).wait_send()
            x_copy(part, step, x).wait_send()
    store_vg.wait()
    store_tg.wait()
    store_wg.wait()


def on_device(sizes, tokens, qk_weight, values, cotangent, key_span, key_norm, query_span, query_norm):
    ns, ny, nx, d_model = sizes
    nz = ns // 2
    rows = d_model // ns
    half = H * FD
    piece = half // nx
    width = 2 * H * FD
    key_span, query_span = (jnp.swapaxes(a, 2, 3) for a in (key_span, query_span))
    args = (tokens, qk_weight, values, cotangent, key_span, key_norm, query_span, query_norm)
    out_shape = (
        jax.ShapeDtypeStruct((1, T, d_model), bf16),
        jax.ShapeDtypeStruct((1, T, H * DV), bf16),
        jax.ShapeDtypeStruct((rows, width), f32),
    )
    vmem, dma = pltpu.VMEM, pltpu.SemaphoreType.DMA
    scratch = [vmem(a.shape, a.dtype) for a in args] + [vmem(o.shape, o.dtype) for o in out_shape]
    scratch += [
        vmem((H * FD, T), f32),
        vmem((H * FD, T), f32),
        vmem((H, R, T), bf16),
        vmem((H, R, T), bf16),
        vmem((H, T, R), bf16),
        vmem((H, T, R), bf16),
        vmem((R, F), bf16),
        vmem((H, T, T), f32),
        vmem((H, T, T), bf16),
        vmem((H, T, DV), f32),
        vmem((H, T, DV), f32),
        vmem((H, T, DV), bf16),
        vmem((H, T, T), bf16),
        vmem((H, R, DV), bf16),
        vmem((R, 4 * H), bf16),
        vmem((H, R, DV), f32),
        vmem((2, H, R, DV), f32),
        vmem((2, HALF, R, DV), f32),
        vmem((2, 2, R, DV), f32),
        vmem((2, 2, R, DV), f32),
        vmem((2, 2, R, DV), f32),
        vmem((2, 2, R, DV), f32),
        vmem((2, 2, R, DV), f32),
        vmem((2, 2, R, DV), f32),
        vmem((2, H, R, DV), f32),
        vmem((2, HALF, R, DV), f32),
        vmem((R * H, DV), f32),
        vmem((R * H, DV), f32),
        vmem((2, H, R), f32),
        vmem((2, H, R), f32),
        vmem((2, H, R), f32),
        vmem((2, nz, H, R), f32),
        vmem((H, T), f32),
        vmem((width, T), f32),
        vmem((2, ns, half, rows), f32),
        vmem((2, nz, half, rows), f32),
        vmem((2, nx, nz, piece, rows), f32),
        vmem((2, nx, nz, piece, rows), f32),
        vmem((2, nz, piece, rows), f32),
        vmem((2, nz, piece, rows), f32),
        vmem((2, ny, piece, rows), f32),
        vmem((2, nx, piece, rows), f32),
        dma((8,)), dma((3,)),
        dma((2,)), dma((2,)),
        dma((2, nz)), dma((2, nz)),
        dma((2, HALF)), dma((2, HALF)),
        dma((2, 2)), dma((2, 2)),
        dma((2, 2)), dma((2, 2)),
        dma((2, 2)), dma((2, 2)),
        dma((2, HALF)), dma((2, HALF)),
        dma((2, nz)), dma((2, nz)),
        dma((2, nx)), dma((2, nx)),
        dma((2, nz)), dma((2, nz)),
        dma((2, ny)), dma((2, ny)),
        dma((2, nx)), dma((2, nx)),
    ]
    return pl.pallas_call(
        functools.partial(kernel, sizes),
        out_shape=out_shape,
        in_specs=[pl.BlockSpec(memory_space=pl.ANY)] * 8,
        out_specs=(pl.BlockSpec(memory_space=pl.ANY),) * 3,
        scratch_shapes=scratch,
        compiler_params=pltpu.CompilerParams(
            collective_id=0, has_side_effects=True, vmem_limit_bytes=60 * 1024 * 1024
        ),
    )(*args)


def solution(mesh):
    ns, docs = mesh.shape["seq"], mesh.shape["dp"]
    nx = 4 if docs >= 16 else 2

    def whole(*args):
        sizes = (ns, docs // nx, nx, args[0].shape[2])
        in_specs = (
            P("dp", "seq", None),
            P(),
            P("dp", "seq", None),
            P("dp", "seq", None),
            P("dp", "seq", None, None, None),
            P("dp", "seq", None, None),
            P("dp", "seq", None, None, None),
            P("dp", "seq", None, None),
        )
        out_specs = (P("dp", "seq", None), P("dp", "seq", None), P("seq", None))
        return jax.shard_map(
            functools.partial(on_device, sizes),
            mesh=mesh,
            in_specs=in_specs,
            out_specs=out_specs,
            check_vma=False,
        )(*args)

    return whole
```

```python
import functools
import math

import jax
import jax.numpy as jnp
from jax import lax
from jax.experimental import pallas as pl
from jax.experimental.pallas import tpu as pltpu
from jax.sharding import PartitionSpec as P

H = 8
FD = 16
DV = 128
F = 273
T = 128
R = 160
HALF = H // 2
PARTS = ((0, H * FD), (H * FD, H * FD * 3 // 2), (H * FD * 3 // 2, 2 * H * FD))
PAIR = 1.0 / math.sqrt(2.0 * FD)
LINEAR = 1.0 / FD**0.25
f32 = jnp.float32
bf16 = jnp.bfloat16
MESH = pl.DeviceIdType.MESH


def dot(left, right, left_dim=1, right_dim=0):
    return lax.dot_general(
        left, right, (((left_dim,), (right_dim,)), ((), ())), preferred_element_type=f32
    )


def split(x, parts):
    out = []
    for _ in range(parts):
        low = x.astype(bf16)
        out.append(low)
        x = x - low.astype(f32)
    return out


def fold_matrix():
    row = lax.broadcasted_iota(jnp.int32, (R, F), 0)
    col = lax.broadcasted_iota(jnp.int32, (R, F), 1)
    pair = col - 17
    a, b = (pair >> 4) & 15, pair & 15
    d = (b - a) & 15
    target = jnp.where(d <= 7, d * 16 + a, (16 - d) * 16 + b)
    target = jnp.where(d == 8, 144 + jnp.minimum(a, b), target)
    target = jnp.where(col <= 16, 127 + col, target)
    target = jnp.where(col == 0, 152, target)
    return jnp.where(row == target, 1.0, 0.0).astype(bf16)


def twice(shape, dim):
    row = lax.broadcasted_iota(jnp.int32, shape, dim)
    doubled = ((row >= 16) & (row < 128)) | ((row >= 144) & (row < 152))
    return jnp.where(doubled, 2.0, 1.0)


def features(u):
    rows = [u * (u if d == 0 else pltpu.roll(u, FD - d, 0)) * PAIR for d in range(8)]
    rows.append(u * LINEAR)
    rows.append(u[:8] * u[8:] * PAIR)
    rows.append(jnp.where(lax.broadcasted_iota(jnp.int32, (8, T), 0) == 0, 1.0, 0.0))
    return jnp.concatenate(rows, 0)


def feature_grad(u, y):
    acc = 2.0 * y[:16] * u
    for d in range(1, 8):
        part = y[16 * d : 16 * d + 16]
        acc = acc + part * pltpu.roll(u, FD - d, 0) + pltpu.roll(part * u, d, 0)
    last = y[144:152]
    acc = acc + jnp.concatenate([last * u[8:], last * u[:8]], 0)
    return y[128:144] * LINEAR + acc * PAIR


def kernel(
    sizes,
    tok_h, w_h, val_h, cot_h, ks_h, kn_h, qs_h, qn_h,
    tg_h, vg_h, wg_h,
    tok, w, val, cot, ks, kn, qs, qn,
    tg, vg, wg,
    qt, kt, phi_q, phi_k, phi_qt, phi_kt, fold,
    score, a_low, value_part, den, g_low, gs, p_low, norm_t,
    span, contrib, other, pair_out, pair_in, chain_in, chain_out, back_out, back_in, pre, pre_out,
    row_sum, query_sum, wg_t, norm_own, norm_mate, norm_chip, norm_in, gden_t, dproj_t,
    term, core_in, xs_out, xs_in, xz_out, xz_in, y_part, x_part,
    in_sem, out_sem,
    mate_send, mate_recv, norm_send, norm_recv, other_send, other_recv, pair_send, pair_recv,
    chain_send, chain_recv, back_send, back_recv, pre_send, pre_recv,
    core_send, core_recv, xs_send, xs_recv, xz_send, xz_recv,
    y_send, y_recv, x_send, x_recv,
):
    ns, ny, nx, d_model = sizes
    nz = ns // 2
    rows = d_model // ns
    pairs = nz // 2
    dp = lax.axis_index("dp")
    me = lax.axis_index("seq")
    z, c = me // 2, lax.rem(me, 2)
    y, x = dp // nx, lax.rem(dp, nx)
    p, e = z // 2, lax.rem(z, 2)
    mate = 2 * z + (1 - c)
    partner = 4 * p + 2 * (1 - e) + c

    def z_peer(step):
        return lax.rem(z + step, nz)

    def y_peer(step):
        return lax.rem(y + step, ny)

    def x_peer(step):
        return lax.rem(x + step, nx)

    loads = [
        pltpu.make_async_copy(src, dst, in_sem.at[i])
        for i, (src, dst) in enumerate(
            [(tok_h, tok), (w_h, w), (val_h, val), (ks_h, ks), (kn_h, kn), (cot_h, cot), (qs_h, qs), (qn_h, qn)]
        )
    ]
    for load in loads:
        load.start()

    def across_z(step):
        return (dp, 2 * z_peer(step) + c)

    def across_y(step):
        return (y_peer(step) * nx + x, me)

    def across_x(step):
        return (y * nx + x_peer(step), me)

    barrier = pltpu.get_barrier_semaphore()
    pl.semaphore_signal(barrier, inc=1, device_id=(dp, mate), device_id_type=MESH)
    for step in range(1, nz):
        pl.semaphore_signal(barrier, inc=1, device_id=across_z(step), device_id_type=MESH)
    for step in range(1, ny):
        pl.semaphore_signal(barrier, inc=1, device_id=across_y(step), device_id_type=MESH)
    for step in range(1, nx):
        pl.semaphore_signal(barrier, inc=1, device_id=across_x(step), device_id_type=MESH)

    def remote(src, dst, send, recv, device):
        return pltpu.make_async_remote_copy(
            src_ref=src, dst_ref=dst, send_sem=send, recv_sem=recv, device_id=device, device_id_type=MESH
        )

    def mate_copy(which):
        return remote(
            norm_own.at[which], norm_mate.at[which], mate_send.at[which], mate_recv.at[which], (dp, mate)
        )

    def norm_copy(which, step):
        return remote(
            norm_chip.at[which], norm_in.at[which, step],
            norm_send.at[which, step], norm_recv.at[which, step], across_z(step),
        )

    def other_copy(which, k):
        return remote(
            contrib.at[which, (1 - c) * HALF + k], other.at[which, k],
            other_send.at[which, k], other_recv.at[which, k], (dp, mate),
        )

    def pair_copy(which, j):
        return remote(
            pair_out.at[which, j], pair_in.at[which, j],
            pair_send.at[which, j], pair_recv.at[which, j], (dp, partner),
        )

    def chain_copy(which, j):
        target = jnp.clip(p + 1 - 2 * which, 0, pairs - 1)
        return remote(
            chain_out.at[which, j], chain_in.at[which, j],
            chain_send.at[which, j], chain_recv.at[which, j], (dp, 4 * target + 2 * e + c),
        )

    def back_copy(which, j):
        return remote(
            back_out.at[which, j], back_in.at[which, j],
            back_send.at[which, j], back_recv.at[which, j], (dp, partner),
        )

    def pre_copy(which, k):
        return remote(
            pre_out.at[which, k], pre.at[which, c * HALF + k],
            pre_send.at[which, k], pre_recv.at[which, k], (dp, mate),
        )

    def core_copy(part, k):
        return remote(
            term[part].at[2 * k + (1 - c)], core_in[part].at[k],
            core_send.at[part, k], core_recv.at[part, k], (dp, mate),
        )

    def xs_copy(part, step):
        return remote(
            xs_out[part].at[x_peer(step)], xs_in[part].at[step],
            xs_send.at[part, step], xs_recv.at[part, step], across_x(step),
        )

    def xz_copy(part, step):
        return remote(
            xz_out[part].at[z_peer(step)], xz_in[part].at[step],
            xz_send.at[part, step], xz_recv.at[part, step], across_z(step),
        )

    def y_copy(part, step, source):
        return remote(
            y_part[part].at[source], y_part[part].at[source],
            y_send.at[part, step], y_recv.at[part, step], across_y(step),
        )

    def x_copy(part, step, source):
        return remote(
            x_part[part].at[source], x_part[part].at[source],
            x_send.at[part, step], x_recv.at[part, step], across_x(step),
        )

    coef = twice((R, DV), 0)
    coef_row = twice((H, R), 1)
    head_row = lax.broadcasted_iota(jnp.int32, (H, R), 0)
    fold[...] = fold_matrix()

    def lanes(h):
        return slice(h * DV, (h + 1) * DV)

    def feat(h):
        return slice(h * FD, (h + 1) * FD)

    def fold_rows(source, row_sum):
        def lap(a, carry):
            for d in range(8):
                b = (a + d) & 15
                row = source[0, 0, 17 + 16 * a + b].astype(f32)
                if d:
                    row = row + source[0, 0, 17 + 16 * b + a].astype(f32)
                row_sum[pl.ds(pl.multiple_of((16 * d + a) * H, H), H), :] = row
            row_sum[pl.ds(pl.multiple_of((128 + a) * H, H), H), :] = source[0, 0, 1 + a].astype(f32)
            return carry

        def last_lap(a, carry):
            row = source[0, 0, 25 + 17 * a].astype(f32) + source[0, 0, 17 + 16 * (a + 8) + a].astype(f32)
            row_sum[pl.ds(pl.multiple_of((144 + a) * H, H), H), :] = row
            return carry

        lax.fori_loop(0, 16, lap, 0)
        lax.fori_loop(0, 8, last_lap, 0)
        row_sum[152 * H : 153 * H, :] = source[0, 0, 0].astype(f32)
        row_sum[153 * H :, :] = jnp.zeros(((R - 153) * H, DV), f32)

    def fold_norm(value):
        return sum(dot(part, fold[...], 1, 1) for part in split(value, 3))

    loads[0].wait()
    loads[1].wait()
    projected = dot(tok[0], w[...]).astype(bf16)
    qt[...] = projected[:, : H * FD].astype(f32).T
    kt[...] = projected[:, H * FD :].astype(f32).T
    total = jnp.zeros((H, R), f32)
    ones = jnp.ones((H, T), bf16)
    for h in range(H):
        phi = features(kt[feat(h), :])
        phi_k[h] = phi.astype(bf16)
        total = jnp.where(head_row == h, dot(ones, phi_k[h], 1, 1), total)
    loads[4].wait()
    own_norm = fold_norm(kn[0, 0])
    norm_own[0] = total * coef_row + own_norm
    pl.semaphore_wait(barrier, nz + ny + nx - 2)
    mate_copy(0).start()

    loads[2].wait()
    loads[3].wait()
    fold_rows(ks, row_sum)
    for h in range(H):
        span[h] = row_sum[pl.ds(h, R, stride=H), :]
        contrib[0, h] = dot(phi_k[h], val[0, :, lanes(h)]) * coef + span[h]
    for k in range(HALF):
        other_copy(0, k).start()
    mate_copy(0).wait_recv()
    norm_chip[0] = norm_own[0] + norm_mate[0]
    for step in range(1, nz):
        norm_copy(0, step).start()

    causal = lax.broadcasted_iota(jnp.int32, (T, T), 0) >= lax.broadcasted_iota(jnp.int32, (T, T), 1)
    head_lane = lax.broadcasted_iota(jnp.int32, (T, H * FD), 1) // FD
    query, key = projected[:, : H * FD], projected[:, H * FD :]
    for h in range(H):
        phi = features(qt[feat(h), :])
        phi_q[h] = phi.astype(bf16)
        phi_qt[h] = phi.T.astype(bf16)
        masked = jnp.where(head_lane == h, query, jnp.zeros_like(query))
        s = dot(masked, key, 1, 1) * (1.0 / math.sqrt(FD))
        score[h] = s
        a = jnp.where(causal, 1.0 + s + 0.5 * s * s, 0.0)
        a_low[h] = a.astype(bf16)
        den[h] = jnp.broadcast_to(jnp.sum(a, axis=1, keepdims=True), (T, DV))

    def step_one(which):
        for j in range(2):
            k = 2 * (1 - e) + j
            other_copy(which, k).wait_recv()
            pair_out[which, j] = contrib[which, c * HALF + k] + other[which, k]
            pair_copy(which, j).start()

    def finish(which, k, before):
        second = (c ^ which) == 1
        mine = c * HALF + k
        pre[which, mine] = before + jnp.where(second, other[which, k], 0.0)
        pre_out[which, k] = before + jnp.where(second, 0.0, contrib[which, mine])
        pre_copy(which, k).start()

    def step_two(which):
        first = jnp.where(which == 0, p == 0, p == pairs - 1)
        last = jnp.where(which == 0, p == pairs - 1, p == 0)
        for j in range(2):
            k = 2 * e + j
            other_copy(which, k).wait_recv()
            pair_copy(which, j).wait_recv()

            @pl.when(first)
            def _():
                chain_in[which, j] = jnp.zeros((R, DV), f32)

            @pl.when(jnp.logical_not(first))
            def _():
                chain_copy(which, j).wait_recv()

            before = chain_in[which, j]
            here = contrib[which, c * HALF + k] + other[which, k]
            there = pair_in[which, j]

            @pl.when(jnp.logical_not(last))
            def _():
                chain_out[which, j] = before + (here + there)
                chain_copy(which, j).start()

            second = (e ^ which) == 1
            back_out[which, j] = before + jnp.where(second, 0.0, here)
            back_copy(which, j).start()
            finish(which, k, before + jnp.where(second, there, 0.0))

    def step_three(which):
        for j in range(2):
            back_copy(which, j).wait_recv()
            finish(which, 2 * (1 - e) + j, back_in[which, j])

    def step_four(which):
        for k in range(HALF):
            pre_copy(which, k).wait_recv()

    early = 2 * p < pairs
    late = jnp.logical_not(early)
    step_one(0)
    loads[6].wait()
    fold_rows(qs, query_sum)

    @pl.when(early)
    def _():
        step_two(0)

    for step in range(1, nz):
        norm_copy(0, step).wait_recv()
    norm = own_norm + jnp.where(c == 1, norm_mate[0], 0.0)
    for step in range(1, nz):
        norm = norm + jnp.where(z >= step, norm_in[0, step], 0.0)
    norm_parts = jnp.concatenate(split(norm, 3), 0)
    two_parts = split(norm, 2)
    norm_t[...] = jnp.concatenate(two_parts + two_parts, 0).astype(f32).T.astype(bf16)

    loads[5].wait()
    part_lane = lax.broadcasted_iota(jnp.int32, (T, 3 * H), 1) & (H - 1)
    for h in range(H):
        inner = dot(phi_qt[h], norm_parts, 1, 1)
        whole = den[h] + jnp.sum(jnp.where(part_lane == h, inner, 0.0), axis=1, keepdims=True)
        den[h] = whole
        g_low[h] = (cot[0, :, lanes(h)].astype(f32) / whole).astype(bf16)
        contrib[1, h] = dot(phi_q[h], g_low[h]) * coef + query_sum[pl.ds(h, R, stride=H), :]
    for k in range(HALF):
        other_copy(1, k).start()
    step_one(1)
    for h in range(H):
        value_part[h] = dot(a_low[h], val[0, :, lanes(h)])
        phi_kt[h] = phi_k[h].astype(f32).T.astype(bf16)

    @pl.when(late)
    def _():
        def either(i, carry):
            step_two(i ^ (p == pairs - 1).astype(jnp.int32))
            return carry

        lax.fori_loop(0, 2, either, 0)
        step_three(1)

    step_three(0)
    step_four(0)

    def send_terms(part):
        left = dproj_t[PARTS[part][0] : PARTS[part][1], :].astype(bf16)
        for k in range(nz):
            chunk = pl.ds(pl.multiple_of((2 * k + 1 - c) * rows, rows), rows)
            term[part][2 * k + 1 - c] = dot(left, tok[0, :, chunk])
            core_copy(part, k).start()
        for k in range(nz):
            chunk = pl.ds(pl.multiple_of((2 * k + c) * rows, rows), rows)
            term[part][2 * k + c] = dot(left, tok[0, :, chunk])

    def send_x(part):
        for k in range(nz):
            core_copy(part, k).wait_recv()
            both = term[part][2 * k + c] + core_in[part][k]
            piece = both.shape[0] // nx
            for j in range(nx):
                xs_out[part][j, k] = both[j * piece : (j + 1) * piece]
        for step in range(1, nx):
            xs_copy(part, step).start()

    def send_z(part):
        for step in range(1, nx):
            xs_copy(part, step).wait_recv()
        for k in range(nz):
            acc = xs_out[part][x, k]
            for step in range(1, nx):
                acc = acc + xs_in[part][step, k]
            xz_out[part][k] = acc
        for step in range(1, nz):
            xz_copy(part, step).start()

    def send_y(part):
        acc = xz_out[part][z]
        for step in range(1, nz):
            xz_copy(part, step).wait_recv()
            acc = acc + xz_in[part][step]
        y_part[part][y] = acc
        for step in range(1, ny):
            y_copy(part, step, y).start()

    def send_all(part):
        for step in range(1, ny):
            y_copy(part, step, lax.rem(y + ny - step, ny)).wait_recv()
        acc = y_part[part][0]
        for j in range(1, ny):
            acc = acc + y_part[part][j]
        x_part[part][x] = acc * (1.0 / (ny * nx))
        for step in range(1, nx):
            x_copy(part, step, x).start()

    def collect(part):
        for step in range(1, nx):
            x_copy(part, step, lax.rem(x + nx - step, nx)).wait_recv()
        start, stop = PARTS[part]
        wg_t[start:stop, :] = x_part[part][...].reshape(stop - start, rows)

    lane = lax.broadcasted_iota(jnp.int32, (T, DV), 1)
    gden_all = jnp.zeros((T, DV), f32)
    for h in range(H):
        p_low[h] = (pre[0, h] + span[h]).astype(bf16)
        numer = dot(phi_qt[h], p_low[h]) + value_part[h]
        weighted = jnp.sum(cot[0, :, lanes(h)].astype(f32) * numer, axis=1, keepdims=True)
        gden = -weighted / (den[h] * den[h])
        gden_all = jnp.where(lane == h, gden, gden_all)
        den[h] = jnp.broadcast_to(gden, (T, DV))
    gden_t[...] = gden_all.T[:H]
    gden_parts = jnp.concatenate(split(gden_t[...], 3), 0)
    total = jnp.zeros((H, R), f32)
    for h in range(H):
        every = dot(gden_parts, phi_q[h], 1, 1)
        every = every[:H] + every[H : 2 * H] + every[2 * H :]
        total = jnp.where(head_row == h, every, total)
    loads[7].wait()
    norm_own[1] = total * coef_row + fold_norm(qn[0, 0])
    mate_copy(1).start()
    mate_copy(1).wait_recv()
    norm_chip[1] = norm_own[1] + norm_mate[1]
    for step in range(1, nz):
        norm_copy(1, step).start()

    high, low = split(gden_t[...], 2)
    gden_rows = jnp.concatenate([high, high, low, low], 0)
    four_row = lax.broadcasted_iota(jnp.int32, (4 * H, T), 0) & (H - 1)
    for h in range(H):
        ga = jnp.where(causal, dot(g_low[h], val[0, :, lanes(h)], 1, 1) + den[h], 0.0)
        gs[h] = (ga * (1.0 + score[h]) * (1.0 / math.sqrt(FD))).astype(bf16)
        only = jnp.where(four_row == h, gden_rows, jnp.zeros_like(gden_rows))
        up = dot(p_low[h], g_low[h], 1, 1) + dot(norm_t[...], only)
        u = qt[feat(h), :]
        dproj_t[feat(h), :] = feature_grad(u, up) + dot(kt[feat(h), :].astype(bf16), gs[h], 1, 1)
    send_terms(0)
    send_x(0)

    @pl.when(early)
    def _():
        step_two(1)
        step_three(1)

    step_four(1)
    for step in range(1, nz):
        norm_copy(1, step).wait_recv()
    norm = jnp.where(c == 0, norm_mate[1], 0.0)
    for step in range(1, nz):
        norm = norm + jnp.where(z < step, norm_in[1, step], 0.0)
    parts = split(norm, 3)
    norm_t[...] = jnp.concatenate(parts + [jnp.zeros_like(parts[0])], 0).astype(f32).T.astype(bf16)
    for h in range(H):
        only = jnp.where(four_row == h, 1.0, 0.0).astype(bf16)
        p_low[h] = pre[1, h].astype(bf16)
        up = dot(p_low[h], val[0, :, lanes(h)], 1, 1) + dot(norm_t[...], only)
        u = kt[feat(h), :]
        inner = dot(qt[feat(h), :].astype(bf16), gs[h])
        dproj_t[H * FD + h * FD : H * FD + (h + 1) * FD, :] = feature_grad(u, up) + inner
        if h == HALF - 1:
            send_terms(1)
    send_terms(2)
    send_z(0)
    send_x(1)
    send_x(2)

    for h in range(H):
        vg[0, :, lanes(h)] = (dot(a_low[h], g_low[h], 0, 0) + dot(phi_kt[h], p_low[h])).astype(bf16)
    store_vg = pltpu.make_async_copy(vg, vg_h, out_sem.at[0])
    store_vg.start()
    dproj = dproj_t[...].T.astype(bf16)
    cols = min(512, d_model)
    for j in range(d_model // cols):
        tg[0, :, j * cols : (j + 1) * cols] = dot(dproj, w[j * cols : (j + 1) * cols, :], 1, 1).astype(bf16)
    store_tg = pltpu.make_async_copy(tg, tg_h, out_sem.at[1])
    store_tg.start()

    send_y(0)
    send_z(1)
    send_z(2)
    send_all(0)
    send_y(1)
    send_y(2)
    collect(0)
    send_all(1)
    send_all(2)
    collect(1)
    collect(2)
    wg[...] = wg_t[...].T
    store_wg = pltpu.make_async_copy(wg, wg_h, out_sem.at[2])
    store_wg.start()

    for which in range(2):
        mate_copy(which).wait_send()
        for step in range(1, nz):
            norm_copy(which, step).wait_send()
        last = (p == pairs - 1) if which == 0 else (p == 0)
        for k in range(HALF):
            other_copy(which, k).wait_send()
            pre_copy(which, k).wait_send()
        for j in range(2):
            pair_copy(which, j).wait_send()
            back_copy(which, j).wait_send()

            @pl.when(jnp.logical_not(last))
            def _():
                chain_copy(which, j).wait_send()

    for part in range(len(PARTS)):
        for k in range(nz):
            core_copy(part, k).wait_send()
        for step in range(1, nz):
            xz_copy(part, step).wait_send()
        for step in range(1, ny):
            y_copy(part, step, y).wait_send()
        for step in range(1, nx):
            xs_copy(part, step).wait_send()
            x_copy(part, step, x).wait_send()
    store_vg.wait()
    store_tg.wait()
    store_wg.wait()


def hand_over(*refs):
    sems = refs[6]
    copies = [pltpu.make_async_copy(refs[i], refs[3 + i], sems.at[i]) for i in range(3)]
    for copy in copies:
        copy.start()
    for copy in copies:
        copy.wait()


def on_device(sizes, tokens, qk_weight, values, cotangent, key_span, key_norm, query_span, query_norm):
    ns, ny, nx, d_model = sizes
    nz = ns // 2
    rows = d_model // ns
    width = 2 * H * FD
    key_span, query_span = (jnp.swapaxes(a, 2, 3) for a in (key_span, query_span))
    args = (tokens, qk_weight, values, cotangent, key_span, key_norm, query_span, query_norm)
    out_shape = (
        jax.ShapeDtypeStruct((1, T, d_model), bf16),
        jax.ShapeDtypeStruct((1, T, H * DV), bf16),
        jax.ShapeDtypeStruct((rows, width), f32),
    )
    vmem, dma = pltpu.VMEM, pltpu.SemaphoreType.DMA

    def each(shape):
        return tuple(vmem(shape(stop - start), f32) for start, stop in PARTS)

    scratch = [vmem(a.shape, a.dtype) for a in args] + [vmem(o.shape, o.dtype) for o in out_shape]
    scratch += [
        vmem((H * FD, T), f32),
        vmem((H * FD, T), f32),
        vmem((H, R, T), bf16),
        vmem((H, R, T), bf16),
        vmem((H, T, R), bf16),
        vmem((H, T, R), bf16),
        vmem((R, F), bf16),
        vmem((H, T, T), f32),
        vmem((H, T, T), bf16),
        vmem((H, T, DV), f32),
        vmem((H, T, DV), f32),
        vmem((H, T, DV), bf16),
        vmem((H, T, T), bf16),
        vmem((H, R, DV), bf16),
        vmem((R, 4 * H), bf16),
        vmem((H, R, DV), f32),
        vmem((2, H, R, DV), f32),
        vmem((2, HALF, R, DV), f32),
        vmem((2, 2, R, DV), f32),
        vmem((2, 2, R, DV), f32),
        vmem((2, 2, R, DV), f32),
        vmem((2, 2, R, DV), f32),
        vmem((2, 2, R, DV), f32),
        vmem((2, 2, R, DV), f32),
        vmem((2, H, R, DV), f32),
        vmem((2, HALF, R, DV), f32),
        vmem((R * H, DV), f32),
        vmem((R * H, DV), f32),
        vmem((width, rows), f32),
        vmem((2, H, R), f32),
        vmem((2, H, R), f32),
        vmem((2, H, R), f32),
        vmem((2, nz, H, R), f32),
        vmem((H, T), f32),
        vmem((width, T), f32),
        each(lambda n: (ns, n, rows)),
        each(lambda n: (nz, n, rows)),
        each(lambda n: (nx, nz, n // nx, rows)),
        each(lambda n: (nx, nz, n // nx, rows)),
        each(lambda n: (nz, n // nx, rows)),
        each(lambda n: (nz, n // nx, rows)),
        each(lambda n: (ny, n // nx, rows)),
        each(lambda n: (nx, n // nx, rows)),
        dma((8,)), dma((3,)),
        dma((2,)), dma((2,)),
        dma((2, nz)), dma((2, nz)),
        dma((2, HALF)), dma((2, HALF)),
        dma((2, 2)), dma((2, 2)),
        dma((2, 2)), dma((2, 2)),
        dma((2, 2)), dma((2, 2)),
        dma((2, HALF)), dma((2, HALF)),
        dma((len(PARTS), nz)), dma((len(PARTS), nz)),
        dma((len(PARTS), nx)), dma((len(PARTS), nx)),
        dma((len(PARTS), nz)), dma((len(PARTS), nz)),
        dma((len(PARTS), ny)), dma((len(PARTS), ny)),
        dma((len(PARTS), nx)), dma((len(PARTS), nx)),
    ]
    results = pl.pallas_call(
        functools.partial(kernel, sizes),
        out_shape=out_shape,
        in_specs=[pl.BlockSpec(memory_space=pl.ANY)] * 8,
        out_specs=(pl.BlockSpec(memory_space=pl.ANY),) * 3,
        scratch_shapes=scratch,
        compiler_params=pltpu.CompilerParams(
            collective_id=0, has_side_effects=True, vmem_limit_bytes=60 * 1024 * 1024
        ),
    )(*args)
    return pl.pallas_call(
        hand_over,
        out_shape=out_shape,
        in_specs=[pl.BlockSpec(memory_space=pl.ANY)] * 3,
        out_specs=(pl.BlockSpec(memory_space=pl.ANY),) * 3,
        scratch_shapes=[dma((3,))],
    )(*results)


def solution(mesh):
    ns, docs = mesh.shape["seq"], mesh.shape["dp"]
    nx = 4 if docs >= 16 else 2

    def whole(*args):
        sizes = (ns, docs // nx, nx, args[0].shape[2])
        in_specs = (
            P("dp", "seq", None),
            P(),
            P("dp", "seq", None),
            P("dp", "seq", None),
            P("dp", "seq", None, None, None),
            P("dp", "seq", None, None),
            P("dp", "seq", None, None, None),
            P("dp", "seq", None, None),
        )
        out_specs = (P("dp", "seq", None), P("dp", "seq", None), P("seq", None))
        return jax.shard_map(
            functools.partial(on_device, sizes),
            mesh=mesh,
            in_specs=in_specs,
            out_specs=out_specs,
            check_vma=False,
        )(*args)

    return whole
```

```python
import functools
import math

import jax
import jax.numpy as jnp
from jax import lax
from jax.experimental import pallas as pl
from jax.experimental.pallas import tpu as pltpu
from jax.sharding import PartitionSpec as P

H = 8
FD = 16
DV = 128
F = 273
T = 128
R = 160
HALF = H // 2
PARTS = ((0, H * FD), (H * FD, 2 * H * FD))
PAIR = 1.0 / math.sqrt(2.0 * FD)
LINEAR = 1.0 / FD**0.25
f32 = jnp.float32
bf16 = jnp.bfloat16
MESH = pl.DeviceIdType.MESH


def dot(left, right, left_dim=1, right_dim=0):
    return lax.dot_general(
        left, right, (((left_dim,), (right_dim,)), ((), ())), preferred_element_type=f32
    )


def far_first(n):
    return sorted(range(1, n), key=lambda step: -min(step, n - step))


def split(x, parts):
    out = []
    for _ in range(parts):
        low = x.astype(bf16)
        out.append(low)
        x = x - low.astype(f32)
    return out


def fold_matrix():
    row = lax.broadcasted_iota(jnp.int32, (R, F), 0)
    col = lax.broadcasted_iota(jnp.int32, (R, F), 1)
    pair = col - 17
    a, b = (pair >> 4) & 15, pair & 15
    d = (b - a) & 15
    target = jnp.where(d <= 7, d * 16 + a, (16 - d) * 16 + b)
    target = jnp.where(d == 8, 144 + jnp.minimum(a, b), target)
    target = jnp.where(col <= 16, 127 + col, target)
    target = jnp.where(col == 0, 152, target)
    return jnp.where(row == target, 1.0, 0.0).astype(bf16)


def twice(shape, dim):
    row = lax.broadcasted_iota(jnp.int32, shape, dim)
    doubled = ((row >= 16) & (row < 128)) | ((row >= 144) & (row < 152))
    return jnp.where(doubled, 2.0, 1.0)


def features(u):
    rows = [u * (u if d == 0 else pltpu.roll(u, FD - d, 0)) * PAIR for d in range(8)]
    rows.append(u * LINEAR)
    rows.append(u[:8] * u[8:] * PAIR)
    rows.append(jnp.where(lax.broadcasted_iota(jnp.int32, (8, T), 0) == 0, 1.0, 0.0))
    return jnp.concatenate(rows, 0)


def feature_grad(u, y):
    acc = 2.0 * y[:16] * u
    for d in range(1, 8):
        part = y[16 * d : 16 * d + 16]
        acc = acc + part * pltpu.roll(u, FD - d, 0) + pltpu.roll(part * u, d, 0)
    last = y[144:152]
    acc = acc + jnp.concatenate([last * u[8:], last * u[:8]], 0)
    return y[128:144] * LINEAR + acc * PAIR


def kernel(
    sizes,
    tok_h, w_h, val_h, cot_h, ks_h, kn_h, qs_h, qn_h,
    tg_h, vg_h, wg_h,
    tok, w, val, cot, ks, kn, qs, qn,
    tg, vg, wg,
    qt, kt, phi_q, phi_k, phi_qt, phi_kt, fold,
    score, a_low, value_part, den, g_low, gs, p_low, norm_t,
    span, contrib, other, pair_out, pair_in, chain_in, chain_out, back_out, back_in, pre, pre_out,
    row_sum, query_sum, wg_t, norm_own, norm_mate, norm_chip, norm_in, gden_t, dproj_t,
    term, core_in, xs_out, xs_in, xz_out, xz_in, y_part, x_part,
    in_sem, out_sem,
    mate_send, mate_recv, norm_send, norm_recv, other_send, other_recv, pair_send, pair_recv,
    chain_send, chain_recv, back_send, back_recv, pre_send, pre_recv,
    core_send, core_recv, xs_send, xs_recv, xz_send, xz_recv,
    y_send, y_recv, x_send, x_recv,
):
    ns, ny, nx, d_model = sizes
    nz = ns // 2
    rows = d_model // ns
    pairs = nz // 2
    dp = lax.axis_index("dp")
    me = lax.axis_index("seq")
    z, c = me // 2, lax.rem(me, 2)
    y, x = dp // nx, lax.rem(dp, nx)
    p, e = z // 2, lax.rem(z, 2)
    mate = 2 * z + (1 - c)
    partner = 4 * p + 2 * (1 - e) + c

    def z_peer(step):
        return lax.rem(z + step, nz)

    def y_peer(step):
        return lax.rem(y + step, ny)

    def x_peer(step):
        return lax.rem(x + step, nx)

    loads = [
        pltpu.make_async_copy(src, dst, in_sem.at[i])
        for i, (src, dst) in enumerate(
            [(tok_h, tok), (w_h, w), (val_h, val), (ks_h, ks), (kn_h, kn), (cot_h, cot), (qs_h, qs), (qn_h, qn)]
        )
    ]
    for load in loads:
        load.start()

    def across_z(step):
        return (dp, 2 * z_peer(step) + c)

    def across_y(step):
        return (y_peer(step) * nx + x, me)

    def across_x(step):
        return (y * nx + x_peer(step), me)

    barrier = pltpu.get_barrier_semaphore()
    pl.semaphore_signal(barrier, inc=1, device_id=(dp, mate), device_id_type=MESH)
    for step in range(1, nz):
        pl.semaphore_signal(barrier, inc=1, device_id=across_z(step), device_id_type=MESH)
    for step in range(1, ny):
        pl.semaphore_signal(barrier, inc=1, device_id=across_y(step), device_id_type=MESH)
    for step in range(1, nx):
        pl.semaphore_signal(barrier, inc=1, device_id=across_x(step), device_id_type=MESH)

    def remote(src, dst, send, recv, device):
        return pltpu.make_async_remote_copy(
            src_ref=src, dst_ref=dst, send_sem=send, recv_sem=recv, device_id=device, device_id_type=MESH
        )

    def mate_copy(which):
        return remote(
            norm_own.at[which], norm_mate.at[which], mate_send.at[which], mate_recv.at[which], (dp, mate)
        )

    def norm_copy(which, step):
        return remote(
            norm_chip.at[which], norm_in.at[which, step],
            norm_send.at[which, step], norm_recv.at[which, step], across_z(step),
        )

    def other_copy(which, k):
        return remote(
            contrib.at[which, (1 - c) * HALF + k], other.at[which, k],
            other_send.at[which, k], other_recv.at[which, k], (dp, mate),
        )

    def pair_copy(which, j):
        return remote(
            pair_out.at[which, j], pair_in.at[which, j],
            pair_send.at[which, j], pair_recv.at[which, j], (dp, partner),
        )

    def chain_copy(which, j):
        target = jnp.clip(p + 1 - 2 * which, 0, pairs - 1)
        return remote(
            chain_out.at[which, j], chain_in.at[which, j],
            chain_send.at[which, j], chain_recv.at[which, j], (dp, 4 * target + 2 * e + c),
        )

    def back_copy(which, j):
        return remote(
            back_out.at[which, j], back_in.at[which, j],
            back_send.at[which, j], back_recv.at[which, j], (dp, partner),
        )

    def pre_copy(which, k):
        return remote(
            pre_out.at[which, k], pre.at[which, c * HALF + k],
            pre_send.at[which, k], pre_recv.at[which, k], (dp, mate),
        )

    def core_copy(part, j):
        run = pl.ds(j * (nz // 2), nz // 2)
        return remote(
            term[part].at[1 - c, run], core_in[part].at[run],
            core_send.at[part, j], core_recv.at[part, j], (dp, mate),
        )

    def xs_copy(part, step):
        return remote(
            xs_out[part].at[x_peer(step)], xs_in[part].at[step],
            xs_send.at[part, step], xs_recv.at[part, step], across_x(step),
        )

    def xz_copy(part, step):
        return remote(
            xz_out[part].at[z_peer(step)], xz_in[part].at[step],
            xz_send.at[part, step], xz_recv.at[part, step], across_z(step),
        )

    def y_copy(part, step, source):
        return remote(
            y_part[part].at[source], y_part[part].at[source],
            y_send.at[part, step], y_recv.at[part, step], across_y(step),
        )

    def x_copy(part, step, source):
        return remote(
            x_part[part].at[source], x_part[part].at[source],
            x_send.at[part, step], x_recv.at[part, step], across_x(step),
        )

    coef = twice((R, DV), 0)
    coef_row = twice((H, R), 1)
    head_row = lax.broadcasted_iota(jnp.int32, (H, R), 0)
    fold[...] = fold_matrix()

    def lanes(h):
        return slice(h * DV, (h + 1) * DV)

    def feat(h):
        return slice(h * FD, (h + 1) * FD)

    def fold_rows(source, row_sum):
        def lap(a, carry):
            for d in range(8):
                b = (a + d) & 15
                row = source[0, 0, 17 + 16 * a + b].astype(f32)
                if d:
                    row = row + source[0, 0, 17 + 16 * b + a].astype(f32)
                row_sum[pl.ds(pl.multiple_of((16 * d + a) * H, H), H), :] = row
            row_sum[pl.ds(pl.multiple_of((128 + a) * H, H), H), :] = source[0, 0, 1 + a].astype(f32)
            return carry

        def last_lap(a, carry):
            row = source[0, 0, 25 + 17 * a].astype(f32) + source[0, 0, 17 + 16 * (a + 8) + a].astype(f32)
            row_sum[pl.ds(pl.multiple_of((144 + a) * H, H), H), :] = row
            return carry

        lax.fori_loop(0, 16, lap, 0)
        lax.fori_loop(0, 8, last_lap, 0)
        row_sum[152 * H : 153 * H, :] = source[0, 0, 0].astype(f32)
        row_sum[153 * H :, :] = jnp.zeros(((R - 153) * H, DV), f32)

    def fold_norm(value):
        return sum(dot(part, fold[...], 1, 1) for part in split(value, 3))

    loads[0].wait()
    loads[1].wait()
    projected = dot(tok[0], w[...]).astype(bf16)
    qt[...] = projected[:, : H * FD].astype(f32).T
    kt[...] = projected[:, H * FD :].astype(f32).T
    total = jnp.zeros((H, R), f32)
    ones = jnp.ones((H, T), bf16)
    for h in range(H):
        phi = features(kt[feat(h), :])
        phi_k[h] = phi.astype(bf16)
        total = jnp.where(head_row == h, dot(ones, phi_k[h], 1, 1), total)
    loads[4].wait()
    own_norm = fold_norm(kn[0, 0])
    norm_own[0] = total * coef_row + own_norm
    pl.semaphore_wait(barrier, nz + ny + nx - 2)
    mate_copy(0).start()

    loads[2].wait()
    loads[3].wait()
    fold_rows(ks, row_sum)
    for h in range(H):
        span[h] = row_sum[pl.ds(h, R, stride=H), :]
        contrib[0, h] = dot(phi_k[h], val[0, :, lanes(h)]) * coef + span[h]
    for k in range(HALF):
        other_copy(0, k).start()
    mate_copy(0).wait_recv()
    norm_chip[0] = norm_own[0] + norm_mate[0]
    for step in far_first(nz):
        norm_copy(0, step).start()

    causal = lax.broadcasted_iota(jnp.int32, (T, T), 0) >= lax.broadcasted_iota(jnp.int32, (T, T), 1)
    head_lane = lax.broadcasted_iota(jnp.int32, (T, H * FD), 1) // FD
    query, key = projected[:, : H * FD], projected[:, H * FD :]
    for h in range(H):
        phi = features(qt[feat(h), :])
        phi_q[h] = phi.astype(bf16)
        phi_qt[h] = phi.T.astype(bf16)
        masked = jnp.where(head_lane == h, query, jnp.zeros_like(query))
        s = dot(masked, key, 1, 1) * (1.0 / math.sqrt(FD))
        score[h] = s
        a = jnp.where(causal, 1.0 + s + 0.5 * s * s, 0.0)
        a_low[h] = a.astype(bf16)
        den[h] = jnp.broadcast_to(jnp.sum(a, axis=1, keepdims=True), (T, DV))

    def step_one(which):
        for j in range(2):
            k = 2 * (1 - e) + j
            other_copy(which, k).wait_recv()
            pair_out[which, j] = contrib[which, c * HALF + k] + other[which, k]
            pair_copy(which, j).start()

    def finish(which, k, before):
        second = (c ^ which) == 1
        mine = c * HALF + k
        pre[which, mine] = before + jnp.where(second, other[which, k], 0.0)
        pre_out[which, k] = before + jnp.where(second, 0.0, contrib[which, mine])
        pre_copy(which, k).start()

    def step_two(which):
        first = jnp.where(which == 0, p == 0, p == pairs - 1)
        last = jnp.where(which == 0, p == pairs - 1, p == 0)
        for j in range(2):
            k = 2 * e + j
            other_copy(which, k).wait_recv()
            pair_copy(which, j).wait_recv()

            @pl.when(first)
            def _():
                chain_in[which, j] = jnp.zeros((R, DV), f32)

            @pl.when(jnp.logical_not(first))
            def _():
                chain_copy(which, j).wait_recv()

            before = chain_in[which, j]
            here = contrib[which, c * HALF + k] + other[which, k]
            there = pair_in[which, j]

            @pl.when(jnp.logical_not(last))
            def _():
                chain_out[which, j] = before + (here + there)
                chain_copy(which, j).start()

            second = (e ^ which) == 1
            back_out[which, j] = before + jnp.where(second, 0.0, here)
            back_copy(which, j).start()
            finish(which, k, before + jnp.where(second, there, 0.0))

    def step_three(which):
        for j in range(2):
            back_copy(which, j).wait_recv()
            finish(which, 2 * (1 - e) + j, back_in[which, j])

    def step_four(which):
        for k in range(HALF):
            pre_copy(which, k).wait_recv()

    early = 2 * p < pairs
    late = jnp.logical_not(early)
    step_one(0)
    loads[6].wait()
    fold_rows(qs, query_sum)

    @pl.when(early)
    def _():
        step_two(0)

    for step in range(1, nz):
        norm_copy(0, step).wait_recv()
    norm = own_norm + jnp.where(c == 1, norm_mate[0], 0.0)
    for step in range(1, nz):
        norm = norm + jnp.where(z >= step, norm_in[0, step], 0.0)
    norm_parts = jnp.concatenate(split(norm, 3), 0)
    two_parts = split(norm, 2)
    norm_t[...] = jnp.concatenate(two_parts + two_parts, 0).astype(f32).T.astype(bf16)

    loads[5].wait()
    part_lane = lax.broadcasted_iota(jnp.int32, (T, 3 * H), 1) & (H - 1)
    for h in range(H):
        inner = dot(phi_qt[h], norm_parts, 1, 1)
        whole = den[h] + jnp.sum(jnp.where(part_lane == h, inner, 0.0), axis=1, keepdims=True)
        den[h] = whole
        g_low[h] = (cot[0, :, lanes(h)].astype(f32) / whole).astype(bf16)
        contrib[1, h] = dot(phi_q[h], g_low[h]) * coef + query_sum[pl.ds(h, R, stride=H), :]
    for k in range(HALF):
        other_copy(1, k).start()
    step_one(1)
    for h in range(H):
        value_part[h] = dot(a_low[h], val[0, :, lanes(h)])
        phi_kt[h] = phi_k[h].astype(f32).T.astype(bf16)

    @pl.when(late)
    def _():
        def either(i, carry):
            step_two(i ^ (p == pairs - 1).astype(jnp.int32))
            return carry

        lax.fori_loop(0, 2, either, 0)
        step_three(1)

    step_three(0)
    step_four(0)

    def send_terms(part):
        left = dproj_t[PARTS[part][0] : PARTS[part][1], :].astype(bf16)
        for k in range(nz):
            chunk = pl.ds(pl.multiple_of((2 * k + 1 - c) * rows, rows), rows)
            term[part][1 - c, k] = dot(left, tok[0, :, chunk])
            if k % (nz // 2) == nz // 2 - 1:
                core_copy(part, k // (nz // 2)).start()
        for k in range(nz):
            chunk = pl.ds(pl.multiple_of((2 * k + c) * rows, rows), rows)
            term[part][c, k] = dot(left, tok[0, :, chunk])

    def send_x(part):
        for k in range(nz):
            if k % (nz // 2) == 0:
                core_copy(part, k // (nz // 2)).wait_recv()
            both = term[part][c, k] + core_in[part][k]
            piece = both.shape[0] // nx
            for j in range(nx):
                xs_out[part][j, k] = both[j * piece : (j + 1) * piece]
        for step in far_first(nx):
            xs_copy(part, step).start()

    def send_z(part):
        for step in range(1, nx):
            xs_copy(part, step).wait_recv()
        for k in range(nz):
            acc = xs_out[part][x, k]
            for step in range(1, nx):
                acc = acc + xs_in[part][step, k]
            xz_out[part][k] = acc
        for step in far_first(nz):
            xz_copy(part, step).start()

    def send_y(part):
        acc = xz_out[part][z]
        for step in range(1, nz):
            xz_copy(part, step).wait_recv()
            acc = acc + xz_in[part][step]
        y_part[part][y] = acc
        for step in far_first(ny):
            y_copy(part, step, y).start()

    def send_all(part):
        for step in range(1, ny):
            y_copy(part, step, lax.rem(y + ny - step, ny)).wait_recv()
        acc = y_part[part][0]
        for j in range(1, ny):
            acc = acc + y_part[part][j]
        x_part[part][x] = acc * (1.0 / (ny * nx))
        for step in far_first(nx):
            x_copy(part, step, x).start()

    def collect(part):
        for step in range(1, nx):
            x_copy(part, step, lax.rem(x + nx - step, nx)).wait_recv()
        start, stop = PARTS[part]
        wg_t[start:stop, :] = x_part[part][...].reshape(stop - start, rows)

    lane = lax.broadcasted_iota(jnp.int32, (T, DV), 1)
    gden_all = jnp.zeros((T, DV), f32)
    for h in range(H):
        p_low[h] = (pre[0, h] + span[h]).astype(bf16)
        numer = dot(phi_qt[h], p_low[h]) + value_part[h]
        weighted = jnp.sum(cot[0, :, lanes(h)].astype(f32) * numer, axis=1, keepdims=True)
        gden = -weighted / (den[h] * den[h])
        gden_all = jnp.where(lane == h, gden, gden_all)
        den[h] = jnp.broadcast_to(gden, (T, DV))
    gden_t[...] = gden_all.T[:H]
    gden_parts = jnp.concatenate(split(gden_t[...], 3), 0)
    total = jnp.zeros((H, R), f32)
    for h in range(H):
        every = dot(gden_parts, phi_q[h], 1, 1)
        every = every[:H] + every[H : 2 * H] + every[2 * H :]
        total = jnp.where(head_row == h, every, total)
    loads[7].wait()
    norm_own[1] = total * coef_row + fold_norm(qn[0, 0])
    mate_copy(1).start()
    mate_copy(1).wait_recv()
    norm_chip[1] = norm_own[1] + norm_mate[1]
    for step in far_first(nz):
        norm_copy(1, step).start()

    high, low = split(gden_t[...], 2)
    gden_rows = jnp.concatenate([high, high, low, low], 0)
    four_row = lax.broadcasted_iota(jnp.int32, (4 * H, T), 0) & (H - 1)
    for h in range(H):
        ga = jnp.where(causal, dot(g_low[h], val[0, :, lanes(h)], 1, 1) + den[h], 0.0)
        gs[h] = (ga * (1.0 + score[h]) * (1.0 / math.sqrt(FD))).astype(bf16)
        only = jnp.where(four_row == h, gden_rows, jnp.zeros_like(gden_rows))
        up = dot(p_low[h], g_low[h], 1, 1) + dot(norm_t[...], only)
        u = qt[feat(h), :]
        dproj_t[feat(h), :] = feature_grad(u, up) + dot(kt[feat(h), :].astype(bf16), gs[h], 1, 1)
    send_terms(0)

    @pl.when(early)
    def _():
        step_two(1)

    send_x(0)

    @pl.when(early)
    def _():
        step_three(1)

    step_four(1)
    for step in range(1, nz):
        norm_copy(1, step).wait_recv()
    norm = jnp.where(c == 0, norm_mate[1], 0.0)
    for step in range(1, nz):
        norm = norm + jnp.where(z < step, norm_in[1, step], 0.0)
    parts = split(norm, 3)
    norm_t[...] = jnp.concatenate(parts + [jnp.zeros_like(parts[0])], 0).astype(f32).T.astype(bf16)
    for h in range(H):
        only = jnp.where(four_row == h, 1.0, 0.0).astype(bf16)
        p_low[h] = pre[1, h].astype(bf16)
        up = dot(p_low[h], val[0, :, lanes(h)], 1, 1) + dot(norm_t[...], only)
        u = kt[feat(h), :]
        inner = dot(qt[feat(h), :].astype(bf16), gs[h])
        dproj_t[H * FD + h * FD : H * FD + (h + 1) * FD, :] = feature_grad(u, up) + inner
    send_terms(1)
    send_z(0)
    send_x(1)

    for h in range(H):
        vg[0, :, lanes(h)] = (dot(a_low[h], g_low[h], 0, 0) + dot(phi_kt[h], p_low[h])).astype(bf16)
    store_vg = pltpu.make_async_copy(vg, vg_h, out_sem.at[0])
    store_vg.start()
    dproj = dproj_t[...].T.astype(bf16)
    cols = min(512, d_model)
    for j in range(d_model // cols):
        tg[0, :, j * cols : (j + 1) * cols] = dot(dproj, w[j * cols : (j + 1) * cols, :], 1, 1).astype(bf16)
    store_tg = pltpu.make_async_copy(tg, tg_h, out_sem.at[1])
    store_tg.start()

    for which in range(2):
        mate_copy(which).wait_send()
        for step in range(1, nz):
            norm_copy(which, step).wait_send()
        last = (p == pairs - 1) if which == 0 else (p == 0)
        for k in range(HALF):
            other_copy(which, k).wait_send()
            pre_copy(which, k).wait_send()
        for j in range(2):
            pair_copy(which, j).wait_send()
            back_copy(which, j).wait_send()

            @pl.when(jnp.logical_not(last))
            def _():
                chain_copy(which, j).wait_send()

    def sent(part):
        for j in range(2):
            core_copy(part, j).wait_send()
        for step in range(1, nx):
            xs_copy(part, step).wait_send()
        for step in range(1, nz):
            xz_copy(part, step).wait_send()

    send_y(0)
    sent(0)
    send_z(1)
    send_all(0)
    send_y(1)
    collect(0)
    sent(1)
    store_vg.wait()
    store_tg.wait()
    send_all(1)
    for part in range(len(PARTS)):
        for step in range(1, ny):
            y_copy(part, step, y).wait_send()
    collect(1)
    wg[...] = wg_t[...].T
    store_wg = pltpu.make_async_copy(wg, wg_h, out_sem.at[2])
    store_wg.start()
    for part in range(len(PARTS)):
        for step in range(1, nx):
            x_copy(part, step, x).wait_send()
    store_wg.wait()


def hand_over(*refs):
    held, load_sem, store_sem = refs[6:9], refs[9], refs[10]
    loads = [pltpu.make_async_copy(refs[i], held[i], load_sem.at[i]) for i in range(3)]
    stores = [pltpu.make_async_copy(held[i], refs[3 + i], store_sem.at[i]) for i in range(3)]
    for load in loads:
        load.start()
    for load, store in zip(loads, stores):
        load.wait()
        store.start()
    for store in stores:
        store.wait()


def on_device(sizes, tokens, qk_weight, values, cotangent, key_span, key_norm, query_span, query_norm):
    ns, ny, nx, d_model = sizes
    nz = ns // 2
    rows = d_model // ns
    width = 2 * H * FD
    key_span, query_span = (jnp.swapaxes(a, 2, 3) for a in (key_span, query_span))
    args = (tokens, qk_weight, values, cotangent, key_span, key_norm, query_span, query_norm)
    out_shape = (
        jax.ShapeDtypeStruct((1, T, d_model), bf16),
        jax.ShapeDtypeStruct((1, T, H * DV), bf16),
        jax.ShapeDtypeStruct((rows, width), f32),
    )
    vmem, dma = pltpu.VMEM, pltpu.SemaphoreType.DMA

    def each(shape):
        return tuple(vmem(shape(stop - start), f32) for start, stop in PARTS)

    scratch = [vmem(a.shape, a.dtype) for a in args] + [vmem(o.shape, o.dtype) for o in out_shape]
    scratch += [
        vmem((H * FD, T), f32),
        vmem((H * FD, T), f32),
        vmem((H, R, T), bf16),
        vmem((H, R, T), bf16),
        vmem((H, T, R), bf16),
        vmem((H, T, R), bf16),
        vmem((R, F), bf16),
        vmem((H, T, T), f32),
        vmem((H, T, T), bf16),
        vmem((H, T, DV), f32),
        vmem((H, T, DV), f32),
        vmem((H, T, DV), bf16),
        vmem((H, T, T), bf16),
        vmem((H, R, DV), bf16),
        vmem((R, 4 * H), bf16),
        vmem((H, R, DV), f32),
        vmem((2, H, R, DV), f32),
        vmem((2, HALF, R, DV), f32),
        vmem((2, 2, R, DV), f32),
        vmem((2, 2, R, DV), f32),
        vmem((2, 2, R, DV), f32),
        vmem((2, 2, R, DV), f32),
        vmem((2, 2, R, DV), f32),
        vmem((2, 2, R, DV), f32),
        vmem((2, H, R, DV), f32),
        vmem((2, HALF, R, DV), f32),
        vmem((R * H, DV), f32),
        vmem((R * H, DV), f32),
        vmem((width, rows), f32),
        vmem((2, H, R), f32),
        vmem((2, H, R), f32),
        vmem((2, H, R), f32),
        vmem((2, nz, H, R), f32),
        vmem((H, T), f32),
        vmem((width, T), f32),
        each(lambda n: (2, nz, n, rows)),
        each(lambda n: (nz, n, rows)),
        each(lambda n: (nx, nz, n // nx, rows)),
        each(lambda n: (nx, nz, n // nx, rows)),
        each(lambda n: (nz, n // nx, rows)),
        each(lambda n: (nz, n // nx, rows)),
        each(lambda n: (ny, n // nx, rows)),
        each(lambda n: (nx, n // nx, rows)),
        dma((8,)), dma((3,)),
        dma((2,)), dma((2,)),
        dma((2, nz)), dma((2, nz)),
        dma((2, HALF)), dma((2, HALF)),
        dma((2, 2)), dma((2, 2)),
        dma((2, 2)), dma((2, 2)),
        dma((2, 2)), dma((2, 2)),
        dma((2, HALF)), dma((2, HALF)),
        dma((len(PARTS), 2)), dma((len(PARTS), 2)),
        dma((len(PARTS), nx)), dma((len(PARTS), nx)),
        dma((len(PARTS), nz)), dma((len(PARTS), nz)),
        dma((len(PARTS), ny)), dma((len(PARTS), ny)),
        dma((len(PARTS), nx)), dma((len(PARTS), nx)),
    ]
    results = pl.pallas_call(
        functools.partial(kernel, sizes),
        out_shape=out_shape,
        in_specs=[pl.BlockSpec(memory_space=pl.ANY)] * 8,
        out_specs=(pl.BlockSpec(memory_space=pl.ANY),) * 3,
        scratch_shapes=scratch,
        compiler_params=pltpu.CompilerParams(
            collective_id=0, has_side_effects=True, vmem_limit_bytes=60 * 1024 * 1024
        ),
    )(*args)
    return pl.pallas_call(
        hand_over,
        out_shape=out_shape,
        in_specs=[pl.BlockSpec(memory_space=pl.ANY)] * 3,
        out_specs=(pl.BlockSpec(memory_space=pl.ANY),) * 3,
        scratch_shapes=[vmem(o.shape, o.dtype) for o in out_shape] + [dma((3,)), dma((3,))],
    )(*results)


def solution(mesh):
    ns, docs = mesh.shape["seq"], mesh.shape["dp"]
    nx = 4 if docs >= 16 else 2

    def whole(*args):
        sizes = (ns, docs // nx, nx, args[0].shape[2])
        in_specs = (
            P("dp", "seq", None),
            P(),
            P("dp", "seq", None),
            P("dp", "seq", None),
            P("dp", "seq", None, None, None),
            P("dp", "seq", None, None),
            P("dp", "seq", None, None, None),
            P("dp", "seq", None, None),
        )
        out_specs = (P("dp", "seq", None), P("dp", "seq", None), P("seq", None))
        return jax.shard_map(
            functools.partial(on_device, sizes),
            mesh=mesh,
            in_specs=in_specs,
            out_specs=out_specs,
            check_vma=False,
        )(*args)

    return whole
```

```python
import functools
import math

import jax
import jax.numpy as jnp
from jax import lax
from jax.experimental import pallas as pl
from jax.experimental.pallas import tpu as pltpu
from jax.sharding import PartitionSpec as P

H = 8
FD = 16
DV = 128
F = 273
T = 128
R = 160
HALF = H // 2
PARTS = ((0, H * FD), (H * FD, 2 * H * FD))
PAIR = 1.0 / math.sqrt(2.0 * FD)
LINEAR = 1.0 / FD**0.25
f32 = jnp.float32
bf16 = jnp.bfloat16
MESH = pl.DeviceIdType.MESH


def dot(left, right, left_dim=1, right_dim=0):
    return lax.dot_general(
        left, right, (((left_dim,), (right_dim,)), ((), ())), preferred_element_type=f32
    )


def far_first(n):
    return sorted(range(1, n), key=lambda step: -min(step, n - step))


def split(x, parts):
    out = []
    for _ in range(parts):
        low = x.astype(bf16)
        out.append(low)
        x = x - low.astype(f32)
    return out


def fold_matrix():
    row = lax.broadcasted_iota(jnp.int32, (R, F), 0)
    col = lax.broadcasted_iota(jnp.int32, (R, F), 1)
    pair = col - 17
    a, b = (pair >> 4) & 15, pair & 15
    d = (b - a) & 15
    target = jnp.where(d <= 7, d * 16 + a, (16 - d) * 16 + b)
    target = jnp.where(d == 8, 144 + jnp.minimum(a, b), target)
    target = jnp.where(col <= 16, 127 + col, target)
    target = jnp.where(col == 0, 152, target)
    return jnp.where(row == target, 1.0, 0.0).astype(bf16)


def twice(shape, dim):
    row = lax.broadcasted_iota(jnp.int32, shape, dim)
    doubled = ((row >= 16) & (row < 128)) | ((row >= 144) & (row < 152))
    return jnp.where(doubled, 2.0, 1.0)


def features(u):
    rows = [u * (u if d == 0 else pltpu.roll(u, FD - d, 0)) * PAIR for d in range(8)]
    rows.append(u * LINEAR)
    rows.append(u[:8] * u[8:] * PAIR)
    rows.append(jnp.where(lax.broadcasted_iota(jnp.int32, (8, T), 0) == 0, 1.0, 0.0))
    return jnp.concatenate(rows, 0)


def feature_grad(u, y):
    acc = 2.0 * y[:16] * u
    for d in range(1, 8):
        part = y[16 * d : 16 * d + 16]
        acc = acc + part * pltpu.roll(u, FD - d, 0) + pltpu.roll(part * u, d, 0)
    last = y[144:152]
    acc = acc + jnp.concatenate([last * u[8:], last * u[:8]], 0)
    return y[128:144] * LINEAR + acc * PAIR


def kernel(
    sizes,
    tok_h, w_h, val_h, cot_h, ks_h, kn_h, qs_h, qn_h,
    tg_h, vg_h, wg_h,
    tok, w, val, cot, ks, kn, qs, qn,
    tg, vg, wg,
    qt, kt, phi_q, phi_k, phi_qt, phi_kt, fold,
    score, a_low, value_part, den, g_low, gs, p_low, norm_t,
    span, contrib, other, pair_out, pair_in, chain_in, chain_out, back_out, back_in, pre, pre_out,
    row_sum, query_sum, wg_t, norm_own, norm_mate, norm_chip, norm_in, gden_t, dproj_t,
    term, core_in, xs_out, xs_in, xz_out, xz_in, y_part, x_part,
    in_sem, out_sem,
    mate_send, mate_recv, norm_send, norm_recv, other_send, other_recv, pair_send, pair_recv,
    chain_send, chain_recv, back_send, back_recv, pre_send, pre_recv,
    core_send, core_recv, xs_send, xs_recv, xz_send, xz_recv,
    y_send, y_recv, x_send, x_recv,
):
    ns, ny, nx, d_model = sizes
    nz = ns // 2
    rows = d_model // ns
    pairs = nz // 2
    dp = lax.axis_index("dp")
    me = lax.axis_index("seq")
    z, c = me // 2, lax.rem(me, 2)
    y, x = dp // nx, lax.rem(dp, nx)
    p, e = z // 2, lax.rem(z, 2)
    mate = 2 * z + (1 - c)
    partner = 4 * p + 2 * (1 - e) + c

    def z_peer(step):
        return lax.rem(z + step, nz)

    def y_peer(step):
        return lax.rem(y + step, ny)

    def x_peer(step):
        return lax.rem(x + step, nx)

    loads = [
        pltpu.make_async_copy(src, dst, in_sem.at[i])
        for i, (src, dst) in enumerate(
            [(tok_h, tok), (w_h, w), (val_h, val), (ks_h, ks), (kn_h, kn), (cot_h, cot), (qs_h, qs), (qn_h, qn)]
        )
    ]
    for load in loads:
        load.start()

    def across_z(step):
        return (dp, 2 * z_peer(step) + c)

    def across_y(step):
        return (y_peer(step) * nx + x, me)

    def across_x(step):
        return (y * nx + x_peer(step), me)

    barrier = pltpu.get_barrier_semaphore()
    pl.semaphore_signal(barrier, inc=1, device_id=(dp, mate), device_id_type=MESH)
    for step in range(1, nz):
        pl.semaphore_signal(barrier, inc=1, device_id=across_z(step), device_id_type=MESH)
    for step in range(1, ny):
        pl.semaphore_signal(barrier, inc=1, device_id=across_y(step), device_id_type=MESH)
    for step in range(1, nx):
        pl.semaphore_signal(barrier, inc=1, device_id=across_x(step), device_id_type=MESH)

    def remote(src, dst, send, recv, device):
        return pltpu.make_async_remote_copy(
            src_ref=src, dst_ref=dst, send_sem=send, recv_sem=recv, device_id=device, device_id_type=MESH
        )

    def mate_copy(which):
        return remote(
            norm_own.at[which], norm_mate.at[which], mate_send.at[which], mate_recv.at[which], (dp, mate)
        )

    def norm_copy(which, step):
        return remote(
            norm_chip.at[which], norm_in.at[which, step],
            norm_send.at[which, step], norm_recv.at[which, step], across_z(step),
        )

    def other_copy(which, k):
        return remote(
            contrib.at[which, (1 - c) * HALF + k], other.at[which, k],
            other_send.at[which, k], other_recv.at[which, k], (dp, mate),
        )

    def pair_copy(which, j):
        return remote(
            pair_out.at[which, j], pair_in.at[which, j],
            pair_send.at[which, j], pair_recv.at[which, j], (dp, partner),
        )

    def chain_copy(which, j):
        target = jnp.clip(p + 1 - 2 * which, 0, pairs - 1)
        return remote(
            chain_out.at[which, j], chain_in.at[which, j],
            chain_send.at[which, j], chain_recv.at[which, j], (dp, 4 * target + 2 * e + c),
        )

    def back_copy(which, j):
        return remote(
            back_out.at[which, j], back_in.at[which, j],
            back_send.at[which, j], back_recv.at[which, j], (dp, partner),
        )

    def pre_copy(which, k):
        return remote(
            pre_out.at[which, k], pre.at[which, c * HALF + k],
            pre_send.at[which, k], pre_recv.at[which, k], (dp, mate),
        )

    def core_copy(part, j):
        run = pl.ds(j * (nz // 2), nz // 2)
        return remote(
            term[part].at[1 - c, run], core_in[part].at[run],
            core_send.at[part, j], core_recv.at[part, j], (dp, mate),
        )

    def xs_copy(part, step):
        return remote(
            xs_out[part].at[x_peer(step)], xs_in[part].at[step],
            xs_send.at[part, step], xs_recv.at[part, step], across_x(step),
        )

    def xz_copy(part, step):
        return remote(
            xz_out[part].at[z_peer(step)], xz_in[part].at[step],
            xz_send.at[part, step], xz_recv.at[part, step], across_z(step),
        )

    def y_copy(part, step, source):
        return remote(
            y_part[part].at[source], y_part[part].at[source],
            y_send.at[part, step], y_recv.at[part, step], across_y(step),
        )

    def x_copy(part, step, source):
        return remote(
            x_part[part].at[source], x_part[part].at[source],
            x_send.at[part, step], x_recv.at[part, step], across_x(step),
        )

    coef = twice((R, DV), 0)
    coef_row = twice((H, R), 1)
    head_row = lax.broadcasted_iota(jnp.int32, (H, R), 0)
    fold[...] = fold_matrix()

    def lanes(h):
        return slice(h * DV, (h + 1) * DV)

    def feat(h):
        return slice(h * FD, (h + 1) * FD)

    def fold_rows(source, row_sum):
        def lap(a, carry):
            for d in range(8):
                b = (a + d) & 15
                row = source[0, 0, 17 + 16 * a + b].astype(f32)
                if d:
                    row = row + source[0, 0, 17 + 16 * b + a].astype(f32)
                row_sum[pl.ds(pl.multiple_of((16 * d + a) * H, H), H), :] = row
            row_sum[pl.ds(pl.multiple_of((128 + a) * H, H), H), :] = source[0, 0, 1 + a].astype(f32)
            return carry

        def last_lap(a, carry):
            row = source[0, 0, 25 + 17 * a].astype(f32) + source[0, 0, 17 + 16 * (a + 8) + a].astype(f32)
            row_sum[pl.ds(pl.multiple_of((144 + a) * H, H), H), :] = row
            return carry

        lax.fori_loop(0, 16, lap, 0)
        lax.fori_loop(0, 8, last_lap, 0)
        row_sum[152 * H : 153 * H, :] = source[0, 0, 0].astype(f32)
        row_sum[153 * H :, :] = jnp.zeros(((R - 153) * H, DV), f32)

    def fold_norm(value):
        return sum(dot(part, fold[...], 1, 1) for part in split(value, 3))

    loads[0].wait()
    loads[1].wait()
    projected = dot(tok[0], w[...]).astype(bf16)
    qt[...] = projected[:, : H * FD].astype(f32).T
    kt[...] = projected[:, H * FD :].astype(f32).T
    total = jnp.zeros((H, R), f32)
    ones = jnp.ones((H, T), bf16)
    for h in range(H):
        phi = features(kt[feat(h), :])
        phi_k[h] = phi.astype(bf16)
        total = jnp.where(head_row == h, dot(ones, phi_k[h], 1, 1), total)
    loads[4].wait()
    own_norm = fold_norm(kn[0, 0])
    norm_own[0] = total * coef_row + own_norm
    pl.semaphore_wait(barrier, nz + ny + nx - 2)
    mate_copy(0).start()

    loads[2].wait()
    loads[3].wait()
    fold_rows(ks, row_sum)
    for h in range(H):
        span[h] = row_sum[pl.ds(h, R, stride=H), :]
        contrib[0, h] = dot(phi_k[h], val[0, :, lanes(h)]) * coef + span[h]
    for k in range(HALF):
        other_copy(0, k).start()
    mate_copy(0).wait_recv()
    norm_chip[0] = norm_own[0] + norm_mate[0]
    for step in far_first(nz):
        norm_copy(0, step).start()

    causal = lax.broadcasted_iota(jnp.int32, (T, T), 0) >= lax.broadcasted_iota(jnp.int32, (T, T), 1)
    head_lane = lax.broadcasted_iota(jnp.int32, (T, H * FD), 1) // FD
    query, key = projected[:, : H * FD], projected[:, H * FD :]
    for h in range(H):
        phi = features(qt[feat(h), :])
        phi_q[h] = phi.astype(bf16)
        phi_qt[h] = phi.T.astype(bf16)
        masked = jnp.where(head_lane == h, query, jnp.zeros_like(query))
        s = dot(masked, key, 1, 1) * (1.0 / math.sqrt(FD))
        score[h] = s
        a = jnp.where(causal, 1.0 + s + 0.5 * s * s, 0.0)
        a_low[h] = a.astype(bf16)
        den[h] = jnp.broadcast_to(jnp.sum(a, axis=1, keepdims=True), (T, DV))

    def step_one(which):
        for j in range(2):
            k = 2 * (1 - e) + j
            other_copy(which, k).wait_recv()
            pair_out[which, j] = contrib[which, c * HALF + k] + other[which, k]
            pair_copy(which, j).start()

    def finish(which, k, before):
        second = (c ^ which) == 1
        mine = c * HALF + k
        pre[which, mine] = before + jnp.where(second, other[which, k], 0.0)
        pre_out[which, k] = before + jnp.where(second, 0.0, contrib[which, mine])
        pre_copy(which, k).start()

    def step_two(which):
        first = jnp.where(which == 0, p == 0, p == pairs - 1)
        last = jnp.where(which == 0, p == pairs - 1, p == 0)
        for j in range(2):
            k = 2 * e + j
            other_copy(which, k).wait_recv()
            pair_copy(which, j).wait_recv()

            @pl.when(first)
            def _():
                chain_in[which, j] = jnp.zeros((R, DV), f32)

            @pl.when(jnp.logical_not(first))
            def _():
                chain_copy(which, j).wait_recv()

            before = chain_in[which, j]
            here = contrib[which, c * HALF + k] + other[which, k]
            there = pair_in[which, j]

            @pl.when(jnp.logical_not(last))
            def _():
                chain_out[which, j] = before + (here + there)
                chain_copy(which, j).start()

            second = (e ^ which) == 1
            back_out[which, j] = before + jnp.where(second, 0.0, here)
            back_copy(which, j).start()
            finish(which, k, before + jnp.where(second, there, 0.0))

    def step_three(which):
        for j in range(2):
            back_copy(which, j).wait_recv()
            finish(which, 2 * (1 - e) + j, back_in[which, j])

    def step_four(which):
        for k in range(HALF):
            pre_copy(which, k).wait_recv()

    early = 2 * p < pairs
    late = jnp.logical_not(early)
    step_one(0)
    loads[6].wait()
    fold_rows(qs, query_sum)

    @pl.when(early)
    def _():
        step_two(0)

    for step in range(1, nz):
        norm_copy(0, step).wait_recv()
    norm = own_norm + jnp.where(c == 1, norm_mate[0], 0.0)
    for step in range(1, nz):
        norm = norm + jnp.where(z >= step, norm_in[0, step], 0.0)
    norm_parts = jnp.concatenate(split(norm, 3), 0)
    two_parts = split(norm, 2)
    norm_t[...] = jnp.concatenate(two_parts + two_parts, 0).astype(f32).T.astype(bf16)

    loads[5].wait()
    part_lane = lax.broadcasted_iota(jnp.int32, (T, 3 * H), 1) & (H - 1)
    for h in range(H):
        inner = dot(phi_qt[h], norm_parts, 1, 1)
        whole = den[h] + jnp.sum(jnp.where(part_lane == h, inner, 0.0), axis=1, keepdims=True)
        den[h] = whole
        g_low[h] = (cot[0, :, lanes(h)].astype(f32) / whole).astype(bf16)
        contrib[1, h] = dot(phi_q[h], g_low[h]) * coef + query_sum[pl.ds(h, R, stride=H), :]
    for k in range(HALF):
        other_copy(1, k).start()
    step_one(1)
    for h in range(H):
        value_part[h] = dot(a_low[h], val[0, :, lanes(h)])
        phi_kt[h] = phi_k[h].astype(f32).T.astype(bf16)

    @pl.when(late)
    def _():
        def either(i, carry):
            step_two(i ^ (p == pairs - 1).astype(jnp.int32))
            return carry

        lax.fori_loop(0, 2, either, 0)
        step_three(1)

    step_three(0)
    step_four(0)

    def send_terms(part):
        left = dproj_t[PARTS[part][0] : PARTS[part][1], :].astype(bf16)
        for k in range(nz):
            chunk = pl.ds(pl.multiple_of((2 * k + 1 - c) * rows, rows), rows)
            term[part][1 - c, k] = dot(left, tok[0, :, chunk])
            if k % (nz // 2) == nz // 2 - 1:
                core_copy(part, k // (nz // 2)).start()
        for k in range(nz):
            chunk = pl.ds(pl.multiple_of((2 * k + c) * rows, rows), rows)
            term[part][c, k] = dot(left, tok[0, :, chunk])

    def send_x(part):
        for k in range(nz):
            if k % (nz // 2) == 0:
                core_copy(part, k // (nz // 2)).wait_recv()
            both = term[part][c, k] + core_in[part][k]
            piece = both.shape[0] // nx
            for j in range(nx):
                xs_out[part][j, k] = both[j * piece : (j + 1) * piece]
        for step in far_first(nx):
            xs_copy(part, step).start()

    def send_z(part):
        for step in range(1, nx):
            xs_copy(part, step).wait_recv()
        for k in range(nz):
            acc = xs_out[part][x, k]
            for step in range(1, nx):
                acc = acc + xs_in[part][step, k]
            xz_out[part][k] = acc
        for step in far_first(nz):
            xz_copy(part, step).start()

    def send_y(part):
        acc = xz_out[part][z]
        for step in range(1, nz):
            xz_copy(part, step).wait_recv()
            acc = acc + xz_in[part][step]
        y_part[part][y] = acc
        for step in far_first(ny):
            y_copy(part, step, y).start()

    def send_all(part):
        for step in range(1, ny):
            y_copy(part, step, lax.rem(y + ny - step, ny)).wait_recv()
        acc = y_part[part][0]
        for j in range(1, ny):
            acc = acc + y_part[part][j]
        x_part[part][x] = acc * (1.0 / (ny * nx))
        for step in far_first(nx):
            x_copy(part, step, x).start()

    def collect(part):
        for step in range(1, nx):
            x_copy(part, step, lax.rem(x + nx - step, nx)).wait_recv()
        start, stop = PARTS[part]
        wg_t[start:stop, :] = x_part[part][...].reshape(stop - start, rows)

    lane = lax.broadcasted_iota(jnp.int32, (T, DV), 1)
    gden_all = jnp.zeros((T, DV), f32)
    for h in range(H):
        p_low[h] = (pre[0, h] + span[h]).astype(bf16)
        numer = dot(phi_qt[h], p_low[h]) + value_part[h]
        weighted = jnp.sum(cot[0, :, lanes(h)].astype(f32) * numer, axis=1, keepdims=True)
        gden = -weighted / (den[h] * den[h])
        gden_all = jnp.where(lane == h, gden, gden_all)
        den[h] = jnp.broadcast_to(gden, (T, DV))
    gden_t[...] = gden_all.T[:H]
    gden_parts = jnp.concatenate(split(gden_t[...], 3), 0)
    total = jnp.zeros((H, R), f32)
    for h in range(H):
        every = dot(gden_parts, phi_q[h], 1, 1)
        every = every[:H] + every[H : 2 * H] + every[2 * H :]
        total = jnp.where(head_row == h, every, total)
    loads[7].wait()
    norm_own[1] = total * coef_row + fold_norm(qn[0, 0])
    mate_copy(1).start()
    mate_copy(1).wait_recv()
    norm_chip[1] = norm_own[1] + norm_mate[1]
    for step in far_first(nz):
        norm_copy(1, step).start()

    high, low = split(gden_t[...], 2)
    gden_rows = jnp.concatenate([high, high, low, low], 0)
    four_row = lax.broadcasted_iota(jnp.int32, (4 * H, T), 0) & (H - 1)
    for h in range(H):
        ga = jnp.where(causal, dot(g_low[h], val[0, :, lanes(h)], 1, 1) + den[h], 0.0)
        gs[h] = (ga * (1.0 + score[h]) * (1.0 / math.sqrt(FD))).astype(bf16)
        only = jnp.where(four_row == h, gden_rows, jnp.zeros_like(gden_rows))
        up = dot(p_low[h], g_low[h], 1, 1) + dot(norm_t[...], only)
        u = qt[feat(h), :]
        dproj_t[feat(h), :] = feature_grad(u, up) + dot(kt[feat(h), :].astype(bf16), gs[h], 1, 1)
    send_terms(0)

    @pl.when(early)
    def _():
        step_two(1)

    send_x(0)

    @pl.when(early)
    def _():
        step_three(1)

    step_four(1)
    for step in range(1, nz):
        norm_copy(1, step).wait_recv()
    norm = jnp.where(c == 0, norm_mate[1], 0.0)
    for step in range(1, nz):
        norm = norm + jnp.where(z < step, norm_in[1, step], 0.0)
    parts = split(norm, 3)
    norm_t[...] = jnp.concatenate(parts + [jnp.zeros_like(parts[0])], 0).astype(f32).T.astype(bf16)
    for h in range(H):
        only = jnp.where(four_row == h, 1.0, 0.0).astype(bf16)
        p_low[h] = pre[1, h].astype(bf16)
        up = dot(p_low[h], val[0, :, lanes(h)], 1, 1) + dot(norm_t[...], only)
        u = kt[feat(h), :]
        inner = dot(qt[feat(h), :].astype(bf16), gs[h])
        dproj_t[H * FD + h * FD : H * FD + (h + 1) * FD, :] = feature_grad(u, up) + inner
    send_terms(1)
    send_x(1)
    send_z(0)

    for h in range(H):
        vg[0, :, lanes(h)] = (dot(a_low[h], g_low[h], 0, 0) + dot(phi_kt[h], p_low[h])).astype(bf16)
    store_vg = pltpu.make_async_copy(vg, vg_h, out_sem.at[0])
    store_vg.start()
    dproj = dproj_t[...].T.astype(bf16)
    cols = min(512, d_model)
    for j in range(d_model // cols):
        tg[0, :, j * cols : (j + 1) * cols] = dot(dproj, w[j * cols : (j + 1) * cols, :], 1, 1).astype(bf16)
    store_tg = pltpu.make_async_copy(tg, tg_h, out_sem.at[1])
    store_tg.start()

    for which in range(2):
        mate_copy(which).wait_send()
        for step in range(1, nz):
            norm_copy(which, step).wait_send()
        last = (p == pairs - 1) if which == 0 else (p == 0)
        for k in range(HALF):
            other_copy(which, k).wait_send()
            pre_copy(which, k).wait_send()
        for j in range(2):
            pair_copy(which, j).wait_send()
            back_copy(which, j).wait_send()

            @pl.when(jnp.logical_not(last))
            def _():
                chain_copy(which, j).wait_send()

    def sent(part):
        for j in range(2):
            core_copy(part, j).wait_send()
        for step in range(1, nx):
            xs_copy(part, step).wait_send()
        for step in range(1, nz):
            xz_copy(part, step).wait_send()

    send_z(1)
    send_y(0)
    sent(0)
    send_y(1)
    send_all(0)
    sent(1)
    store_vg.wait()
    store_tg.wait()
    send_all(1)
    collect(0)
    for part in range(len(PARTS)):
        for step in range(1, ny):
            y_copy(part, step, y).wait_send()
    collect(1)
    wg[...] = wg_t[...].T
    store_wg = pltpu.make_async_copy(wg, wg_h, out_sem.at[2])
    store_wg.start()
    for part in range(len(PARTS)):
        for step in range(1, nx):
            x_copy(part, step, x).wait_send()
    store_wg.wait()


def hand_over(*refs):
    held, load_sem, store_sem = refs[6:9], refs[9], refs[10]
    loads = [pltpu.make_async_copy(refs[i], held[i], load_sem.at[i]) for i in range(3)]
    stores = [pltpu.make_async_copy(held[i], refs[3 + i], store_sem.at[i]) for i in range(3)]
    for load in loads:
        load.start()
    for load, store in zip(loads, stores):
        load.wait()
        store.start()
    for store in stores:
        store.wait()


def on_device(sizes, tokens, qk_weight, values, cotangent, key_span, key_norm, query_span, query_norm):
    ns, ny, nx, d_model = sizes
    nz = ns // 2
    rows = d_model // ns
    width = 2 * H * FD
    key_span, query_span = (jnp.swapaxes(a, 2, 3) for a in (key_span, query_span))
    args = (tokens, qk_weight, values, cotangent, key_span, key_norm, query_span, query_norm)
    out_shape = (
        jax.ShapeDtypeStruct((1, T, d_model), bf16),
        jax.ShapeDtypeStruct((1, T, H * DV), bf16),
        jax.ShapeDtypeStruct((rows, width), f32),
    )
    vmem, dma = pltpu.VMEM, pltpu.SemaphoreType.DMA

    def each(shape):
        return tuple(vmem(shape(stop - start), f32) for start, stop in PARTS)

    scratch = [vmem(a.shape, a.dtype) for a in args] + [vmem(o.shape, o.dtype) for o in out_shape]
    scratch += [
        vmem((H * FD, T), f32),
        vmem((H * FD, T), f32),
        vmem((H, R, T), bf16),
        vmem((H, R, T), bf16),
        vmem((H, T, R), bf16),
        vmem((H, T, R), bf16),
        vmem((R, F), bf16),
        vmem((H, T, T), f32),
        vmem((H, T, T), bf16),
        vmem((H, T, DV), f32),
        vmem((H, T, DV), f32),
        vmem((H, T, DV), bf16),
        vmem((H, T, T), bf16),
        vmem((H, R, DV), bf16),
        vmem((R, 4 * H), bf16),
        vmem((H, R, DV), f32),
        vmem((2, H, R, DV), f32),
        vmem((2, HALF, R, DV), f32),
        vmem((2, 2, R, DV), f32),
        vmem((2, 2, R, DV), f32),
        vmem((2, 2, R, DV), f32),
        vmem((2, 2, R, DV), f32),
        vmem((2, 2, R, DV), f32),
        vmem((2, 2, R, DV), f32),
        vmem((2, H, R, DV), f32),
        vmem((2, HALF, R, DV), f32),
        vmem((R * H, DV), f32),
        vmem((R * H, DV), f32),
        vmem((width, rows), f32),
        vmem((2, H, R), f32),
        vmem((2, H, R), f32),
        vmem((2, H, R), f32),
        vmem((2, nz, H, R), f32),
        vmem((H, T), f32),
        vmem((width, T), f32),
        each(lambda n: (2, nz, n, rows)),
        each(lambda n: (nz, n, rows)),
        each(lambda n: (nx, nz, n // nx, rows)),
        each(lambda n: (nx, nz, n // nx, rows)),
        each(lambda n: (nz, n // nx, rows)),
        each(lambda n: (nz, n // nx, rows)),
        each(lambda n: (ny, n // nx, rows)),
        each(lambda n: (nx, n // nx, rows)),
        dma((8,)), dma((3,)),
        dma((2,)), dma((2,)),
        dma((2, nz)), dma((2, nz)),
        dma((2, HALF)), dma((2, HALF)),
        dma((2, 2)), dma((2, 2)),
        dma((2, 2)), dma((2, 2)),
        dma((2, 2)), dma((2, 2)),
        dma((2, HALF)), dma((2, HALF)),
        dma((len(PARTS), 2)), dma((len(PARTS), 2)),
        dma((len(PARTS), nx)), dma((len(PARTS), nx)),
        dma((len(PARTS), nz)), dma((len(PARTS), nz)),
        dma((len(PARTS), ny)), dma((len(PARTS), ny)),
        dma((len(PARTS), nx)), dma((len(PARTS), nx)),
    ]
    results = pl.pallas_call(
        functools.partial(kernel, sizes),
        out_shape=out_shape,
        in_specs=[pl.BlockSpec(memory_space=pl.ANY)] * 8,
        out_specs=(pl.BlockSpec(memory_space=pl.ANY),) * 3,
        scratch_shapes=scratch,
        compiler_params=pltpu.CompilerParams(
            collective_id=0, has_side_effects=True, vmem_limit_bytes=60 * 1024 * 1024
        ),
    )(*args)
    return pl.pallas_call(
        hand_over,
        out_shape=out_shape,
        in_specs=[pl.BlockSpec(memory_space=pl.ANY)] * 3,
        out_specs=(pl.BlockSpec(memory_space=pl.ANY),) * 3,
        scratch_shapes=[vmem(o.shape, o.dtype) for o in out_shape] + [dma((3,)), dma((3,))],
    )(*results)


def solution(mesh):
    ns, docs = mesh.shape["seq"], mesh.shape["dp"]
    nx = 4 if docs >= 16 else 2

    def whole(*args):
        sizes = (ns, docs // nx, nx, args[0].shape[2])
        in_specs = (
            P("dp", "seq", None),
            P(),
            P("dp", "seq", None),
            P("dp", "seq", None),
            P("dp", "seq", None, None, None),
            P("dp", "seq", None, None),
            P("dp", "seq", None, None, None),
            P("dp", "seq", None, None),
        )
        out_specs = (P("dp", "seq", None), P("dp", "seq", None), P("seq", None))
        return jax.shard_map(
            functools.partial(on_device, sizes),
            mesh=mesh,
            in_specs=in_specs,
            out_specs=out_specs,
            check_vma=False,
        )(*args)

    return whole
```

```python
import functools
import math

import jax
import jax.numpy as jnp
from jax import lax
from jax.experimental import pallas as pl
from jax.experimental.pallas import tpu as pltpu
from jax.sharding import PartitionSpec as P

H = 8
FD = 16
DV = 128
F = 273
T = 128
R = 160
HALF = H // 2
PARTS = ((0, H * FD), (H * FD, 2 * H * FD))
PAIR = 1.0 / math.sqrt(2.0 * FD)
LINEAR = 1.0 / FD**0.25
f32 = jnp.float32
bf16 = jnp.bfloat16
MESH = pl.DeviceIdType.MESH


def dot(left, right, left_dim=1, right_dim=0):
    return lax.dot_general(
        left, right, (((left_dim,), (right_dim,)), ((), ())), preferred_element_type=f32
    )


def far_first(n):
    return sorted(range(1, n), key=lambda step: -min(step, n - step))


def split(x, parts):
    out = []
    for _ in range(parts):
        low = x.astype(bf16)
        out.append(low)
        x = x - low.astype(f32)
    return out


def fold_matrix():
    row = lax.broadcasted_iota(jnp.int32, (R, F), 0)
    col = lax.broadcasted_iota(jnp.int32, (R, F), 1)
    pair = col - 17
    a, b = (pair >> 4) & 15, pair & 15
    d = (b - a) & 15
    target = jnp.where(d <= 7, d * 16 + a, (16 - d) * 16 + b)
    target = jnp.where(d == 8, 144 + jnp.minimum(a, b), target)
    target = jnp.where(col <= 16, 127 + col, target)
    target = jnp.where(col == 0, 152, target)
    return jnp.where(row == target, 1.0, 0.0).astype(bf16)


def twice(shape, dim):
    row = lax.broadcasted_iota(jnp.int32, shape, dim)
    doubled = ((row >= 16) & (row < 128)) | ((row >= 144) & (row < 152))
    return jnp.where(doubled, 2.0, 1.0)


def features(u):
    rows = [u * (u if d == 0 else pltpu.roll(u, FD - d, 0)) * PAIR for d in range(8)]
    rows.append(u * LINEAR)
    rows.append(u[:8] * u[8:] * PAIR)
    rows.append(jnp.where(lax.broadcasted_iota(jnp.int32, (8, T), 0) == 0, 1.0, 0.0))
    return jnp.concatenate(rows, 0)


def feature_grad(u, y):
    acc = 2.0 * y[:16] * u
    for d in range(1, 8):
        part = y[16 * d : 16 * d + 16]
        acc = acc + part * pltpu.roll(u, FD - d, 0) + pltpu.roll(part * u, d, 0)
    last = y[144:152]
    acc = acc + jnp.concatenate([last * u[8:], last * u[:8]], 0)
    return y[128:144] * LINEAR + acc * PAIR


def kernel(
    sizes,
    tok_h, w_h, val_h, cot_h, ks_h, kn_h, qs_h, qn_h,
    tg_h, vg_h, wg_h,
    tok, w, val, cot, ks, kn, qs, qn,
    tg, vg, wg,
    qt, kt, phi_q, phi_k, phi_qt, phi_kt, fold,
    score, a_low, value_part, den, g_low, gs, p_low, norm_t,
    span, contrib, other, pair_out, pair_in, chain_in, chain_out, back_out, back_in, pre, pre_out,
    row_sum, query_sum, wg_t, norm_own, norm_mate, norm_chip, norm_in, gden_t, dproj_t,
    term, core_in, xs_out, xs_in, xz_out, xz_in, y_part, x_part,
    in_sem, out_sem,
    mate_send, mate_recv, norm_send, norm_recv, other_send, other_recv, pair_send, pair_recv,
    chain_send, chain_recv, back_send, back_recv, pre_send, pre_recv,
    core_send, core_recv, xs_send, xs_recv, xz_send, xz_recv,
    y_send, y_recv, x_send, x_recv,
):
    ns, ny, nx, d_model = sizes
    nz = ns // 2
    rows = d_model // ns
    pairs = nz // 2
    dp = lax.axis_index("dp")
    me = lax.axis_index("seq")
    z, c = me // 2, lax.rem(me, 2)
    y, x = dp // nx, lax.rem(dp, nx)
    p, e = z // 2, lax.rem(z, 2)
    mate = 2 * z + (1 - c)
    partner = 4 * p + 2 * (1 - e) + c

    def z_peer(step):
        return lax.rem(z + step, nz)

    def y_peer(step):
        return lax.rem(y + step, ny)

    def x_peer(step):
        return lax.rem(x + step, nx)

    loads = [
        pltpu.make_async_copy(src, dst, in_sem.at[i])
        for i, (src, dst) in enumerate(
            [(tok_h, tok), (w_h, w), (val_h, val), (ks_h, ks), (kn_h, kn), (cot_h, cot), (qs_h, qs), (qn_h, qn)]
        )
    ]
    for load in loads:
        load.start()

    def across_z(step):
        return (dp, 2 * z_peer(step) + c)

    def across_y(step):
        return (y_peer(step) * nx + x, me)

    def across_x(step):
        return (y * nx + x_peer(step), me)

    barrier = pltpu.get_barrier_semaphore()
    pl.semaphore_signal(barrier, inc=1, device_id=(dp, mate), device_id_type=MESH)
    for step in range(1, nz):
        pl.semaphore_signal(barrier, inc=1, device_id=across_z(step), device_id_type=MESH)
    for step in range(1, ny):
        pl.semaphore_signal(barrier, inc=1, device_id=across_y(step), device_id_type=MESH)
    for step in range(1, nx):
        pl.semaphore_signal(barrier, inc=1, device_id=across_x(step), device_id_type=MESH)

    def remote(src, dst, send, recv, device):
        return pltpu.make_async_remote_copy(
            src_ref=src, dst_ref=dst, send_sem=send, recv_sem=recv, device_id=device, device_id_type=MESH
        )

    def mate_copy(which):
        return remote(
            norm_own.at[which], norm_mate.at[which], mate_send.at[which], mate_recv.at[which], (dp, mate)
        )

    def norm_copy(which, step):
        return remote(
            norm_chip.at[which], norm_in.at[which, step],
            norm_send.at[which, step], norm_recv.at[which, step], across_z(step),
        )

    def other_copy(which, k):
        return remote(
            contrib.at[which, (1 - c) * HALF + k], other.at[which, k],
            other_send.at[which, k], other_recv.at[which, k], (dp, mate),
        )

    def pair_copy(which, j):
        return remote(
            pair_out.at[which, j], pair_in.at[which, j],
            pair_send.at[which, j], pair_recv.at[which, j], (dp, partner),
        )

    def chain_copy(which, j):
        target = jnp.clip(p + 1 - 2 * which, 0, pairs - 1)
        return remote(
            chain_out.at[which, j], chain_in.at[which, j],
            chain_send.at[which, j], chain_recv.at[which, j], (dp, 4 * target + 2 * e + c),
        )

    def back_copy(which, j):
        return remote(
            back_out.at[which, j], back_in.at[which, j],
            back_send.at[which, j], back_recv.at[which, j], (dp, partner),
        )

    def pre_copy(which, k):
        return remote(
            pre_out.at[which, k], pre.at[which, c * HALF + k],
            pre_send.at[which, k], pre_recv.at[which, k], (dp, mate),
        )

    def core_copy(part, j):
        run = pl.ds(j * (nz // 2), nz // 2)
        return remote(
            term[part].at[1 - c, run], core_in[part].at[run],
            core_send.at[part, j], core_recv.at[part, j], (dp, mate),
        )

    def xs_copy(part, step, group):
        run = pl.ds(group * (nz // 2), nz // 2)
        return remote(
            xs_out[part].at[x_peer(step), run], xs_in[part].at[step, run],
            xs_send.at[part, group, step], xs_recv.at[part, group, step], across_x(step),
        )

    def xz_copy(part, step):
        return remote(
            xz_out[part].at[z_peer(step)], xz_in[part].at[step],
            xz_send.at[part, step], xz_recv.at[part, step], across_z(step),
        )

    def y_copy(part, step, source):
        return remote(
            y_part[part].at[source], y_part[part].at[source],
            y_send.at[part, step], y_recv.at[part, step], across_y(step),
        )

    def x_copy(part, step, source):
        return remote(
            x_part[part].at[source], x_part[part].at[source],
            x_send.at[part, step], x_recv.at[part, step], across_x(step),
        )

    coef = twice((R, DV), 0)
    coef_row = twice((H, R), 1)
    head_row = lax.broadcasted_iota(jnp.int32, (H, R), 0)
    fold[...] = fold_matrix()

    def lanes(h):
        return slice(h * DV, (h + 1) * DV)

    def feat(h):
        return slice(h * FD, (h + 1) * FD)

    def fold_rows(source, row_sum):
        def lap(a, carry):
            for d in range(8):
                b = (a + d) & 15
                row = source[0, 0, 17 + 16 * a + b].astype(f32)
                if d:
                    row = row + source[0, 0, 17 + 16 * b + a].astype(f32)
                row_sum[pl.ds(pl.multiple_of((16 * d + a) * H, H), H), :] = row
            row_sum[pl.ds(pl.multiple_of((128 + a) * H, H), H), :] = source[0, 0, 1 + a].astype(f32)
            return carry

        def last_lap(a, carry):
            row = source[0, 0, 25 + 17 * a].astype(f32) + source[0, 0, 17 + 16 * (a + 8) + a].astype(f32)
            row_sum[pl.ds(pl.multiple_of((144 + a) * H, H), H), :] = row
            return carry

        lax.fori_loop(0, 16, lap, 0)
        lax.fori_loop(0, 8, last_lap, 0)
        row_sum[152 * H : 153 * H, :] = source[0, 0, 0].astype(f32)
        row_sum[153 * H :, :] = jnp.zeros(((R - 153) * H, DV), f32)

    def fold_norm(value):
        return sum(dot(part, fold[...], 1, 1) for part in split(value, 3))

    loads[0].wait()
    loads[1].wait()
    projected = dot(tok[0], w[...]).astype(bf16)
    qt[...] = projected[:, : H * FD].astype(f32).T
    kt[...] = projected[:, H * FD :].astype(f32).T
    total = jnp.zeros((H, R), f32)
    ones = jnp.ones((H, T), bf16)
    for h in range(H):
        phi = features(kt[feat(h), :])
        phi_k[h] = phi.astype(bf16)
        total = jnp.where(head_row == h, dot(ones, phi_k[h], 1, 1), total)
    loads[4].wait()
    own_norm = fold_norm(kn[0, 0])
    norm_own[0] = total * coef_row + own_norm
    pl.semaphore_wait(barrier, nz + ny + nx - 2)
    mate_copy(0).start()

    loads[2].wait()
    loads[3].wait()
    fold_rows(ks, row_sum)
    for h in range(H):
        span[h] = row_sum[pl.ds(h, R, stride=H), :]
        contrib[0, h] = dot(phi_k[h], val[0, :, lanes(h)]) * coef + span[h]
    for k in range(HALF):
        other_copy(0, k).start()
    mate_copy(0).wait_recv()
    norm_chip[0] = norm_own[0] + norm_mate[0]
    for step in far_first(nz):
        norm_copy(0, step).start()

    causal = lax.broadcasted_iota(jnp.int32, (T, T), 0) >= lax.broadcasted_iota(jnp.int32, (T, T), 1)
    head_lane = lax.broadcasted_iota(jnp.int32, (T, H * FD), 1) // FD
    query, key = projected[:, : H * FD], projected[:, H * FD :]
    for h in range(H):
        phi = features(qt[feat(h), :])
        phi_q[h] = phi.astype(bf16)
        phi_qt[h] = phi.T.astype(bf16)
        masked = jnp.where(head_lane == h, query, jnp.zeros_like(query))
        s = dot(masked, key, 1, 1) * (1.0 / math.sqrt(FD))
        score[h] = s
        a = jnp.where(causal, 1.0 + s + 0.5 * s * s, 0.0)
        a_low[h] = a.astype(bf16)
        den[h] = jnp.broadcast_to(jnp.sum(a, axis=1, keepdims=True), (T, DV))

    def step_one(which):
        for j in range(2):
            k = 2 * (1 - e) + j
            other_copy(which, k).wait_recv()
            pair_out[which, j] = contrib[which, c * HALF + k] + other[which, k]
            pair_copy(which, j).start()

    def finish(which, k, before):
        second = (c ^ which) == 1
        mine = c * HALF + k
        pre[which, mine] = before + jnp.where(second, other[which, k], 0.0)
        pre_out[which, k] = before + jnp.where(second, 0.0, contrib[which, mine])
        pre_copy(which, k).start()

    def step_two(which):
        first = jnp.where(which == 0, p == 0, p == pairs - 1)
        last = jnp.where(which == 0, p == pairs - 1, p == 0)
        for j in range(2):
            k = 2 * e + j
            other_copy(which, k).wait_recv()
            pair_copy(which, j).wait_recv()

            @pl.when(first)
            def _():
                chain_in[which, j] = jnp.zeros((R, DV), f32)

            @pl.when(jnp.logical_not(first))
            def _():
                chain_copy(which, j).wait_recv()

            before = chain_in[which, j]
            here = contrib[which, c * HALF + k] + other[which, k]
            there = pair_in[which, j]

            @pl.when(jnp.logical_not(last))
            def _():
                chain_out[which, j] = before + (here + there)
                chain_copy(which, j).start()

            second = (e ^ which) == 1
            back_out[which, j] = before + jnp.where(second, 0.0, here)
            back_copy(which, j).start()
            finish(which, k, before + jnp.where(second, there, 0.0))

    def step_three(which):
        for j in range(2):
            back_copy(which, j).wait_recv()
            finish(which, 2 * (1 - e) + j, back_in[which, j])

    def step_four(which):
        for k in range(HALF):
            pre_copy(which, k).wait_recv()

    early = 2 * p < pairs
    late = jnp.logical_not(early)
    step_one(0)
    loads[6].wait()
    fold_rows(qs, query_sum)

    @pl.when(early)
    def _():
        step_two(0)

    for step in range(1, nz):
        norm_copy(0, step).wait_recv()
    norm = own_norm + jnp.where(c == 1, norm_mate[0], 0.0)
    for step in range(1, nz):
        norm = norm + jnp.where(z >= step, norm_in[0, step], 0.0)
    norm_parts = jnp.concatenate(split(norm, 3), 0)
    two_parts = split(norm, 2)
    norm_t[...] = jnp.concatenate(two_parts + two_parts, 0).astype(f32).T.astype(bf16)

    loads[5].wait()
    part_lane = lax.broadcasted_iota(jnp.int32, (T, 3 * H), 1) & (H - 1)
    for h in range(H):
        inner = dot(phi_qt[h], norm_parts, 1, 1)
        whole = den[h] + jnp.sum(jnp.where(part_lane == h, inner, 0.0), axis=1, keepdims=True)
        den[h] = whole
        g_low[h] = (cot[0, :, lanes(h)].astype(f32) / whole).astype(bf16)
        contrib[1, h] = dot(phi_q[h], g_low[h]) * coef + query_sum[pl.ds(h, R, stride=H), :]
    for k in range(HALF):
        other_copy(1, k).start()
    step_one(1)
    for h in range(H):
        value_part[h] = dot(a_low[h], val[0, :, lanes(h)])
        phi_kt[h] = phi_k[h].astype(f32).T.astype(bf16)

    @pl.when(late)
    def _():
        def either(i, carry):
            step_two(i ^ (p == pairs - 1).astype(jnp.int32))
            return carry

        lax.fori_loop(0, 2, either, 0)
        step_three(1)

    step_three(0)
    step_four(0)

    def send_terms(part):
        left = dproj_t[PARTS[part][0] : PARTS[part][1], :].astype(bf16)
        for k in range(nz):
            chunk = pl.ds(pl.multiple_of((2 * k + 1 - c) * rows, rows), rows)
            term[part][1 - c, k] = dot(left, tok[0, :, chunk])
            if k % (nz // 2) == nz // 2 - 1:
                core_copy(part, k // (nz // 2)).start()
        for k in range(nz):
            chunk = pl.ds(pl.multiple_of((2 * k + c) * rows, rows), rows)
            term[part][c, k] = dot(left, tok[0, :, chunk])

    def send_x(part):
        for group in range(2):
            core_copy(part, group).wait_recv()
            for k in range(group * (nz // 2), (group + 1) * (nz // 2)):
                both = term[part][c, k] + core_in[part][k]
                piece = both.shape[0] // nx
                for j in range(nx):
                    xs_out[part][j, k] = both[j * piece : (j + 1) * piece]
            for step in far_first(nx):
                xs_copy(part, step, group).start()

    def send_z(part):
        for group in range(2):
            for step in range(1, nx):
                xs_copy(part, step, group).wait_recv()
            for k in range(group * (nz // 2), (group + 1) * (nz // 2)):
                acc = xs_out[part][x, k]
                for step in range(1, nx):
                    acc = acc + xs_in[part][step, k]
                xz_out[part][k] = acc

                @pl.when(k != z)
                def _():
                    xz_copy(part, lax.rem(k + nz - z, nz)).start()

    def send_y(part):
        acc = xz_out[part][z]
        for step in range(1, nz):
            xz_copy(part, step).wait_recv()
            acc = acc + xz_in[part][step]
        y_part[part][y] = acc
        for step in far_first(ny):
            y_copy(part, step, y).start()

    def send_all(part):
        for step in range(1, ny):
            y_copy(part, step, lax.rem(y + ny - step, ny)).wait_recv()
        acc = y_part[part][0]
        for j in range(1, ny):
            acc = acc + y_part[part][j]
        x_part[part][x] = acc * (1.0 / (ny * nx))
        for step in far_first(nx):
            x_copy(part, step, x).start()

    def collect(part):
        for step in range(1, nx):
            x_copy(part, step, lax.rem(x + nx - step, nx)).wait_recv()
        start, stop = PARTS[part]
        wg_t[start:stop, :] = x_part[part][...].reshape(stop - start, rows)

    lane = lax.broadcasted_iota(jnp.int32, (T, DV), 1)
    gden_all = jnp.zeros((T, DV), f32)
    for h in range(H):
        p_low[h] = (pre[0, h] + span[h]).astype(bf16)
        numer = dot(phi_qt[h], p_low[h]) + value_part[h]
        weighted = jnp.sum(cot[0, :, lanes(h)].astype(f32) * numer, axis=1, keepdims=True)
        gden = -weighted / (den[h] * den[h])
        gden_all = jnp.where(lane == h, gden, gden_all)
        den[h] = jnp.broadcast_to(gden, (T, DV))
    gden_t[...] = gden_all.T[:H]
    gden_parts = jnp.concatenate(split(gden_t[...], 3), 0)
    total = jnp.zeros((H, R), f32)
    for h in range(H):
        every = dot(gden_parts, phi_q[h], 1, 1)
        every = every[:H] + every[H : 2 * H] + every[2 * H :]
        total = jnp.where(head_row == h, every, total)
    loads[7].wait()
    norm_own[1] = total * coef_row + fold_norm(qn[0, 0])
    mate_copy(1).start()
    mate_copy(1).wait_recv()
    norm_chip[1] = norm_own[1] + norm_mate[1]
    for step in far_first(nz):
        norm_copy(1, step).start()

    high, low = split(gden_t[...], 2)
    gden_rows = jnp.concatenate([high, high, low, low], 0)
    four_row = lax.broadcasted_iota(jnp.int32, (4 * H, T), 0) & (H - 1)
    for h in range(H):
        ga = jnp.where(causal, dot(g_low[h], val[0, :, lanes(h)], 1, 1) + den[h], 0.0)
        gs[h] = (ga * (1.0 + score[h]) * (1.0 / math.sqrt(FD))).astype(bf16)
        only = jnp.where(four_row == h, gden_rows, jnp.zeros_like(gden_rows))
        up = dot(p_low[h], g_low[h], 1, 1) + dot(norm_t[...], only)
        u = qt[feat(h), :]
        dproj_t[feat(h), :] = feature_grad(u, up) + dot(kt[feat(h), :].astype(bf16), gs[h], 1, 1)
    send_terms(0)

    @pl.when(early)
    def _():
        step_two(1)

    send_x(0)

    @pl.when(early)
    def _():
        step_three(1)

    step_four(1)
    for step in range(1, nz):
        norm_copy(1, step).wait_recv()
    norm = jnp.where(c == 0, norm_mate[1], 0.0)
    for step in range(1, nz):
        norm = norm + jnp.where(z < step, norm_in[1, step], 0.0)
    parts = split(norm, 3)
    norm_t[...] = jnp.concatenate(parts + [jnp.zeros_like(parts[0])], 0).astype(f32).T.astype(bf16)
    for h in range(H):
        only = jnp.where(four_row == h, 1.0, 0.0).astype(bf16)
        p_low[h] = pre[1, h].astype(bf16)
        up = dot(p_low[h], val[0, :, lanes(h)], 1, 1) + dot(norm_t[...], only)
        u = kt[feat(h), :]
        inner = dot(qt[feat(h), :].astype(bf16), gs[h])
        dproj_t[H * FD + h * FD : H * FD + (h + 1) * FD, :] = feature_grad(u, up) + inner
    send_terms(1)
    send_x(1)
    send_z(0)

    for h in range(H):
        vg[0, :, lanes(h)] = (dot(a_low[h], g_low[h], 0, 0) + dot(phi_kt[h], p_low[h])).astype(bf16)
    store_vg = pltpu.make_async_copy(vg, vg_h, out_sem.at[0])
    store_vg.start()
    dproj = dproj_t[...].T.astype(bf16)
    cols = min(512, d_model)
    for j in range(d_model // cols):
        tg[0, :, j * cols : (j + 1) * cols] = dot(dproj, w[j * cols : (j + 1) * cols, :], 1, 1).astype(bf16)
    store_tg = pltpu.make_async_copy(tg, tg_h, out_sem.at[1])
    store_tg.start()

    for which in range(2):
        mate_copy(which).wait_send()
        for step in range(1, nz):
            norm_copy(which, step).wait_send()
        last = (p == pairs - 1) if which == 0 else (p == 0)
        for k in range(HALF):
            other_copy(which, k).wait_send()
            pre_copy(which, k).wait_send()
        for j in range(2):
            pair_copy(which, j).wait_send()
            back_copy(which, j).wait_send()

            @pl.when(jnp.logical_not(last))
            def _():
                chain_copy(which, j).wait_send()

    def sent(part):
        for j in range(2):
            core_copy(part, j).wait_send()
        for step in range(1, nx):
            for group in range(2):
                xs_copy(part, step, group).wait_send()
        for step in range(1, nz):
            xz_copy(part, step).wait_send()

    send_z(1)
    send_y(0)
    sent(0)
    send_y(1)
    send_all(0)
    sent(1)
    store_vg.wait()
    store_tg.wait()
    send_all(1)
    collect(0)
    for part in range(len(PARTS)):
        for step in range(1, ny):
            y_copy(part, step, y).wait_send()
    collect(1)
    wg[...] = wg_t[...].T
    store_wg = pltpu.make_async_copy(wg, wg_h, out_sem.at[2])
    store_wg.start()
    for part in range(len(PARTS)):
        for step in range(1, nx):
            x_copy(part, step, x).wait_send()
    store_wg.wait()


def hand_over(*refs):
    held, load_sem, store_sem = refs[6:9], refs[9], refs[10]
    loads = [pltpu.make_async_copy(refs[i], held[i], load_sem.at[i]) for i in range(3)]
    stores = [pltpu.make_async_copy(held[i], refs[3 + i], store_sem.at[i]) for i in range(3)]
    for load in loads:
        load.start()
    for load, store in zip(loads, stores):
        load.wait()
        store.start()
    for store in stores:
        store.wait()


def on_device(sizes, tokens, qk_weight, values, cotangent, key_span, key_norm, query_span, query_norm):
    ns, ny, nx, d_model = sizes
    nz = ns // 2
    rows = d_model // ns
    width = 2 * H * FD
    key_span, query_span = (jnp.swapaxes(a, 2, 3) for a in (key_span, query_span))
    args = (tokens, qk_weight, values, cotangent, key_span, key_norm, query_span, query_norm)
    out_shape = (
        jax.ShapeDtypeStruct((1, T, d_model), bf16),
        jax.ShapeDtypeStruct((1, T, H * DV), bf16),
        jax.ShapeDtypeStruct((rows, width), f32),
    )
    vmem, dma = pltpu.VMEM, pltpu.SemaphoreType.DMA

    def each(shape):
        return tuple(vmem(shape(stop - start), f32) for start, stop in PARTS)

    scratch = [vmem(a.shape, a.dtype) for a in args] + [vmem(o.shape, o.dtype) for o in out_shape]
    scratch += [
        vmem((H * FD, T), f32),
        vmem((H * FD, T), f32),
        vmem((H, R, T), bf16),
        vmem((H, R, T), bf16),
        vmem((H, T, R), bf16),
        vmem((H, T, R), bf16),
        vmem((R, F), bf16),
        vmem((H, T, T), f32),
        vmem((H, T, T), bf16),
        vmem((H, T, DV), f32),
        vmem((H, T, DV), f32),
        vmem((H, T, DV), bf16),
        vmem((H, T, T), bf16),
        vmem((H, R, DV), bf16),
        vmem((R, 4 * H), bf16),
        vmem((H, R, DV), f32),
        vmem((2, H, R, DV), f32),
        vmem((2, HALF, R, DV), f32),
        vmem((2, 2, R, DV), f32),
        vmem((2, 2, R, DV), f32),
        vmem((2, 2, R, DV), f32),
        vmem((2, 2, R, DV), f32),
        vmem((2, 2, R, DV), f32),
        vmem((2, 2, R, DV), f32),
        vmem((2, H, R, DV), f32),
        vmem((2, HALF, R, DV), f32),
        vmem((R * H, DV), f32),
        vmem((R * H, DV), f32),
        vmem((width, rows), f32),
        vmem((2, H, R), f32),
        vmem((2, H, R), f32),
        vmem((2, H, R), f32),
        vmem((2, nz, H, R), f32),
        vmem((H, T), f32),
        vmem((width, T), f32),
        each(lambda n: (2, nz, n, rows)),
        each(lambda n: (nz, n, rows)),
        each(lambda n: (nx, nz, n // nx, rows)),
        each(lambda n: (nx, nz, n // nx, rows)),
        each(lambda n: (nz, n // nx, rows)),
        each(lambda n: (nz, n // nx, rows)),
        each(lambda n: (ny, n // nx, rows)),
        each(lambda n: (nx, n // nx, rows)),
        dma((8,)), dma((3,)),
        dma((2,)), dma((2,)),
        dma((2, nz)), dma((2, nz)),
        dma((2, HALF)), dma((2, HALF)),
        dma((2, 2)), dma((2, 2)),
        dma((2, 2)), dma((2, 2)),
        dma((2, 2)), dma((2, 2)),
        dma((2, HALF)), dma((2, HALF)),
        dma((len(PARTS), 2)), dma((len(PARTS), 2)),
        dma((len(PARTS), 2, nx)), dma((len(PARTS), 2, nx)),
        dma((len(PARTS), nz)), dma((len(PARTS), nz)),
        dma((len(PARTS), ny)), dma((len(PARTS), ny)),
        dma((len(PARTS), nx)), dma((len(PARTS), nx)),
    ]
    results = pl.pallas_call(
        functools.partial(kernel, sizes),
        out_shape=out_shape,
        in_specs=[pl.BlockSpec(memory_space=pl.ANY)] * 8,
        out_specs=(pl.BlockSpec(memory_space=pl.ANY),) * 3,
        scratch_shapes=scratch,
        compiler_params=pltpu.CompilerParams(
            collective_id=0, has_side_effects=True, vmem_limit_bytes=60 * 1024 * 1024
        ),
    )(*args)
    return pl.pallas_call(
        hand_over,
        out_shape=out_shape,
        in_specs=[pl.BlockSpec(memory_space=pl.ANY)] * 3,
        out_specs=(pl.BlockSpec(memory_space=pl.ANY),) * 3,
        scratch_shapes=[vmem(o.shape, o.dtype) for o in out_shape] + [dma((3,)), dma((3,))],
    )(*results)


def solution(mesh):
    ns, docs = mesh.shape["seq"], mesh.shape["dp"]
    nx = 4 if docs >= 16 else 2

    def whole(*args):
        sizes = (ns, docs // nx, nx, args[0].shape[2])
        in_specs = (
            P("dp", "seq", None),
            P(),
            P("dp", "seq", None),
            P("dp", "seq", None),
            P("dp", "seq", None, None, None),
            P("dp", "seq", None, None),
            P("dp", "seq", None, None, None),
            P("dp", "seq", None, None),
        )
        out_specs = (P("dp", "seq", None), P("dp", "seq", None), P("seq", None))
        return jax.shard_map(
            functools.partial(on_device, sizes),
            mesh=mesh,
            in_specs=in_specs,
            out_specs=out_specs,
            check_vma=False,
        )(*args)

    return whole
```

```python
import functools
import math

import jax
import jax.numpy as jnp
from jax import lax
from jax.experimental import pallas as pl
from jax.experimental.pallas import tpu as pltpu
from jax.sharding import PartitionSpec as P

H = 8
FD = 16
DV = 128
F = 273
T = 128
R = 160
HALF = H // 2
PARTS = ((0, H * FD), (H * FD, 2 * H * FD))
PAIR = 1.0 / math.sqrt(2.0 * FD)
LINEAR = 1.0 / FD**0.25
f32 = jnp.float32
bf16 = jnp.bfloat16
MESH = pl.DeviceIdType.MESH


def dot(left, right, left_dim=1, right_dim=0):
    return lax.dot_general(
        left, right, (((left_dim,), (right_dim,)), ((), ())), preferred_element_type=f32
    )


def far_first(n):
    return sorted(range(1, n), key=lambda step: -min(step, n - step))


def split(x, parts):
    out = []
    for _ in range(parts):
        low = x.astype(bf16)
        out.append(low)
        x = x - low.astype(f32)
    return out


def fold_matrix():
    row = lax.broadcasted_iota(jnp.int32, (R, F), 0)
    col = lax.broadcasted_iota(jnp.int32, (R, F), 1)
    pair = col - 17
    a, b = (pair >> 4) & 15, pair & 15
    d = (b - a) & 15
    target = jnp.where(d <= 7, d * 16 + a, (16 - d) * 16 + b)
    target = jnp.where(d == 8, 144 + jnp.minimum(a, b), target)
    target = jnp.where(col <= 16, 127 + col, target)
    target = jnp.where(col == 0, 152, target)
    return jnp.where(row == target, 1.0, 0.0).astype(bf16)


def twice(shape, dim):
    row = lax.broadcasted_iota(jnp.int32, shape, dim)
    doubled = ((row >= 16) & (row < 128)) | ((row >= 144) & (row < 152))
    return jnp.where(doubled, 2.0, 1.0)


def features(u):
    rows = [u * (u if d == 0 else pltpu.roll(u, FD - d, 0)) * PAIR for d in range(8)]
    rows.append(u * LINEAR)
    rows.append(u[:8] * u[8:] * PAIR)
    rows.append(jnp.where(lax.broadcasted_iota(jnp.int32, (8, T), 0) == 0, 1.0, 0.0))
    return jnp.concatenate(rows, 0)


def feature_grad(u, y):
    acc = 2.0 * y[:16] * u
    for d in range(1, 8):
        part = y[16 * d : 16 * d + 16]
        acc = acc + part * pltpu.roll(u, FD - d, 0) + pltpu.roll(part * u, d, 0)
    last = y[144:152]
    acc = acc + jnp.concatenate([last * u[8:], last * u[:8]], 0)
    return y[128:144] * LINEAR + acc * PAIR


def kernel(
    sizes,
    tok_h, w_h, val_h, cot_h, ks_h, kn_h, qs_h, qn_h,
    tg_h, vg_h, wg_h,
    tok, w, val, cot, ks, kn, qs, qn,
    tg, vg, wg,
    qt, kt, phi_q, phi_k, phi_qt, phi_kt, fold,
    score, a_low, value_part, den, g_low, gs, p_low, norm_t,
    span, contrib, other, pair_out, pair_in, chain_in, chain_out, back_out, back_in, pre, pre_out,
    row_sum, query_sum, wg_t, norm_own, norm_mate, norm_chip, norm_in, gden_t, dproj_t,
    term, core_in, xs_out, xs_in, xz_out, xz_in, y_part, x_part,
    in_sem, out_sem,
    mate_send, mate_recv, norm_send, norm_recv, other_send, other_recv, pair_send, pair_recv,
    chain_send, chain_recv, back_send, back_recv, pre_send, pre_recv,
    core_send, core_recv, xs_send, xs_recv, xz_send, xz_recv,
    y_send, y_recv, x_send, x_recv,
):
    ns, ny, nx, d_model = sizes
    nz = ns // 2
    rows = d_model // ns
    pairs = nz // 2
    groups = min(4, nz)
    run_len = nz // groups
    dp = lax.axis_index("dp")
    me = lax.axis_index("seq")
    z, c = me // 2, lax.rem(me, 2)
    y, x = dp // nx, lax.rem(dp, nx)
    p, e = z // 2, lax.rem(z, 2)
    mate = 2 * z + (1 - c)
    partner = 4 * p + 2 * (1 - e) + c

    def z_peer(step):
        return lax.rem(z + step, nz)

    def y_peer(step):
        return lax.rem(y + step, ny)

    def x_peer(step):
        return lax.rem(x + step, nx)

    loads = [
        pltpu.make_async_copy(src, dst, in_sem.at[i])
        for i, (src, dst) in enumerate(
            [(tok_h, tok), (w_h, w), (val_h, val), (ks_h, ks), (kn_h, kn), (cot_h, cot), (qs_h, qs), (qn_h, qn)]
        )
    ]
    for load in loads:
        load.start()

    def across_z(step):
        return (dp, 2 * z_peer(step) + c)

    def across_y(step):
        return (y_peer(step) * nx + x, me)

    def across_x(step):
        return (y * nx + x_peer(step), me)

    barrier = pltpu.get_barrier_semaphore()
    pl.semaphore_signal(barrier, inc=1, device_id=(dp, mate), device_id_type=MESH)
    for step in range(1, nz):
        pl.semaphore_signal(barrier, inc=1, device_id=across_z(step), device_id_type=MESH)
    for step in range(1, ny):
        pl.semaphore_signal(barrier, inc=1, device_id=across_y(step), device_id_type=MESH)
    for step in range(1, nx):
        pl.semaphore_signal(barrier, inc=1, device_id=across_x(step), device_id_type=MESH)

    def remote(src, dst, send, recv, device):
        return pltpu.make_async_remote_copy(
            src_ref=src, dst_ref=dst, send_sem=send, recv_sem=recv, device_id=device, device_id_type=MESH
        )

    def mate_copy(which):
        return remote(
            norm_own.at[which], norm_mate.at[which], mate_send.at[which], mate_recv.at[which], (dp, mate)
        )

    def norm_copy(which, step):
        return remote(
            norm_chip.at[which], norm_in.at[which, step],
            norm_send.at[which, step], norm_recv.at[which, step], across_z(step),
        )

    def other_copy(which, k):
        return remote(
            contrib.at[which, (1 - c) * HALF + k], other.at[which, k],
            other_send.at[which, k], other_recv.at[which, k], (dp, mate),
        )

    def pair_copy(which, j):
        return remote(
            pair_out.at[which, j], pair_in.at[which, j],
            pair_send.at[which, j], pair_recv.at[which, j], (dp, partner),
        )

    def chain_copy(which, j):
        target = jnp.clip(p + 1 - 2 * which, 0, pairs - 1)
        return remote(
            chain_out.at[which, j], chain_in.at[which, j],
            chain_send.at[which, j], chain_recv.at[which, j], (dp, 4 * target + 2 * e + c),
        )

    def back_copy(which, j):
        return remote(
            back_out.at[which, j], back_in.at[which, j],
            back_send.at[which, j], back_recv.at[which, j], (dp, partner),
        )

    def pre_copy(which, k):
        return remote(
            pre_out.at[which, k], pre.at[which, c * HALF + k],
            pre_send.at[which, k], pre_recv.at[which, k], (dp, mate),
        )

    def core_copy(part, j):
        run = pl.ds(j * run_len, run_len)
        return remote(
            term[part].at[1 - c, run], core_in[part].at[run],
            core_send.at[part, j], core_recv.at[part, j], (dp, mate),
        )

    def xs_copy(part, step, group):
        run = pl.ds(group * run_len, run_len)
        return remote(
            xs_out[part].at[x_peer(step), run], xs_in[part].at[step, run],
            xs_send.at[part, group, step], xs_recv.at[part, group, step], across_x(step),
        )

    def xz_copy(part, step):
        return remote(
            xz_out[part].at[z_peer(step)], xz_in[part].at[step],
            xz_send.at[part, step], xz_recv.at[part, step], across_z(step),
        )

    def y_copy(part, step, source):
        return remote(
            y_part[part].at[source], y_part[part].at[source],
            y_send.at[part, step], y_recv.at[part, step], across_y(step),
        )

    def x_copy(part, step, source):
        return remote(
            x_part[part].at[source], x_part[part].at[source],
            x_send.at[part, step], x_recv.at[part, step], across_x(step),
        )

    coef = twice((R, DV), 0)
    coef_row = twice((H, R), 1)
    head_row = lax.broadcasted_iota(jnp.int32, (H, R), 0)
    fold[...] = fold_matrix()

    def lanes(h):
        return slice(h * DV, (h + 1) * DV)

    def feat(h):
        return slice(h * FD, (h + 1) * FD)

    def fold_rows(source, row_sum):
        def lap(a, carry):
            for d in range(8):
                b = (a + d) & 15
                row = source[0, 0, 17 + 16 * a + b].astype(f32)
                if d:
                    row = row + source[0, 0, 17 + 16 * b + a].astype(f32)
                row_sum[pl.ds(pl.multiple_of((16 * d + a) * H, H), H), :] = row
            row_sum[pl.ds(pl.multiple_of((128 + a) * H, H), H), :] = source[0, 0, 1 + a].astype(f32)
            return carry

        def last_lap(a, carry):
            row = source[0, 0, 25 + 17 * a].astype(f32) + source[0, 0, 17 + 16 * (a + 8) + a].astype(f32)
            row_sum[pl.ds(pl.multiple_of((144 + a) * H, H), H), :] = row
            return carry

        lax.fori_loop(0, 16, lap, 0)
        lax.fori_loop(0, 8, last_lap, 0)
        row_sum[152 * H : 153 * H, :] = source[0, 0, 0].astype(f32)
        row_sum[153 * H :, :] = jnp.zeros(((R - 153) * H, DV), f32)

    def fold_norm(value):
        return sum(dot(part, fold[...], 1, 1) for part in split(value, 3))

    loads[0].wait()
    loads[1].wait()
    projected = dot(tok[0], w[...]).astype(bf16)
    qt[...] = projected[:, : H * FD].astype(f32).T
    kt[...] = projected[:, H * FD :].astype(f32).T
    total = jnp.zeros((H, R), f32)
    ones = jnp.ones((H, T), bf16)
    for h in range(H):
        phi = features(kt[feat(h), :])
        phi_k[h] = phi.astype(bf16)
        total = jnp.where(head_row == h, dot(ones, phi_k[h], 1, 1), total)
    loads[4].wait()
    own_norm = fold_norm(kn[0, 0])
    norm_own[0] = total * coef_row + own_norm
    pl.semaphore_wait(barrier, nz + ny + nx - 2)
    mate_copy(0).start()

    loads[2].wait()
    loads[3].wait()
    fold_rows(ks, row_sum)
    for h in range(H):
        span[h] = row_sum[pl.ds(h, R, stride=H), :]
        contrib[0, h] = dot(phi_k[h], val[0, :, lanes(h)]) * coef + span[h]
    for k in range(HALF):
        other_copy(0, k).start()
    mate_copy(0).wait_recv()
    norm_chip[0] = norm_own[0] + norm_mate[0]
    for step in far_first(nz):
        norm_copy(0, step).start()

    causal = lax.broadcasted_iota(jnp.int32, (T, T), 0) >= lax.broadcasted_iota(jnp.int32, (T, T), 1)
    head_lane = lax.broadcasted_iota(jnp.int32, (T, H * FD), 1) // FD
    query, key = projected[:, : H * FD], projected[:, H * FD :]
    for h in range(H):
        phi = features(qt[feat(h), :])
        phi_q[h] = phi.astype(bf16)
        phi_qt[h] = phi.T.astype(bf16)
        masked = jnp.where(head_lane == h, query, jnp.zeros_like(query))
        s = dot(masked, key, 1, 1) * (1.0 / math.sqrt(FD))
        score[h] = s
        a = jnp.where(causal, 1.0 + s + 0.5 * s * s, 0.0)
        a_low[h] = a.astype(bf16)
        den[h] = jnp.broadcast_to(jnp.sum(a, axis=1, keepdims=True), (T, DV))

    def step_one(which):
        for j in range(2):
            k = 2 * (1 - e) + j
            other_copy(which, k).wait_recv()
            pair_out[which, j] = contrib[which, c * HALF + k] + other[which, k]
            pair_copy(which, j).start()

    def finish(which, k, before):
        second = (c ^ which) == 1
        mine = c * HALF + k
        pre[which, mine] = before + jnp.where(second, other[which, k], 0.0)
        pre_out[which, k] = before + jnp.where(second, 0.0, contrib[which, mine])
        pre_copy(which, k).start()

    def step_two(which):
        first = jnp.where(which == 0, p == 0, p == pairs - 1)
        last = jnp.where(which == 0, p == pairs - 1, p == 0)
        for j in range(2):
            k = 2 * e + j
            other_copy(which, k).wait_recv()
            pair_copy(which, j).wait_recv()

            @pl.when(first)
            def _():
                chain_in[which, j] = jnp.zeros((R, DV), f32)

            @pl.when(jnp.logical_not(first))
            def _():
                chain_copy(which, j).wait_recv()

            before = chain_in[which, j]
            here = contrib[which, c * HALF + k] + other[which, k]
            there = pair_in[which, j]

            @pl.when(jnp.logical_not(last))
            def _():
                chain_out[which, j] = before + (here + there)
                chain_copy(which, j).start()

            second = (e ^ which) == 1
            back_out[which, j] = before + jnp.where(second, 0.0, here)
            back_copy(which, j).start()
            finish(which, k, before + jnp.where(second, there, 0.0))

    def step_three(which):
        for j in range(2):
            back_copy(which, j).wait_recv()
            finish(which, 2 * (1 - e) + j, back_in[which, j])

    def step_four(which):
        for k in range(HALF):
            pre_copy(which, k).wait_recv()

    early = 2 * p < pairs
    late = jnp.logical_not(early)
    step_one(0)
    loads[6].wait()
    fold_rows(qs, query_sum)

    @pl.when(early)
    def _():
        step_two(0)

    for step in range(1, nz):
        norm_copy(0, step).wait_recv()
    norm = own_norm + jnp.where(c == 1, norm_mate[0], 0.0)
    for step in range(1, nz):
        norm = norm + jnp.where(z >= step, norm_in[0, step], 0.0)
    norm_parts = jnp.concatenate(split(norm, 3), 0)
    two_parts = split(norm, 2)
    norm_t[...] = jnp.concatenate(two_parts + two_parts, 0).astype(f32).T.astype(bf16)

    loads[5].wait()
    part_lane = lax.broadcasted_iota(jnp.int32, (T, 3 * H), 1) & (H - 1)
    for h in range(H):
        inner = dot(phi_qt[h], norm_parts, 1, 1)
        whole = den[h] + jnp.sum(jnp.where(part_lane == h, inner, 0.0), axis=1, keepdims=True)
        den[h] = whole
        g_low[h] = (cot[0, :, lanes(h)].astype(f32) / whole).astype(bf16)
        contrib[1, h] = dot(phi_q[h], g_low[h]) * coef + query_sum[pl.ds(h, R, stride=H), :]
    for k in range(HALF):
        other_copy(1, k).start()
    step_one(1)
    for h in range(H):
        value_part[h] = dot(a_low[h], val[0, :, lanes(h)])
        phi_kt[h] = phi_k[h].astype(f32).T.astype(bf16)

    @pl.when(late)
    def _():
        def either(i, carry):
            step_two(i ^ (p == pairs - 1).astype(jnp.int32))
            return carry

        lax.fori_loop(0, 2, either, 0)
        step_three(1)

    step_three(0)
    step_four(0)

    def send_terms(part):
        left = dproj_t[PARTS[part][0] : PARTS[part][1], :].astype(bf16)
        for k in range(nz):
            chunk = pl.ds(pl.multiple_of((2 * k + 1 - c) * rows, rows), rows)
            term[part][1 - c, k] = dot(left, tok[0, :, chunk])
            if k % run_len == run_len - 1:
                core_copy(part, k // run_len).start()
        for k in range(nz):
            chunk = pl.ds(pl.multiple_of((2 * k + c) * rows, rows), rows)
            term[part][c, k] = dot(left, tok[0, :, chunk])

    def send_x(part):
        for group in range(groups):
            core_copy(part, group).wait_recv()
            for k in range(group * run_len, (group + 1) * run_len):
                both = term[part][c, k] + core_in[part][k]
                piece = both.shape[0] // nx
                for j in range(nx):
                    xs_out[part][j, k] = both[j * piece : (j + 1) * piece]
            for step in far_first(nx):
                xs_copy(part, step, group).start()

    def send_z(part):
        for group in range(groups):
            for step in range(1, nx):
                xs_copy(part, step, group).wait_recv()
            for k in range(group * run_len, (group + 1) * run_len):
                acc = xs_out[part][x, k]
                for step in range(1, nx):
                    acc = acc + xs_in[part][step, k]
                xz_out[part][k] = acc

                @pl.when(k != z)
                def _():
                    xz_copy(part, lax.rem(k + nz - z, nz)).start()

    def send_y(part):
        acc = xz_out[part][z]
        for step in range(1, nz):
            xz_copy(part, step).wait_recv()
            acc = acc + xz_in[part][step]
        y_part[part][y] = acc
        for step in far_first(ny):
            y_copy(part, step, y).start()

    def send_all(part):
        for step in range(1, ny):
            y_copy(part, step, lax.rem(y + ny - step, ny)).wait_recv()
        acc = y_part[part][0]
        for j in range(1, ny):
            acc = acc + y_part[part][j]
        x_part[part][x] = acc * (1.0 / (ny * nx))
        for step in far_first(nx):
            x_copy(part, step, x).start()

    def collect(part):
        for step in range(1, nx):
            x_copy(part, step, lax.rem(x + nx - step, nx)).wait_recv()
        start, stop = PARTS[part]
        wg_t[start:stop, :] = x_part[part][...].reshape(stop - start, rows)

    lane = lax.broadcasted_iota(jnp.int32, (T, DV), 1)
    gden_all = jnp.zeros((T, DV), f32)
    for h in range(H):
        p_low[h] = (pre[0, h] + span[h]).astype(bf16)
        numer = dot(phi_qt[h], p_low[h]) + value_part[h]
        weighted = jnp.sum(cot[0, :, lanes(h)].astype(f32) * numer, axis=1, keepdims=True)
        gden = -weighted / (den[h] * den[h])
        gden_all = jnp.where(lane == h, gden, gden_all)
        den[h] = jnp.broadcast_to(gden, (T, DV))
    gden_t[...] = gden_all.T[:H]
    gden_parts = jnp.concatenate(split(gden_t[...], 3), 0)
    total = jnp.zeros((H, R), f32)
    for h in range(H):
        every = dot(gden_parts, phi_q[h], 1, 1)
        every = every[:H] + every[H : 2 * H] + every[2 * H :]
        total = jnp.where(head_row == h, every, total)
    loads[7].wait()
    norm_own[1] = total * coef_row + fold_norm(qn[0, 0])
    mate_copy(1).start()
    mate_copy(1).wait_recv()
    norm_chip[1] = norm_own[1] + norm_mate[1]
    for step in far_first(nz):
        norm_copy(1, step).start()

    high, low = split(gden_t[...], 2)
    gden_rows = jnp.concatenate([high, high, low, low], 0)
    four_row = lax.broadcasted_iota(jnp.int32, (4 * H, T), 0) & (H - 1)
    for h in range(H):
        ga = jnp.where(causal, dot(g_low[h], val[0, :, lanes(h)], 1, 1) + den[h], 0.0)
        gs[h] = (ga * (1.0 + score[h]) * (1.0 / math.sqrt(FD))).astype(bf16)
        only = jnp.where(four_row == h, gden_rows, jnp.zeros_like(gden_rows))
        up = dot(p_low[h], g_low[h], 1, 1) + dot(norm_t[...], only)
        u = qt[feat(h), :]
        dproj_t[feat(h), :] = feature_grad(u, up) + dot(kt[feat(h), :].astype(bf16), gs[h], 1, 1)
    send_terms(0)

    @pl.when(early)
    def _():
        step_two(1)

    send_x(0)

    @pl.when(early)
    def _():
        step_three(1)

    step_four(1)
    for step in range(1, nz):
        norm_copy(1, step).wait_recv()
    norm = jnp.where(c == 0, norm_mate[1], 0.0)
    for step in range(1, nz):
        norm = norm + jnp.where(z < step, norm_in[1, step], 0.0)
    parts = split(norm, 3)
    norm_t[...] = jnp.concatenate(parts + [jnp.zeros_like(parts[0])], 0).astype(f32).T.astype(bf16)
    for h in range(H):
        only = jnp.where(four_row == h, 1.0, 0.0).astype(bf16)
        p_low[h] = pre[1, h].astype(bf16)
        up = dot(p_low[h], val[0, :, lanes(h)], 1, 1) + dot(norm_t[...], only)
        u = kt[feat(h), :]
        inner = dot(qt[feat(h), :].astype(bf16), gs[h])
        dproj_t[H * FD + h * FD : H * FD + (h + 1) * FD, :] = feature_grad(u, up) + inner
    send_terms(1)
    send_x(1)
    send_z(0)

    for h in range(H):
        vg[0, :, lanes(h)] = (dot(a_low[h], g_low[h], 0, 0) + dot(phi_kt[h], p_low[h])).astype(bf16)
    store_vg = pltpu.make_async_copy(vg, vg_h, out_sem.at[0])
    store_vg.start()
    dproj = dproj_t[...].T.astype(bf16)
    cols = min(512, d_model)
    for j in range(d_model // cols):
        tg[0, :, j * cols : (j + 1) * cols] = dot(dproj, w[j * cols : (j + 1) * cols, :], 1, 1).astype(bf16)
    store_tg = pltpu.make_async_copy(tg, tg_h, out_sem.at[1])
    store_tg.start()

    for which in range(2):
        mate_copy(which).wait_send()
        for step in range(1, nz):
            norm_copy(which, step).wait_send()
        last = (p == pairs - 1) if which == 0 else (p == 0)
        for k in range(HALF):
            other_copy(which, k).wait_send()
            pre_copy(which, k).wait_send()
        for j in range(2):
            pair_copy(which, j).wait_send()
            back_copy(which, j).wait_send()

            @pl.when(jnp.logical_not(last))
            def _():
                chain_copy(which, j).wait_send()

    def sent(part):
        for j in range(groups):
            core_copy(part, j).wait_send()
        for step in range(1, nx):
            for group in range(groups):
                xs_copy(part, step, group).wait_send()
        for step in range(1, nz):
            xz_copy(part, step).wait_send()

    send_z(1)
    send_y(0)
    sent(0)
    send_y(1)
    send_all(0)
    sent(1)
    store_vg.wait()
    store_tg.wait()
    send_all(1)
    collect(0)
    for part in range(len(PARTS)):
        for step in range(1, ny):
            y_copy(part, step, y).wait_send()
    collect(1)
    wg[...] = wg_t[...].T
    store_wg = pltpu.make_async_copy(wg, wg_h, out_sem.at[2])
    store_wg.start()
    for part in range(len(PARTS)):
        for step in range(1, nx):
            x_copy(part, step, x).wait_send()
    store_wg.wait()


def hand_over(*refs):
    held, load_sem, store_sem = refs[6:9], refs[9], refs[10]
    loads = [pltpu.make_async_copy(refs[i], held[i], load_sem.at[i]) for i in range(3)]
    stores = [pltpu.make_async_copy(held[i], refs[3 + i], store_sem.at[i]) for i in range(3)]
    for load in loads:
        load.start()
    for load, store in zip(loads, stores):
        load.wait()
        store.start()
    for store in stores:
        store.wait()


def on_device(sizes, tokens, qk_weight, values, cotangent, key_span, key_norm, query_span, query_norm):
    ns, ny, nx, d_model = sizes
    nz = ns // 2
    rows = d_model // ns
    width = 2 * H * FD
    key_span, query_span = (jnp.swapaxes(a, 2, 3) for a in (key_span, query_span))
    args = (tokens, qk_weight, values, cotangent, key_span, key_norm, query_span, query_norm)
    out_shape = (
        jax.ShapeDtypeStruct((1, T, d_model), bf16),
        jax.ShapeDtypeStruct((1, T, H * DV), bf16),
        jax.ShapeDtypeStruct((rows, width), f32),
    )
    vmem, dma = pltpu.VMEM, pltpu.SemaphoreType.DMA

    def each(shape):
        return tuple(vmem(shape(stop - start), f32) for start, stop in PARTS)

    scratch = [vmem(a.shape, a.dtype) for a in args] + [vmem(o.shape, o.dtype) for o in out_shape]
    scratch += [
        vmem((H * FD, T), f32),
        vmem((H * FD, T), f32),
        vmem((H, R, T), bf16),
        vmem((H, R, T), bf16),
        vmem((H, T, R), bf16),
        vmem((H, T, R), bf16),
        vmem((R, F), bf16),
        vmem((H, T, T), f32),
        vmem((H, T, T), bf16),
        vmem((H, T, DV), f32),
        vmem((H, T, DV), f32),
        vmem((H, T, DV), bf16),
        vmem((H, T, T), bf16),
        vmem((H, R, DV), bf16),
        vmem((R, 4 * H), bf16),
        vmem((H, R, DV), f32),
        vmem((2, H, R, DV), f32),
        vmem((2, HALF, R, DV), f32),
        vmem((2, 2, R, DV), f32),
        vmem((2, 2, R, DV), f32),
        vmem((2, 2, R, DV), f32),
        vmem((2, 2, R, DV), f32),
        vmem((2, 2, R, DV), f32),
        vmem((2, 2, R, DV), f32),
        vmem((2, H, R, DV), f32),
        vmem((2, HALF, R, DV), f32),
        vmem((R * H, DV), f32),
        vmem((R * H, DV), f32),
        vmem((width, rows), f32),
        vmem((2, H, R), f32),
        vmem((2, H, R), f32),
        vmem((2, H, R), f32),
        vmem((2, nz, H, R), f32),
        vmem((H, T), f32),
        vmem((width, T), f32),
        each(lambda n: (2, nz, n, rows)),
        each(lambda n: (nz, n, rows)),
        each(lambda n: (nx, nz, n // nx, rows)),
        each(lambda n: (nx, nz, n // nx, rows)),
        each(lambda n: (nz, n // nx, rows)),
        each(lambda n: (nz, n // nx, rows)),
        each(lambda n: (ny, n // nx, rows)),
        each(lambda n: (nx, n // nx, rows)),
        dma((8,)), dma((3,)),
        dma((2,)), dma((2,)),
        dma((2, nz)), dma((2, nz)),
        dma((2, HALF)), dma((2, HALF)),
        dma((2, 2)), dma((2, 2)),
        dma((2, 2)), dma((2, 2)),
        dma((2, 2)), dma((2, 2)),
        dma((2, HALF)), dma((2, HALF)),
        dma((len(PARTS), min(4, nz))), dma((len(PARTS), min(4, nz))),
        dma((len(PARTS), min(4, nz), nx)), dma((len(PARTS), min(4, nz), nx)),
        dma((len(PARTS), nz)), dma((len(PARTS), nz)),
        dma((len(PARTS), ny)), dma((len(PARTS), ny)),
        dma((len(PARTS), nx)), dma((len(PARTS), nx)),
    ]
    results = pl.pallas_call(
        functools.partial(kernel, sizes),
        out_shape=out_shape,
        in_specs=[pl.BlockSpec(memory_space=pl.ANY)] * 8,
        out_specs=(pl.BlockSpec(memory_space=pl.ANY),) * 3,
        scratch_shapes=scratch,
        compiler_params=pltpu.CompilerParams(
            collective_id=0, has_side_effects=True, vmem_limit_bytes=60 * 1024 * 1024
        ),
    )(*args)
    return pl.pallas_call(
        hand_over,
        out_shape=out_shape,
        in_specs=[pl.BlockSpec(memory_space=pl.ANY)] * 3,
        out_specs=(pl.BlockSpec(memory_space=pl.ANY),) * 3,
        scratch_shapes=[vmem(o.shape, o.dtype) for o in out_shape] + [dma((3,)), dma((3,))],
    )(*results)


def solution(mesh):
    ns, docs = mesh.shape["seq"], mesh.shape["dp"]
    nx = 4 if docs >= 16 else 2

    def whole(*args):
        sizes = (ns, docs // nx, nx, args[0].shape[2])
        in_specs = (
            P("dp", "seq", None),
            P(),
            P("dp", "seq", None),
            P("dp", "seq", None),
            P("dp", "seq", None, None, None),
            P("dp", "seq", None, None),
            P("dp", "seq", None, None, None),
            P("dp", "seq", None, None),
        )
        out_specs = (P("dp", "seq", None), P("dp", "seq", None), P("seq", None))
        return jax.shard_map(
            functools.partial(on_device, sizes),
            mesh=mesh,
            in_specs=in_specs,
            out_specs=out_specs,
            check_vma=False,
        )(*args)

    return whole
```
